256 devices in a mesh: req: 8 (over y, core), mp: 32 (over z, x).
Axes of the slice: x: 4, y: 4, z: 8, core: 2. Of those that a mesh axis runs over, the one named last changes fastest.
Arguments:
- draft_hidden: bfloat16 [16, 2048], P('req'), may hold values from -6 to 6
- draft_weight: bfloat16 [4, 2048, 2048], P(None, None, 'mp'), may hold values from -0.125 to 0.125
- vocab_weight: bfloat16 [98304, 2048], P(('req', 'mp')), may hold values from -0.375 to 0.375
- tree_inputs: bfloat16 [768, 2048], P('req')
- tree_parent: int32 [16, 48], P('req'), may hold values from -1 to 41, as said below
- cache_len: int32 [16], P('req'), may hold values from 1 to 8192, as said below
- page_table: int32 [16, 64], P('req'), may hold values from -1 to 1023, as said below
- kv_cache: bfloat16 [1024, 2, 128, 2048], P(('req', 'mp'))
- accepted_node: int32 [16], P('req'), may hold values from 0 to 47
- qkv_weight: bfloat16 [2048, 3, 2048], P(None, None, 'mp'), may hold values from -0.125 to 0.125
- norm_gains: bfloat16 [4, 2048], replicated, may hold values from 0.5 to 1.5
- out_weight: bfloat16 [2048, 2048], P(None, 'mp'), may hold values from -0.125 to 0.125
- gate_up_weight: bfloat16 [2048, 2, 8192], P(None, None, 'mp'), may hold values from -0.125 to 0.125
- down_weight: bfloat16 [8192, 2048], P('mp'), may hold values from -0.0625 to 0.0625
Outputs:
- draft_logits: float32 [16, 4, 98304], P(None, None, ('req', 'mp'))
- layer_out: bfloat16 [768, 2048], P(('req', 'mp'))
- accepted_kv: bfloat16 [16, 4, 2, 2048], P('req', None, None, 'mp')
The draws below stay inside these ranges and needn't reach their ends.
Inputs may be any that keep to these rules, and one draw needn't show every extreme that they name: `page_table`: row r lists the pool pages of request r in the order of its tokens, ceil(cache_len[r] / 128) of them, then -1. The pages of the requests of one index of req lie in that index's part of kv_cache, and no page serves two requests. `cache_len`: on every index of req some request has exactly 8192 cached tokens. `tree_parent`: A parent has a smaller index than its child; a node has at most 3 ancestors.
All inputs are finite; a program needn't handle non-finite values.
Results may differ from the reference program's by a relative error of at most 0.01355.
Values may be sent and summed in bfloat16 or wider, within the bound.
No kernel may reach another device: no remote copies, remote signals or barrier semaphores. Data moves between devices by JAX's collectives and lax.ppermute only.
A program may use at most 128 MiB of HBM per device.

```python
import jax
import jax.numpy as jnp
from jax import lax

D = 2048
HEADS = 16
HEAD_DIM = 128
FF = 8192
DRAFTS = 4
TREE = 48
PAGE = 128
REQ_DEV = 2
REQ = 16
VOCAB = 98304
POOL = 1024
MAXP = 64


def request_plan(base_key):
    groups = REQ // REQ_DEV
    pool_group = 2 * MAXP
    subkeys = jax.random.split(base_key, 4)
    biggest = jax.random.randint(subkeys[1], (groups,), 0, REQ_DEV)
    is_big = jnp.arange(REQ_DEV)[None, :] == biggest[:, None]
    page_counts = jnp.where(is_big, MAXP, 1)
    last_fill = jax.random.randint(subkeys[2], (groups, REQ_DEV), 1, 5)
    last_fill = jnp.where(is_big, PAGE, last_fill)
    lengths = (page_counts - 1) * PAGE + last_fill
    offsets = jnp.cumsum(page_counts, axis=1) - page_counts

    def group_order(group_key):
        order = jax.random.permutation(group_key, pool_group)
        leading = order[0]
        order = jnp.where(order == pool_group - 1, leading, order)
        return order.at[0].set(pool_group - 1)
    orders = jax.vmap(group_order)(jax.random.split(subkeys[3], groups))
    columns = jnp.arange(MAXP)
    wanted = jnp.minimum(offsets[:, :, None] + columns[None, None, :], pool_group - 1)
    picked = jax.vmap(lambda one_order, wanted_rows: one_order[wanted_rows])(orders, wanted)
    slots = picked + jnp.arange(groups)[:, None, None] * pool_group
    page_rows = jnp.where(columns[None, None, :] < page_counts[:, :, None], slots, -1)
    return (lengths.reshape(REQ).astype(jnp.int32), page_rows.reshape(REQ, MAXP).astype(jnp.int32))


def draw_cache_len(key, part):
    return request_plan(jax.random.fold_in(key, 11))[0]


def draw_page_table(key, part):
    return request_plan(jax.random.fold_in(key, 11))[1]


def draw_tree_parent(key, part):
    subkeys = jax.random.split(key, 4)
    first_end = jax.random.randint(subkeys[0], (REQ, 1), 4, 13)
    second_end = first_end + jax.random.randint(subkeys[1], (REQ, 1), 6, 15)
    third_end = second_end + jax.random.randint(subkeys[2], (REQ, 1), 8, 17)
    row_ids = jnp.arange(REQ)[:, None]
    third_end = jnp.where(row_ids == 0, 42, third_end)
    node_ids = jnp.arange(TREE)[None, :]
    node_level = (node_ids >= first_end).astype(jnp.int32) + (node_ids >= second_end).astype(jnp.int32) + (node_ids >= third_end).astype(jnp.int32)
    low_end = jnp.where(node_level == 3, second_end, jnp.where(node_level == 2, first_end, 0))
    high_end = jnp.where(node_level == 3, third_end, jnp.where(node_level == 2, second_end, first_end))
    parent = jax.random.randint(subkeys[3], (REQ, TREE), low_end, high_end)
    parent = jnp.where(node_ids == TREE - 1, third_end - 1, parent)
    return jnp.where(node_level == 0, -1, parent).astype(jnp.int32)


def draw_tree_inputs(key, part):
    subkeys = jax.random.split(key, 3)
    row_total = REQ * TREE
    entries = jax.random.normal(subkeys[0], (row_total, D), jnp.float32)
    scale_span = 3.0
    log_span = jnp.log(scale_span)
    row_scale = jnp.exp(jax.random.uniform(subkeys[1], (row_total, 1), jnp.float32, -log_span, log_span))
    column_scale = jnp.exp(jax.random.uniform(subkeys[2], (1, D), jnp.float32, -log_span, log_span))
    return (entries * row_scale * column_scale).astype(jnp.bfloat16)


def draw_kv_cache(key, part):
    lengths, page_rows = request_plan(jax.random.fold_in(key, 11))
    long_row = lengths == MAXP * PAGE
    targets = jnp.where((page_rows >= 0) & long_row[:, None], page_rows, POOL).reshape(-1)
    long_slot = jnp.zeros((POOL,), jnp.float32).at[targets].set(1.0, mode='drop')
    subkeys = jax.random.split(key, 3)
    entries = jax.random.normal(subkeys[0], (POOL, 2, PAGE, D), jnp.float32)
    long_scale = jnp.exp(jax.random.uniform(subkeys[1], (POOL, 1, PAGE, 1), jnp.float32, jnp.log(0.5), jnp.log(4.0)))
    short_scale = jnp.exp(jax.random.uniform(subkeys[2], (POOL, 1, PAGE, 1), jnp.float32, jnp.log(0.5), jnp.log(1.5)))
    token_scale = jnp.where(long_slot[:, None, None, None] > 0.5, long_scale, short_scale)
    key_side = jnp.arange(2)[None, :, None, None] == 0
    return (entries * jnp.where(key_side, token_scale, 1.0)).astype(jnp.bfloat16)


def set_ends(result, own_key, low, top_value):
    dims = result.shape
    index_at = [jax.random.randint(jax.random.fold_in(own_key, axis), (), 0, dims[axis]) for axis in range(len(dims))]
    result = result.at[tuple(index_at)].set(low)
    longest = dims.index(max(dims))
    index_at[longest] = (index_at[longest] + 1) % dims[longest]
    return result.at[tuple(index_at)].set(top_value)


def level_of(own_key, dims, shards, least, high):
    def one(dim, shards_of):
        steps = jax.random.uniform(jax.random.fold_in(jax.random.fold_in(own_key, 6), dim), (shards_of,), jnp.float32, least / len(shards), high / len(shards))
        return jnp.repeat(jnp.exp(steps), dims[dim] // shards_of).reshape((-1,) + (1,) * (len(dims) - dim - 1))

    loudness = one(*shards[0])
    for cut in shards[1:]:
        loudness = loudness * one(*cut)
    return loudness


def noise(rng, shape, width, most, shards=(), kind=jnp.bfloat16):
    values = jax.random.normal(rng, shape, jnp.float32) * width
    if len(shards) > 0:
        values = level_of(rng, shape, shards, -0.22, 0.18) * values
    return jnp.clip(values, min=-most, max=most).astype(kind)


def setup_inputs(seed: int = 0) -> dict:
    splits = jax.random.split(jax.random.key(seed), 15)
    return {
        "draft_hidden": noise(splits[0], (REQ, D), 1.0, 6.0, ((0, 8),)),
        "draft_weight": noise(splits[1], (DRAFTS, D, D), D ** -0.5, 0.125, ((2, 32),)),
        "vocab_weight": noise(splits[2], (VOCAB, D), (D // 8) ** -0.5, 0.375, ((0, 256),)),
        "tree_inputs": draw_tree_inputs(jax.random.fold_in(splits[14], 71), 0),
        "tree_parent": draw_tree_parent(jax.random.fold_in(splits[14], 71), 0),
        "cache_len": draw_cache_len(jax.random.fold_in(splits[14], 71), 0),
        "page_table": draw_page_table(jax.random.fold_in(splits[14], 71), 0),
        "kv_cache": draw_kv_cache(jax.random.fold_in(splits[14], 71), 0),
        "accepted_node": set_ends(jax.random.randint(splits[8], (REQ,), 0, TREE), jax.random.fold_in(splits[8], 1), 0, TREE - 1).astype(jnp.int32),
        "qkv_weight": noise(splits[9], (D, 3, D), D ** -0.5, 0.125, ((2, 32),)),
        "norm_gains": jnp.clip(1.0 + 0.1 * jax.random.normal(splits[10], (4, D), jnp.float32), 0.5, 1.5).astype(jnp.bfloat16),
        "out_weight": noise(splits[11], (D, D), D ** -0.5, 0.125, ((1, 32),)),
        "gate_up_weight": noise(splits[12], (D, 2, FF), D ** -0.5, 0.125, ((2, 32),)),
        "down_weight": noise(splits[13], (FF, D), FF ** -0.5, 0.0625, ((0, 32),)),
    }


rope_base = 500000.0
norm_epsilon = 1e-06
masked_score = -1e+30

def rms_scaled(entries, gain_row):
    mean_square = lax.optimization_barrier(jnp.mean(entries * entries, axis=-1, keepdims=True))
    return entries * lax.rsqrt(mean_square + norm_epsilon) * gain_row

def tree_shape(parents):
    node_count = parents.shape[-1]
    step_one = (parents[..., :, None] == jnp.arange(node_count, dtype=jnp.int32)[None, None, :]).astype(jnp.float32)
    step_two = jnp.einsum('rij,rjk->rik', step_one, step_one, precision=lax.Precision.HIGHEST)
    step_three = jnp.einsum('rij,rjk->rik', step_two, step_one, precision=lax.Precision.HIGHEST)
    ancestry = jnp.eye(node_count, dtype=jnp.float32)[None] + step_one + step_two + step_three
    return (ancestry, lax.optimization_barrier(jnp.sum(ancestry, axis=-1)))

def rotate(entries, positions):
    row_count = entries.shape[0]
    half_dim = HEAD_DIM // 2
    shaped = entries.reshape(row_count, HEADS, HEAD_DIM)
    freqs = rope_base ** (-jnp.arange(half_dim, dtype=jnp.float32) * 2.0 / HEAD_DIM)
    angles = positions[:, None] * freqs[None, :]
    cosine = jnp.cos(angles)[:, None, :]
    sine_part = jnp.sin(angles)[:, None, :]
    front = shaped[..., :half_dim]
    back_half = shaped[..., half_dim:]
    turned = jnp.concatenate([front * cosine - back_half * sine_part, back_half * cosine + front * sine_part], axis=-1)
    return turned.reshape(row_count, HEADS * HEAD_DIM)

def reference(draft_hidden, draft_weight, vocab_weight, tree_inputs, tree_parent, cache_len, page_table, kv_cache, accepted_node, qkv_weight, norm_gains, out_weight, gate_up_weight, down_weight):
    draft_raw = jnp.stack([jnp.dot(draft_hidden, draft_weight[draft_index], preferred_element_type=jnp.float32) for draft_index in range(DRAFTS)], axis=1)
    drafted = (draft_hidden.astype(jnp.float32)[:, None, :] + jax.nn.silu(draft_raw)).astype(jnp.bfloat16)
    draft_logits = jnp.dot(drafted.reshape(REQ * DRAFTS, D), vocab_weight.T, preferred_element_type=jnp.float32).reshape(REQ, DRAFTS, VOCAB)
    projected = jnp.dot(tree_inputs, qkv_weight.reshape(D, 3 * D), preferred_element_type=jnp.float32).astype(jnp.bfloat16).reshape(REQ * TREE, 3, D)
    ancestry, node_depth = tree_shape(tree_parent)
    positions = (cache_len[:, None].astype(jnp.float32) + node_depth - 1.0).reshape(REQ * TREE)
    gain_rows = norm_gains.astype(jnp.float32)
    queries = rotate(rms_scaled(projected[:, 0].astype(jnp.float32), gain_rows[0]), positions).astype(jnp.bfloat16).reshape(REQ, TREE, HEADS, HEAD_DIM)
    keys_tree = rotate(rms_scaled(projected[:, 1].astype(jnp.float32), gain_rows[1]), positions).astype(jnp.bfloat16).reshape(REQ, TREE, HEADS, HEAD_DIM)
    values_tree = projected[:, 2].reshape(REQ, TREE, HEADS, HEAD_DIM)
    chosen = (accepted_node[:, None] == jnp.arange(TREE, dtype=jnp.int32)[None, :]).astype(jnp.float32)
    on_path = jnp.einsum('rt,rts->rs', chosen, ancestry, precision=lax.Precision.HIGHEST)
    levels = jnp.arange(1, DRAFTS + 1, dtype=jnp.float32)
    picker = on_path[:, None, :] * (node_depth[:, None, :] == levels[None, :, None]).astype(jnp.float32)
    stacked = jnp.stack([keys_tree.reshape(REQ, TREE, D), values_tree.reshape(REQ, TREE, D)], axis=2)
    accepted_kv = jnp.einsum('rjs,rsce->rjce', picker, stacked.astype(jnp.float32), precision=lax.Precision.HIGHEST).astype(jnp.bfloat16)
    scale = HEAD_DIM ** (-0.5)

    def attend_one(packed):
        query_rows, key_rows, value_rows, tree_mask, table_row, length_now = packed
        slots = jnp.maximum(table_row, 0)
        pages = kv_cache[slots]
        cached_keys = pages[:, 0].reshape(MAXP * PAGE, HEADS, HEAD_DIM).astype(jnp.float32)
        cached_values = pages[:, 1].reshape(MAXP * PAGE, HEADS, HEAD_DIM)
        token_valid = jnp.arange(MAXP * PAGE, dtype=jnp.int32) < length_now
        query_wide = query_rows.astype(jnp.float32)
        cached_scores = jnp.einsum('the,she->hts', query_wide, cached_keys) * scale
        tree_scores = jnp.einsum('the,she->hts', query_wide, key_rows.astype(jnp.float32)) * scale
        valid_all = jnp.concatenate([jnp.broadcast_to(token_valid[None, :], (TREE, MAXP * PAGE)), tree_mask > 0.5], axis=1)
        scores = jnp.concatenate([cached_scores, tree_scores], axis=-1)
        scores = jnp.where(valid_all[None], scores, masked_score)
        top_score = lax.optimization_barrier(jnp.max(scores, axis=-1, keepdims=True))
        weights = jnp.where(valid_all[None], jnp.exp(scores - top_score), 0.0)
        totals = lax.optimization_barrier(jnp.sum(weights, axis=-1))
        rounded = lax.optimization_barrier(weights.astype(jnp.bfloat16)).astype(jnp.float32)
        values_all = jnp.concatenate([cached_values, value_rows], axis=0).astype(jnp.float32)
        mixed = jnp.einsum('hts,she->the', rounded, values_all)
        return (mixed / totals.T[:, :, None]).astype(jnp.bfloat16)
    attended = lax.map(attend_one, (queries, keys_tree, values_tree, ancestry, page_table, cache_len)).reshape(REQ * TREE, D)
    projected_out = jnp.dot(attended, out_weight, preferred_element_type=jnp.float32).astype(jnp.bfloat16)
    residual = (tree_inputs.astype(jnp.float32) + rms_scaled(projected_out.astype(jnp.float32), gain_rows[2])).astype(jnp.bfloat16)
    gate_up = jnp.dot(residual, gate_up_weight.reshape(D, 2 * FF), preferred_element_type=jnp.float32).reshape(REQ * TREE, 2, FF)
    hidden = (jax.nn.silu(gate_up[:, 0]) * gate_up[:, 1]).astype(jnp.bfloat16)
    mlp_out = jnp.dot(hidden, down_weight, preferred_element_type=jnp.float32)
    layer_out = (residual.astype(jnp.float32) + rms_scaled(mlp_out, gain_rows[3])).astype(jnp.bfloat16)
    return (draft_logits, layer_out, accepted_kv)
```

```python
import functools

import jax
import jax.numpy as jnp
from jax import lax
from jax.experimental import pallas as pl
from jax.experimental.pallas import tpu as pltpu
from jax.sharding import PartitionSpec as P

HEADS = 16
HEAD_DIM = 128
HALF = HEAD_DIM // 2
LANES = 128

rope_base = 500000.0
norm_epsilon = 1e-06
masked_score = -1e30


def tree_shape(parents):
    node_count = parents.shape[-1]
    step_one = (
        parents[..., :, None] == jnp.arange(node_count, dtype=jnp.int32)[None, None, :]
    ).astype(jnp.float32)
    step_two = jnp.einsum("rij,rjk->rik", step_one, step_one, precision=lax.Precision.HIGHEST)
    step_three = jnp.einsum("rij,rjk->rik", step_two, step_one, precision=lax.Precision.HIGHEST)
    ancestry = jnp.eye(node_count, dtype=jnp.float32)[None] + step_one + step_two + step_three
    return (ancestry, jnp.sum(ancestry, axis=-1))


def split_three(value):
    top = value.astype(jnp.bfloat16).astype(jnp.float32)
    rest = value - top
    middle = rest.astype(jnp.bfloat16).astype(jnp.float32)
    return top, middle, (rest - middle).astype(jnp.bfloat16).astype(jnp.float32)


def rotated(front, back, cosine, sine):
    return front * cosine - back * sine, back * cosine + front * sine


def pages_kernel(
    rows_request, counts, gathered, gains, cosine, sine, cache, out, queries, key_square, kv, sems
):
    pages, _, page_len, width = cache.shape
    groups = sems.shape[0]
    group_width = width // groups

    def fetch(group):
        columns = pl.ds(group * group_width, group_width)
        return pltpu.make_async_copy(
            cache.at[:, :, :, columns], kv.at[:, :, :, columns], sems.at[group]
        )

    for group in range(groups):
        fetch(group).start()
    lane = lax.broadcasted_iota(jnp.int32, (8, LANES), 1)
    squares = jnp.zeros((HALF, LANES), jnp.float32)
    extra = jnp.zeros((8, LANES), jnp.float32)
    for source in range(2 * HEADS):
        chunk = gathered[source].astype(jnp.float32)
        squares = squares + chunk * chunk
        extra = extra + chunk[0:8]
    inverse = lax.rsqrt(jnp.sum(squares, axis=0, keepdims=True) / width + norm_epsilon)
    key_square[...] = extra
    limits = []
    first = lax.broadcasted_iota(jnp.int32, (1, LANES), 1) < rows_request
    for page in range(pages):
        limits.append(jnp.where(first, counts[2 * page], counts[2 * page + 1]))
    token = lax.broadcasted_iota(jnp.int32, (page_len, LANES), 0)
    visible = [token < limit for limit in limits]
    scale = HEAD_DIM ** (-0.5)
    cos_rows = cosine[...]
    sin_rows = sine[...]
    for head in range(HEADS):
        if head % (HEADS // groups) == 0:
            fetch(head // (HEADS // groups)).wait()
        base = head * HEAD_DIM
        front = (
            gathered[2 * head].astype(jnp.float32)
            * inverse
            * gains[base : base + HALF].astype(jnp.float32)
        )
        back = (
            gathered[2 * head + 1].astype(jnp.float32)
            * inverse
            * gains[base + HALF : base + HEAD_DIM].astype(jnp.float32)
        )
        front, back = rotated(front, back, cos_rows, sin_rows)
        query = jnp.concatenate([front, back], axis=0).astype(jnp.bfloat16)
        queries[base : base + HEAD_DIM] = query
        keys = kv[:, 0, :, base : base + HEAD_DIM].reshape(pages * page_len, HEAD_DIM)
        scores = jnp.dot(keys, query, preferred_element_type=jnp.float32) * scale
        parts = [
            jnp.where(
                visible[page], scores[page * page_len : (page + 1) * page_len], masked_score
            )
            for page in range(pages)
        ]
        top = functools.reduce(jnp.maximum, parts)
        top = jnp.max(top, axis=0, keepdims=True)
        weights = [
            jnp.where(visible[page], jnp.exp(parts[page] - top), 0.0) for page in range(pages)
        ]
        total = jnp.sum(functools.reduce(jnp.add, weights), axis=0, keepdims=True)
        weight = jnp.concatenate(weights, axis=0).astype(jnp.bfloat16)
        values = kv[:, 1, :, base : base + HEAD_DIM].reshape(pages * page_len, HEAD_DIM)
        mixed = lax.dot_general(
            values, weight, (((0,), (0,)), ((), ())), preferred_element_type=jnp.float32
        )
        zero = jnp.zeros_like(top)
        stats = jnp.concatenate([*split_three(top), *split_three(total), zero, zero], axis=0)
        tail = jnp.concatenate(
            [
                pltpu.roll(stats, 96, 1),
                pltpu.roll(stats, 64, 1),
                pltpu.roll(stats, 32, 1),
                jnp.zeros((HALF - 24, LANES), jnp.float32),
            ],
            axis=0,
        )
        spare = lax.broadcasted_iota(jnp.int32, (HALF, LANES), 1) >= 96
        out[2 * head] = jnp.where(spare, tail, mixed[:HALF]).astype(jnp.bfloat16)
        out[2 * head + 1] = jnp.where(spare, tail, mixed[HALF:]).astype(jnp.bfloat16)


def unpacked(chunk):
    lane = lax.broadcasted_iota(jnp.int32, (8, LANES), 1)
    return jnp.where(
        lane < 32,
        pltpu.roll(chunk[0:8], 32, 1),
        jnp.where(lane < 64, pltpu.roll(chunk[8:16], 64, 1), pltpu.roll(chunk[16:24], 96, 1)),
    )


def tree_kernel(
    place, query, own_key, other_key, key_square, gain, cosine, sine, values, mask, keys_out, mixed_out, stats_out
):
    width = 2 * HEADS * HALF
    even = place[0] == 0
    packed = key_square[...]
    both = packed[0:3] + packed[3:6]
    lane = lax.broadcasted_iota(jnp.int32, (1, LANES), 1)
    wide = jnp.concatenate([both, jnp.zeros((5, LANES), jnp.float32)], axis=0)
    square = jnp.where(
        lane < 32,
        pltpu.roll(wide, 32, 1)[0:1],
        jnp.where(lane < 64, pltpu.roll(wide, 64, 1)[1:2], pltpu.roll(wide, 96, 1)[2:3]),
    )
    inverse = lax.rsqrt(square / width + norm_epsilon)
    own = own_key[...].astype(jnp.float32)
    other = other_key[...].astype(jnp.float32)
    gain_rows = gain[...].astype(jnp.float32)
    front = jnp.where(even, own, other) * inverse * gain_rows[:HALF]
    back = jnp.where(even, other, own) * inverse * gain_rows[HALF:]
    front, back = rotated(front, back, cosine[...], sine[...])
    keys_out[...] = jnp.where(even, front, back).astype(jnp.bfloat16)
    keys = jnp.concatenate([front, back], axis=0).astype(jnp.bfloat16)
    scores = lax.dot_general(
        keys, query[...], (((0,), (0,)), ((), ())), preferred_element_type=jnp.float32
    ) * (HEAD_DIM ** (-0.5))
    visible = mask[...] > 0.5
    scores = jnp.where(visible, scores, masked_score)
    top = jnp.max(scores, axis=0, keepdims=True)
    weights = jnp.where(visible, jnp.exp(scores - top), 0.0)
    total = jnp.sum(weights, axis=0, keepdims=True)
    mixed_out[...] = jnp.dot(
        values[...], weights.astype(jnp.bfloat16), preferred_element_type=jnp.float32
    )
    stats_out[...] = jnp.concatenate(
        [top, total, jnp.zeros((6, LANES), jnp.float32)], axis=0
    )


def merge_kernel(parts, tree_mixed, tree_stats, drafted, out):
    count = parts.shape[0]
    top_tree = tree_stats[0:1]
    tops = []
    totals = []
    for source in range(count):
        stats = unpacked(parts[source].astype(jnp.float32))
        tops.append((stats[0:1] + stats[1:2]) + stats[2:3])
        totals.append((stats[3:4] + stats[4:5]) + stats[5:6])
    top = functools.reduce(jnp.maximum, tops, top_tree)
    factor = jnp.exp(top_tree - top)
    total = factor * tree_stats[1:2]
    mixed = factor * tree_mixed[...]
    for source in range(count):
        factor = jnp.exp(tops[source] - top)
        total = total + factor * totals[source]
        mixed = mixed + factor * parts[source].astype(jnp.float32)
    spare = lax.broadcasted_iota(jnp.int32, (HALF, LANES), 1) >= 96
    result = jnp.where(spare, drafted[...].astype(jnp.float32), mixed / total).astype(jnp.bfloat16)
    for target in range(count):
        out[target] = result


def vmem(count):
    return [pl.BlockSpec(memory_space=pltpu.VMEM)] * count


SMEM = pl.BlockSpec(memory_space=pltpu.SMEM)


def broadcast_gather(chunk, count):
    copies = jnp.broadcast_to(chunk[None], (count,) + chunk.shape)
    return lax.all_to_all(copies, "mp", 0, 0)


def per_device(
    draft_hidden,
    draft_weight,
    vocab_weight,
    tree_inputs,
    tree_parent,
    cache_len,
    page_table,
    kv_cache,
    accepted_node,
    qkv_weight,
    norm_gains,
    out_weight,
    gate_up_weight,
    down_weight,
):
    mp_count = lax.axis_size("mp")
    req_count = lax.axis_size("req")
    mp_place = lax.axis_index("mp")
    req_place = lax.axis_index("req")
    req_local, model_width = draft_hidden.shape
    draft_count = draft_weight.shape[0]
    slab = draft_weight.shape[2]
    vocab_local = vocab_weight.shape[0]
    rows = tree_inputs.shape[0]
    tree_size = tree_parent.shape[1]
    page_count, _, page_len, _ = kv_cache.shape
    table_width = page_table.shape[1]
    bf16 = jnp.bfloat16
    f32 = jnp.float32

    own = jnp.einsum("td,dce->cet", tree_inputs, qkv_weight, preferred_element_type=f32).astype(bf16)
    key_part = own[1].astype(f32)
    square = jnp.sum(key_part * key_part, axis=0)
    square_top = lax.reduce_precision(square, 8, 7)
    square_rest = lax.reduce_precision(square - square_top, 8, 7)
    packed = jnp.concatenate([square_top.reshape(3, 32), square_rest.reshape(3, 32)], axis=0)
    packed = jnp.pad(packed, ((0, slab - 6), (0, 0))).astype(bf16)
    gathered = broadcast_gather(jnp.concatenate([own[0], packed], axis=1), mp_count)
    other_key = lax.ppermute(own[1], "mp", [(i, i ^ 1) for i in range(mp_count)])

    pair = lax.ppermute(draft_hidden, "req", [(i, i ^ 1) for i in range(req_count)])
    both = jnp.concatenate([draft_hidden, pair], axis=0)
    turns = req_count // 2
    hidden_parts = [both] + [
        lax.ppermute(both, "req", [(i, (i + 2 * k) % req_count) for i in range(req_count)])
        for k in range(1, turns)
    ]
    hidden_all = jnp.concatenate(hidden_parts, axis=0)
    spot = jnp.arange(req_count * req_local, dtype=jnp.int32)
    turn = spot // (2 * req_local)
    side = (spot // req_local) % 2
    holder = 2 * ((req_place // 2 - turn) % turns) + ((req_place % 2) ^ side)
    origin = holder * req_local + spot % req_local
    order = (origin[None, :] == spot[:, None]).astype(bf16)
    hidden_all = jnp.dot(order, hidden_all, preferred_element_type=f32).astype(bf16)
    draft_raw = jnp.einsum("rd,kde->erk", hidden_all, draft_weight, preferred_element_type=f32)
    own_columns = lax.dynamic_slice_in_dim(hidden_all, mp_place * slab, slab, 1).astype(f32).T
    drafted = (own_columns[:, :, None] + jax.nn.silu(draft_raw)).astype(bf16)
    drafted = drafted.reshape(slab, req_count * req_local * draft_count)

    ancestry, node_depth = tree_shape(tree_parent)
    positions = (cache_len[:, None].astype(f32) + node_depth - 1.0).reshape(rows)
    freqs = rope_base ** (-jnp.arange(HALF, dtype=f32) * 2.0 / HEAD_DIM)
    angles = jnp.pad(positions, (0, LANES - rows))[None, :] * freqs[:, None]
    cosine = jnp.cos(angles)
    sine = jnp.sin(angles)
    mask = jnp.zeros((LANES, LANES), f32)
    for r in range(req_local):
        mask = lax.dynamic_update_slice(mask, ancestry[r].T, (r * tree_size, r * tree_size))
    gain_rows = norm_gains.astype(f32)
    query_gain = jnp.broadcast_to(norm_gains[0][:, None], (model_width, LANES))
    key_gain = lax.dynamic_slice_in_dim(
        norm_gains[1], (mp_place // 2) * HEAD_DIM, HEAD_DIM, 0
    )
    key_gain = jnp.broadcast_to(key_gain[:, None], (HEAD_DIM, LANES))

    slots = (req_place * mp_count + mp_place) * page_count + jnp.arange(page_count, dtype=jnp.int32)
    matches = page_table[None, :, :] == slots[:, None, None]
    starts = jnp.arange(table_width, dtype=jnp.int32) * page_len
    left = jnp.clip(cache_len[:, None] - starts[None, :], 0, page_len)
    counts = jnp.sum(jnp.where(matches, left[None], 0), axis=2).reshape(page_count * req_local)

    groups = 4
    parts, queries, key_square = pl.pallas_call(
        functools.partial(pages_kernel, tree_size),
        out_shape=(
            jax.ShapeDtypeStruct((mp_count, slab, LANES), bf16),
            jax.ShapeDtypeStruct((model_width, LANES), bf16),
            jax.ShapeDtypeStruct((8, LANES), f32),
        ),
        in_specs=[SMEM, *vmem(4), pl.BlockSpec(memory_space=pl.ANY)],
        out_specs=tuple(vmem(3)),
        scratch_shapes=[
            pltpu.VMEM(kv_cache.shape, bf16),
            pltpu.SemaphoreType.DMA((groups,)),
        ],
        compiler_params=pltpu.CompilerParams(vmem_limit_bytes=24 * 2**20),
        cost_estimate=pl.CostEstimate(
            flops=4 * page_count * page_len * LANES * model_width,
            bytes_accessed=kv_cache.size * 2,
            transcendentals=page_count * page_len * LANES * HEADS,
        ),
        name="pages",
    )(counts, gathered, query_gain, cosine, sine, kv_cache)
    arrived = lax.all_to_all(parts, "mp", 0, 0)

    wide = lambda a: jnp.pad(a, ((0, 0), (0, LANES - rows)))
    head_query = lax.dynamic_slice_in_dim(queries, (mp_place // 2) * HEAD_DIM, HEAD_DIM, 0)
    own_keys, tree_mixed, tree_stats = pl.pallas_call(
        tree_kernel,
        out_shape=(
            jax.ShapeDtypeStruct((slab, LANES), bf16),
            jax.ShapeDtypeStruct((slab, LANES), f32),
            jax.ShapeDtypeStruct((8, LANES), f32),
        ),
        in_specs=[SMEM, *vmem(9)],
        out_specs=tuple(vmem(3)),
        name="tree",
    )(
        (mp_place % 2).reshape(1),
        head_query,
        wide(own[1]),
        wide(other_key),
        key_square,
        key_gain,
        cosine,
        sine,
        wide(own[2]),
        mask,
    )

    spare = LANES - rows
    attended_copies = pl.pallas_call(
        merge_kernel,
        out_shape=jax.ShapeDtypeStruct((mp_count, slab, LANES), bf16),
        in_specs=vmem(4),
        out_specs=vmem(1)[0],
        name="merge",
    )(
        arrived,
        tree_mixed,
        tree_stats,
        jnp.pad(drafted[:, :spare], ((0, 0), (rows, 0))),
    )
    attended = lax.all_to_all(attended_copies, "mp", 0, 0).reshape(model_width, LANES)
    out_columns = lax.dot_general(
        out_weight, attended, (((0,), (0,)), ((), ())), preferred_element_type=f32
    ).astype(bf16)
    projected_out = broadcast_gather(
        jnp.concatenate([out_columns[:, :rows], drafted[:, spare:]], axis=1), mp_count
    ).reshape(model_width, LANES)

    projected_rows = projected_out[:, :rows].astype(f32)
    mean_square = jnp.mean(projected_rows * projected_rows, axis=0, keepdims=True)
    residual = (
        tree_inputs.T.astype(f32)
        + projected_rows * lax.rsqrt(mean_square + norm_epsilon) * gain_rows[2][:, None]
    ).astype(bf16)
    gate_up = jnp.einsum("dt,dce->tce", residual, gate_up_weight, preferred_element_type=f32)
    hidden = (jax.nn.silu(gate_up[:, 0]) * gate_up[:, 1]).astype(bf16)
    row_share = rows // mp_count
    partial = jnp.dot(hidden, down_weight, preferred_element_type=f32).astype(bf16)
    shares = lax.all_to_all(partial.reshape(mp_count, row_share, model_width), "mp", 0, 0)

    drafted_all = jnp.concatenate([attended[:, rows:], projected_out[:, rows:]], axis=1)
    draft_logits = lax.dot_general(
        drafted_all, vocab_weight, (((0,), (1,)), ((), ())), preferred_element_type=f32
    ).reshape(req_count * req_local, draft_count, vocab_local)
    chosen = (accepted_node[:, None] == jnp.arange(tree_size, dtype=jnp.int32)[None, :]).astype(f32)
    on_path = jnp.einsum("rt,rts->rs", chosen, ancestry, precision=lax.Precision.HIGHEST)
    levels = jnp.arange(1, draft_count + 1, dtype=f32)
    picker = on_path[:, None, :] * (node_depth[:, None, :] == levels[None, :, None]).astype(f32)
    stacked = jnp.stack([own_keys[:, :rows], own[2]]).reshape(2, slab, req_local, tree_size)
    accepted_kv = jnp.einsum(
        "rjs,cers->rjce", picker.astype(bf16), stacked, preferred_element_type=f32
    ).astype(bf16)
    residual_rows = lax.dynamic_slice_in_dim(residual, mp_place * row_share, row_share, 1).T
    own_rows = jnp.sum(shares.astype(f32), axis=0)
    row_square = jnp.mean(own_rows * own_rows, axis=-1, keepdims=True)
    layer_out = (
        residual_rows.astype(f32)
        + own_rows * lax.rsqrt(row_square + norm_epsilon) * gain_rows[3]
    ).astype(bf16)
    return (draft_logits, layer_out, accepted_kv)


def solution(mesh):
    placed = (
        P("req", None),
        P(None, None, "mp"),
        P(("req", "mp"), None),
        P("req", None),
        P("req", None),
        P("req"),
        P("req", None),
        P(("req", "mp"), None, None, None),
        P("req"),
        P(None, None, "mp"),
        P(),
        P(None, "mp"),
        P(None, None, "mp"),
        P("mp", None),
    )
    return jax.shard_map(
        per_device,
        mesh=mesh,
        in_specs=placed,
        out_specs=(
            P(None, None, ("req", "mp")),
            P(("req", "mp"), None),
            P("req", None, None, "mp"),
        ),
        check_vma=False,
    )
```

```python
import functools

import jax
import jax.numpy as jnp
from jax import lax
from jax.experimental import pallas as pl
from jax.experimental.pallas import tpu as pltpu
from jax.sharding import PartitionSpec as P

HEADS = 16
HEAD_DIM = 128
HALF = HEAD_DIM // 2
LANES = 128

rope_base = 500000.0
norm_epsilon = 1e-06
masked_score = -1e30


def tree_shape(parents):
    node_count = parents.shape[-1]
    step_one = (
        parents[..., :, None] == jnp.arange(node_count, dtype=jnp.int32)[None, None, :]
    ).astype(jnp.float32)
    step_two = jnp.einsum("rij,rjk->rik", step_one, step_one, precision=lax.Precision.HIGHEST)
    step_three = jnp.einsum("rij,rjk->rik", step_two, step_one, precision=lax.Precision.HIGHEST)
    ancestry = jnp.eye(node_count, dtype=jnp.float32)[None] + step_one + step_two + step_three
    return (ancestry, jnp.sum(ancestry, axis=-1))


def split_three(value):
    top = value.astype(jnp.bfloat16).astype(jnp.float32)
    rest = value - top
    middle = rest.astype(jnp.bfloat16).astype(jnp.float32)
    return top, middle, (rest - middle).astype(jnp.bfloat16).astype(jnp.float32)


def in_first(rows):
    return lax.broadcasted_iota(jnp.int32, (rows, LANES), 1) < HALF


def paired(left, right):
    first = in_first(left.shape[0])
    return (
        jnp.where(first, left, pltpu.roll(right, HALF, 1)),
        jnp.where(first, pltpu.roll(left, HALF, 1), right),
    )


def packed_inverse(squares, width):
    first = in_first(squares.shape[0])
    zero = jnp.zeros_like(squares)
    left = jnp.sum(jnp.where(first, squares, zero), axis=1, keepdims=True)
    right = jnp.sum(jnp.where(first, zero, squares), axis=1, keepdims=True)
    return lax.rsqrt(jnp.where(first, left, right) / width + norm_epsilon)


def columns_to_rows(columns):
    rest = LANES - columns.shape[0]
    return jnp.concatenate([columns, jnp.zeros((rest, LANES), jnp.float32)], axis=0).T


def pages_kernel(
    counts, owners, gathered, gains, cosine, sine, cache, out, queries, key_square, kv, held, sems
):
    pages, _, page_len, width = cache.shape
    nodes = cosine.shape[0]
    groups = sems.shape[0]
    group_width = width // groups

    def fetch(group):
        columns = pl.ds(group * group_width, group_width)
        return pltpu.make_async_copy(
            cache.at[:, :, :, columns], kv.at[:, :, :, columns], sems.at[group]
        )

    for group in range(groups):
        fetch(group).start()
    squares = jnp.zeros((nodes, LANES), jnp.float32)
    extra = jnp.zeros((8, LANES), jnp.float32)
    for source in range(2 * HEADS):
        chunk = gathered[source].astype(jnp.float32)
        squares = squares + chunk[:nodes] * chunk[:nodes]
        extra = extra + chunk[nodes : nodes + 8]
    inverse = packed_inverse(squares, width)
    key_square[...] = extra
    token = lax.broadcasted_iota(jnp.int32, (nodes, page_len), 1)
    bias = [jnp.where(token < counts[page], 0.0, masked_score) for page in range(pages)]
    second = [jnp.full((nodes, LANES), owners[page], jnp.int32) == 1 for page in range(pages)]
    scale = HEAD_DIM ** (-0.5)
    cos_rows = cosine[...]
    sin_rows = sine[...]
    lane = lax.broadcasted_iota(jnp.int32, (nodes, LANES), 1)
    stats = jnp.zeros((nodes, LANES), jnp.float32)
    for head in range(HEADS):
        if head % (HEADS // groups) == 0:
            fetch(head // (HEADS // groups)).wait()
        base = head * HEAD_DIM
        front = gathered[2 * head][:nodes].astype(jnp.float32) * inverse * gains[2 * head : 2 * head + 1]
        back = gathered[2 * head + 1][:nodes].astype(jnp.float32) * inverse * gains[2 * head + 1 : 2 * head + 2]
        front, back = rotated(front, back, cos_rows, sin_rows)
        mine = paired(front, back)
        both = jnp.concatenate(mine, axis=0).astype(jnp.bfloat16)
        queries[head] = both
        scores = []
        for page in range(pages):
            asked = jnp.where(second[page], mine[1], mine[0]).astype(jnp.bfloat16)
            keys = kv[page, 0, :, base : base + HEAD_DIM]
            score = lax.dot_general(
                asked, keys, (((1,), (1,)), ((), ())), preferred_element_type=jnp.float32
            )
            scores.append(score * scale + bias[page])
        low = jnp.full((nodes, LANES), masked_score, jnp.float32)
        tops = []
        for request in range(2):
            best = functools.reduce(
                jnp.maximum,
                [
                    jnp.where(second[page] == (request == 1), scores[page], low)
                    for page in range(pages)
                ],
            )
            tops.append(jnp.max(best, axis=1, keepdims=True))
        zero = jnp.zeros((nodes, LANES), jnp.float32)
        sums = [zero, zero]
        mixed = [zero, zero]
        for page in range(pages):
            weight = jnp.exp(scores[page] - jnp.where(second[page], tops[1], tops[0]))
            values = kv[page, 1, :, base : base + HEAD_DIM]
            share = jnp.dot(
                weight.astype(jnp.bfloat16), values, preferred_element_type=jnp.float32
            )
            for request in range(2):
                mine_too = second[page] == (request == 1)
                sums[request] = sums[request] + jnp.where(mine_too, weight, zero)
                mixed[request] = mixed[request] + jnp.where(mine_too, share, zero)
        found = [*tops, *[jnp.sum(part, axis=1, keepdims=True) for part in sums]]
        for place, column in enumerate(found):
            stats = jnp.where(lane == place * HEADS + head, column, stats)
        left, right = paired(mixed[0], mixed[1])
        held[2 * head] = left
        held[2 * head + 1] = right
    turned = columns_to_rows(stats)
    first = in_first(HEADS)

    def by_request(place):
        left = turned[place * HEADS : (place + 1) * HEADS]
        right = turned[(place + 1) * HEADS : (place + 2) * HEADS]
        return jnp.where(first, left, pltpu.roll(right, HALF, 1))

    rows = [*split_three(by_request(0)), *split_three(by_request(2))]
    rows += [jnp.zeros_like(rows[0])] * 2
    for head in range(HEADS):
        tail = jnp.concatenate([row[head : head + 1] for row in rows], axis=0)
        for half in range(2):
            block = jnp.concatenate([held[2 * head + half], tail], axis=0)
            out[2 * head + half] = block.astype(jnp.bfloat16)


def tree_kernel(
    place,
    accepted,
    queries,
    own_key,
    other_key,
    own_value,
    key_square,
    gains,
    cosine,
    sine,
    ancestry,
    depth,
    path_out,
    mixed_out,
    stats_out,
):
    width = 2 * HEADS * HALF
    requests, nodes, _ = ancestry.shape
    head = place[0] // 2
    even = jnp.full((nodes, LANES), place[0] % 2, jnp.int32) == 0
    first = in_first(nodes)
    sums = key_square[0:1] + key_square[1:2]
    square = jnp.broadcast_to(sums, (LANES, LANES)).T
    square = jnp.where(first, square[:nodes], square[nodes : 2 * nodes])
    inverse = lax.rsqrt(square / width + norm_epsilon)
    own = own_key[...].astype(jnp.float32)
    other = other_key[...].astype(jnp.float32)
    front = jnp.where(even, own, other) * inverse * gains[pl.ds(2 * head, 1)]
    back = jnp.where(even, other, own) * inverse * gains[pl.ds(2 * head + 1, 1)]
    front, back = rotated(front, back, cosine[...], sine[...])
    kept = jnp.where(even, front, back).astype(jnp.bfloat16)
    keys = paired(front, back)
    value = own_value[...]
    query = queries[head]
    lane = lax.broadcasted_iota(jnp.int32, (nodes, LANES), 1)
    stats = jnp.zeros((nodes, LANES), jnp.float32)
    mixed = []
    pickers = []
    for request in range(requests):
        line = ancestry[request]
        scores = lax.dot_general(
            query[request * nodes : (request + 1) * nodes],
            keys[request].astype(jnp.bfloat16),
            (((1,), (1,)), ((), ())),
            preferred_element_type=jnp.float32,
        ) * (HEAD_DIM ** (-0.5))
        visible = line > 0.5
        scores = jnp.where(visible, scores, masked_score)
        top = jnp.max(scores, axis=1, keepdims=True)
        weights = jnp.where(visible, jnp.exp(scores - top), 0.0)
        total = jnp.sum(weights, axis=1, keepdims=True)
        mixed.append(jnp.dot(weights.astype(jnp.bfloat16), value, preferred_element_type=jnp.float32))
        stats = jnp.where(lane == request, top, stats)
        stats = jnp.where(lane == request + 2, total, stats)
        on_path = ancestry[request, pl.ds(accepted[request], 1), :]
        levels = depth[pl.ds(request, 1), :]
        wanted = (lax.broadcasted_iota(jnp.int32, (8, nodes), 0) + 1).astype(jnp.float32)
        picker = jnp.where(wanted == levels, on_path, 0.0).astype(jnp.bfloat16)
        pickers.append(picker)
    mixed_out[...] = jnp.where(first, mixed[0], mixed[1])
    turned = columns_to_rows(stats)
    row = in_first(1)
    stats_out[0:1] = jnp.where(row, turned[0:1], pltpu.roll(turned[1:2], HALF, 1))
    stats_out[1:2] = jnp.where(row, turned[2:3], pltpu.roll(turned[3:4], HALF, 1))
    for kind, block in enumerate((kept, value)):
        picked = [
            jnp.dot(picker, block, preferred_element_type=jnp.float32) for picker in pickers
        ]
        path_out[kind] = jnp.where(in_first(8), picked[0], picked[1])


def merge_kernel(parts, tree_mixed, tree_stats, drafted, out):
    count = parts.shape[0]
    nodes = tree_mixed.shape[0]
    top_tree = tree_stats[0:1]
    tops = []
    totals = []
    for source in range(count):
        tail = parts[source].astype(jnp.float32)[nodes : nodes + 8]
        tops.append((tail[0:1] + tail[1:2]) + tail[2:3])
        totals.append((tail[3:4] + tail[4:5]) + tail[5:6])
    tops = jnp.concatenate(tops, axis=0)
    totals = jnp.concatenate(totals, axis=0)
    top = jnp.maximum(jnp.max(tops, axis=0, keepdims=True), top_tree)
    factors = jnp.exp(tops - top)
    factor_tree = jnp.exp(top_tree - top)
    total = jnp.sum(factors * totals, axis=0, keepdims=True) + factor_tree * tree_stats[1:2]
    shares = jnp.concatenate([factors / total, factor_tree / total], axis=0)
    turned = columns_to_rows(shares)
    first = in_first(nodes)

    def spread(source):
        return jnp.where(
            first,
            turned[0:nodes, source : source + 1],
            turned[HALF : HALF + nodes, source : source + 1],
        )

    mixed = spread(count) * tree_mixed[...]
    for source in range(count):
        mixed = mixed + spread(source) * parts[source].astype(jnp.float32)[:nodes]
    result = jnp.concatenate([mixed, drafted[...].astype(jnp.float32)], axis=0).astype(jnp.bfloat16)
    for target in range(count):
        out[target] = result


def out_kernel(gathered, weight, drafted, out):
    count = gathered.shape[0]
    nodes = gathered.shape[1] - drafted.shape[0]
    total = jnp.zeros((2 * nodes, LANES), jnp.float32)
    for head in range(count // 2):
        both = paired(
            gathered[2 * head][:nodes].astype(jnp.float32),
            gathered[2 * head + 1][:nodes].astype(jnp.float32),
        )
        block = jnp.concatenate(both, axis=0).astype(jnp.bfloat16)
        total = total + lax.dot_general(
            block,
            weight[:, head * HEAD_DIM : (head + 1) * HEAD_DIM],
            (((1,), (1,)), ((), ())),
            preferred_element_type=jnp.float32,
        )
    packed = jnp.where(in_first(nodes), total[:nodes], total[nodes:])
    result = jnp.concatenate([packed, drafted[...].astype(jnp.float32)], axis=0).astype(jnp.bfloat16)
    for target in range(count):
        out[target] = result


def residual_kernel(gathered, gain, inputs, out):
    count = gathered.shape[0]
    nodes = inputs.shape[0] // 2
    squares = jnp.zeros((nodes, LANES), jnp.float32)
    for source in range(count):
        chunk = gathered[source].astype(jnp.float32)[:nodes]
        squares = squares + chunk * chunk
    inverse = packed_inverse(squares, count * HALF)
    for head in range(count // 2):
        both = paired(
            gathered[2 * head].astype(jnp.float32)[:nodes] * inverse,
            gathered[2 * head + 1].astype(jnp.float32)[:nodes] * inverse,
        )
        columns = slice(head * HEAD_DIM, (head + 1) * HEAD_DIM)
        block = jnp.concatenate(both, axis=0) * gain[:, columns]
        out[:, columns] = (inputs[:, columns].astype(jnp.float32) + block).astype(jnp.bfloat16)


def split_three(value):
    top = value.astype(jnp.bfloat16).astype(jnp.float32)
    rest = value - top
    middle = rest.astype(jnp.bfloat16).astype(jnp.float32)
    return top, middle, (rest - middle).astype(jnp.bfloat16).astype(jnp.float32)


def in_first(rows):
    return lax.broadcasted_iota(jnp.int32, (rows, LANES), 1) < HALF


def paired(left, right):
    first = in_first(left.shape[0])
    return (
        jnp.where(first, left, pltpu.roll(right, HALF, 1)),
        jnp.where(first, pltpu.roll(left, HALF, 1), right),
    )


def packed_inverse(squares, width):
    first = in_first(squares.shape[0])
    zero = jnp.zeros_like(squares)
    left = jnp.sum(jnp.where(first, squares, zero), axis=1, keepdims=True)
    right = jnp.sum(jnp.where(first, zero, squares), axis=1, keepdims=True)
    return lax.rsqrt(jnp.where(first, left, right) / width + norm_epsilon)


def columns_to_rows(columns):
    rest = LANES - columns.shape[0]
    return jnp.concatenate([columns, jnp.zeros((rest, LANES), jnp.float32)], axis=0).T


def pages_kernel(
    counts, owners, gathered, gains, cosine, sine, cache, out, queries, key_square, kv, held, sems
):
    pages, _, page_len, width = cache.shape
    nodes = cosine.shape[0]
    groups = sems.shape[0]
    group_width = width // groups

    def fetch(group):
        columns = pl.ds(group * group_width, group_width)
        return pltpu.make_async_copy(
            cache.at[:, :, :, columns], kv.at[:, :, :, columns], sems.at[group]
        )

    for group in range(groups):
        fetch(group).start()
    squares = jnp.zeros((nodes, LANES), jnp.float32)
    extra = jnp.zeros((8, LANES), jnp.float32)
    for source in range(2 * HEADS):
        chunk = gathered[source].astype(jnp.float32)
        squares = squares + chunk[:nodes] * chunk[:nodes]
        extra = extra + chunk[nodes : nodes + 8]
    inverse = packed_inverse(squares, width)
    key_square[...] = extra
    token = lax.broadcasted_iota(jnp.int32, (nodes, page_len), 1)
    bias = [jnp.where(token < counts[page], 0.0, masked_score) for page in range(pages)]
    second = [jnp.full((nodes, LANES), owners[page], jnp.int32) == 1 for page in range(pages)]
    scale = HEAD_DIM ** (-0.5)
    cos_rows = cosine[...]
    sin_rows = sine[...]
    lane = lax.broadcasted_iota(jnp.int32, (nodes, LANES), 1)
    stats = jnp.zeros((nodes, LANES), jnp.float32)
    for head in range(HEADS):
        if head % (HEADS // groups) == 0:
            fetch(head // (HEADS // groups)).wait()
        base = head * HEAD_DIM
        front = gathered[2 * head][:nodes].astype(jnp.float32) * inverse * gains[2 * head : 2 * head + 1]
        back = gathered[2 * head + 1][:nodes].astype(jnp.float32) * inverse * gains[2 * head + 1 : 2 * head + 2]
        front, back = rotated(front, back, cos_rows, sin_rows)
        mine = paired(front, back)
        both = jnp.concatenate(mine, axis=0).astype(jnp.bfloat16)
        queries[head] = both
        scores = []
        for page in range(pages):
            asked = jnp.where(second[page], mine[1], mine[0]).astype(jnp.bfloat16)
            keys = kv[page, 0, :, base : base + HEAD_DIM]
            score = lax.dot_general(
                asked, keys, (((1,), (1,)), ((), ())), preferred_element_type=jnp.float32
            )
            scores.append(score * scale + bias[page])
        low = jnp.full((nodes, LANES), masked_score, jnp.float32)
        tops = []
        for request in range(2):
            best = functools.reduce(
                jnp.maximum,
                [
                    jnp.where(second[page] == (request == 1), scores[page], low)
                    for page in range(pages)
                ],
            )
            tops.append(jnp.max(best, axis=1, keepdims=True))
        zero = jnp.zeros((nodes, LANES), jnp.float32)
        sums = [zero, zero]
        mixed = [zero, zero]
        for page in range(pages):
            weight = jnp.exp(scores[page] - jnp.where(second[page], tops[1], tops[0]))
            values = kv[page, 1, :, base : base + HEAD_DIM]
            share = jnp.dot(
                weight.astype(jnp.bfloat16), values, preferred_element_type=jnp.float32
            )
            for request in range(2):
                mine_too = second[page] == (request == 1)
                sums[request] = sums[request] + jnp.where(mine_too, weight, zero)
                mixed[request] = mixed[request] + jnp.where(mine_too, share, zero)
        found = [*tops, *[jnp.sum(part, axis=1, keepdims=True) for part in sums]]
        for place, column in enumerate(found):
            stats = jnp.where(lane == place * HEADS + head, column, stats)
        left, right = paired(mixed[0], mixed[1])
        held[2 * head] = left
        held[2 * head + 1] = right
    turned = columns_to_rows(stats)
    first = in_first(HEADS)

    def by_request(place):
        left = turned[place * HEADS : (place + 1) * HEADS]
        right = turned[(place + 1) * HEADS : (place + 2) * HEADS]
        return jnp.where(first, left, pltpu.roll(right, HALF, 1))

    rows = [*split_three(by_request(0)), *split_three(by_request(2))]
    rows += [jnp.zeros_like(rows[0])] * 2
    for head in range(HEADS):
        tail = jnp.concatenate([row[head : head + 1] for row in rows], axis=0)
        for half in range(2):
            block = jnp.concatenate([held[2 * head + half], tail], axis=0)
            out[2 * head + half] = block.astype(jnp.bfloat16)


def tree_kernel(
    place,
    accepted,
    queries,
    own_key,
    other_key,
    own_value,
    key_square,
    gains,
    cosine,
    sine,
    ancestry,
    depth,
    path_out,
    mixed_out,
    stats_out,
):
    width = 2 * HEADS * HALF
    requests, nodes, _ = ancestry.shape
    head = place[0] // 2
    even = jnp.full((nodes, LANES), place[0] % 2, jnp.int32) == 0
    first = in_first(nodes)
    sums = key_square[0:1] + key_square[1:2]
    square = jnp.broadcast_to(sums, (LANES, LANES)).T
    square = jnp.where(first, square[:nodes], square[nodes : 2 * nodes])
    inverse = lax.rsqrt(square / width + norm_epsilon)
    own = own_key[...].astype(jnp.float32)
    other = other_key[...].astype(jnp.float32)
    front = jnp.where(even, own, other) * inverse * gains[pl.ds(2 * head, 1)]
    back = jnp.where(even, other, own) * inverse * gains[pl.ds(2 * head + 1, 1)]
    front, back = rotated(front, back, cosine[...], sine[...])
    kept = jnp.where(even, front, back).astype(jnp.bfloat16)
    keys = paired(front, back)
    value = own_value[...]
    query = queries[head]
    lane = lax.broadcasted_iota(jnp.int32, (nodes, LANES), 1)
    stats = jnp.zeros((nodes, LANES), jnp.float32)
    mixed = []
    pickers = []
    for request in range(requests):
        line = ancestry[request]
        scores = lax.dot_general(
            query[request * nodes : (request + 1) * nodes],
            keys[request].astype(jnp.bfloat16),
            (((1,), (1,)), ((), ())),
            preferred_element_type=jnp.float32,
        ) * (HEAD_DIM ** (-0.5))
        visible = line > 0.5
        scores = jnp.where(visible, scores, masked_score)
        top = jnp.max(scores, axis=1, keepdims=True)
        weights = jnp.where(visible, jnp.exp(scores - top), 0.0)
        total = jnp.sum(weights, axis=1, keepdims=True)
        mixed.append(jnp.dot(weights.astype(jnp.bfloat16), value, preferred_element_type=jnp.float32))
        stats = jnp.where(lane == request, top, stats)
        stats = jnp.where(lane == request + 2, total, stats)
        on_path = ancestry[request, pl.ds(accepted[request], 1), :]
        levels = depth[pl.ds(request, 1), :]
        wanted = (lax.broadcasted_iota(jnp.int32, (8, nodes), 0) + 1).astype(jnp.float32)
        picker = jnp.where(wanted == levels, on_path, 0.0).astype(jnp.bfloat16)
        pickers.append(picker)
    mixed_out[...] = jnp.where(first, mixed[0], mixed[1])
    turned = columns_to_rows(stats)
    row = in_first(1)
    stats_out[0:1] = jnp.where(row, turned[0:1], pltpu.roll(turned[1:2], HALF, 1))
    stats_out[1:2] = jnp.where(row, turned[2:3], pltpu.roll(turned[3:4], HALF, 1))
    for kind, block in enumerate((kept, value)):
        picked = [
            jnp.dot(picker, block, preferred_element_type=jnp.float32) for picker in pickers
        ]
        path_out[kind] = jnp.where(in_first(8), picked[0], picked[1])


def merge_kernel(parts, tree_mixed, tree_stats, drafted, out):
    count = parts.shape[0]
    nodes = tree_mixed.shape[0]
    top_tree = tree_stats[0:1]
    tops = []
    totals = []
    for source in range(count):
        tail = parts[source].astype(jnp.float32)[nodes : nodes + 8]
        tops.append((tail[0:1] + tail[1:2]) + tail[2:3])
        totals.append((tail[3:4] + tail[4:5]) + tail[5:6])
    tops = jnp.concatenate(tops, axis=0)
    totals = jnp.concatenate(totals, axis=0)
    top = jnp.maximum(jnp.max(tops, axis=0, keepdims=True), top_tree)
    factors = jnp.exp(tops - top)
    factor_tree = jnp.exp(top_tree - top)
    total = jnp.sum(factors * totals, axis=0, keepdims=True) + factor_tree * tree_stats[1:2]
    shares = jnp.concatenate([factors / total, factor_tree / total], axis=0)
    turned = columns_to_rows(shares)
    first = in_first(nodes)

    def spread(source):
        return jnp.where(
            first,
            turned[0:nodes, source : source + 1],
            turned[HALF : HALF + nodes, source : source + 1],
        )

    mixed = spread(count) * tree_mixed[...]
    for source in range(count):
        mixed = mixed + spread(source) * parts[source].astype(jnp.float32)[:nodes]
    result = jnp.concatenate([mixed, drafted[...].astype(jnp.float32)], axis=0).astype(jnp.bfloat16)
    for target in range(count):
        out[target] = result


def out_kernel(gathered, weight, drafted, out):
    count = gathered.shape[0]
    nodes = gathered.shape[1] - drafted.shape[0]
    total = jnp.zeros((2 * nodes, LANES), jnp.float32)
    for head in range(count // 2):
        both = paired(
            gathered[2 * head][:nodes].astype(jnp.float32),
            gathered[2 * head + 1][:nodes].astype(jnp.float32),
        )
        block = jnp.concatenate(both, axis=0).astype(jnp.bfloat16)
        total = total + lax.dot_general(
            block,
            weight[:, head * HEAD_DIM : (head + 1) * HEAD_DIM],
            (((1,), (1,)), ((), ())),
            preferred_element_type=jnp.float32,
        )
    packed = jnp.where(in_first(nodes), total[:nodes], total[nodes:])
    result = jnp.concatenate([packed, drafted[...].astype(jnp.float32)], axis=0).astype(jnp.bfloat16)
    for target in range(count):
        out[target] = result


def residual_kernel(gathered, gain, inputs, out):
    count = gathered.shape[0]
    nodes = inputs.shape[0] // 2
    squares = jnp.zeros((nodes, LANES), jnp.float32)
    for source in range(count):
        chunk = gathered[source].astype(jnp.float32)[:nodes]
        squares = squares + chunk * chunk
    inverse = packed_inverse(squares, count * HALF)
    for head in range(count // 2):
        both = paired(
            gathered[2 * head].astype(jnp.float32)[:nodes] * inverse,
            gathered[2 * head + 1].astype(jnp.float32)[:nodes] * inverse,
        )
        columns = slice(head * HEAD_DIM, (head + 1) * HEAD_DIM)
        block = jnp.concatenate(both, axis=0) * gain[:, columns]
        out[:, columns] = (inputs[:, columns].astype(jnp.float32) + block).astype(jnp.bfloat16)


def rotated(front, back, cosine, sine):
    return front * cosine - back * sine, back * cosine + front * sine


def vmem(count):
    return [pl.BlockSpec(memory_space=pltpu.VMEM)] * count


SMEM = pl.BlockSpec(memory_space=pltpu.SMEM)


def broadcast_gather(chunk, count):
    copies = jnp.broadcast_to(chunk[None], (count,) + chunk.shape)
    return lax.all_to_all(copies, "mp", 0, 0)


def per_device(
    draft_hidden,
    draft_weight,
    vocab_weight,
    tree_inputs,
    tree_parent,
    cache_len,
    page_table,
    kv_cache,
    accepted_node,
    qkv_weight,
    norm_gains,
    out_weight,
    gate_up_weight,
    down_weight,
):
    mp_count = lax.axis_size("mp")
    req_count = lax.axis_size("req")
    mp_place = lax.axis_index("mp")
    req_place = lax.axis_index("req")
    req_local, model_width = draft_hidden.shape
    draft_count = draft_weight.shape[0]
    slab = draft_weight.shape[2]
    vocab_local = vocab_weight.shape[0]
    rows = tree_inputs.shape[0]
    tree_size = tree_parent.shape[1]
    page_count, _, page_len, _ = kv_cache.shape
    table_width = page_table.shape[1]
    bf16 = jnp.bfloat16
    f32 = jnp.float32

    own = jnp.einsum(
        "rtd,dce->ctre",
        tree_inputs.reshape(req_local, tree_size, model_width),
        qkv_weight,
        preferred_element_type=f32,
    )
    own = own.astype(bf16).reshape(3, tree_size, LANES)
    key_part = own[1].astype(f32).reshape(tree_size, req_local, slab)
    square = jnp.sum(key_part * key_part, axis=2).T.reshape(1, rows)
    square_top = lax.reduce_precision(square, 8, 7)
    square_rest = lax.reduce_precision(square - square_top, 8, 7)
    extra = jnp.concatenate([square_top, square_rest], axis=0).astype(bf16)
    extra = jnp.pad(extra, ((0, 6), (0, LANES - rows)))
    gathered = broadcast_gather(jnp.concatenate([own[0], extra], axis=0), mp_count)
    other_key = lax.ppermute(own[1], "mp", [(i, i ^ 1) for i in range(mp_count)])

    pair = lax.ppermute(draft_hidden, "req", [(i, i ^ 1) for i in range(req_count)])
    both = jnp.concatenate([draft_hidden, pair], axis=0)
    turns = req_count // 2
    hidden_parts = [both] + [
        lax.ppermute(both, "req", [(i, (i + 2 * k) % req_count) for i in range(req_count)])
        for k in range(1, turns)
    ]
    hidden_all = jnp.concatenate(hidden_parts, axis=0)
    spot = jnp.arange(req_count * req_local, dtype=jnp.int32)
    turn = spot // (2 * req_local)
    side = (spot // req_local) % 2
    holder = 2 * ((req_place // 2 - turn) % turns) + ((req_place % 2) ^ side)
    origin = holder * req_local + spot % req_local
    order = (origin[None, :] == spot[:, None]).astype(bf16)
    hidden_all = jnp.dot(order, hidden_all, preferred_element_type=f32).astype(bf16)
    draft_raw = jnp.einsum("rd,kde->rke", hidden_all, draft_weight, preferred_element_type=f32)
    own_columns = lax.dynamic_slice_in_dim(hidden_all, mp_place * slab, slab, 1).astype(f32)
    drafted = (own_columns[:, None, :] + jax.nn.silu(draft_raw)).astype(bf16)
    half_count = req_count * req_local * draft_count // 2
    drafted = drafted.reshape(2, half_count, slab)
    drafted = jnp.concatenate([drafted[0], drafted[1]], axis=1)

    ancestry, node_depth = tree_shape(tree_parent)
    positions = cache_len[:, None].astype(f32) + node_depth - 1.0
    freqs = rope_base ** (-jnp.arange(HALF, dtype=f32) * 2.0 / HEAD_DIM)
    angles = positions.T[:, :, None] * freqs[None, None, :]
    angles = angles.reshape(tree_size, LANES)
    cosine = jnp.cos(angles)
    sine = jnp.sin(angles)
    gain_rows = norm_gains.astype(f32)
    twice = gain_rows[:2].reshape(2, mp_count, slab)
    twice = jnp.concatenate([twice, twice], axis=2)

    slots = (req_place * mp_count + mp_place) * page_count + jnp.arange(page_count, dtype=jnp.int32)
    matches = page_table[None, :, :] == slots[:, None, None]
    starts = jnp.arange(table_width, dtype=jnp.int32) * page_len
    left = jnp.clip(cache_len[:, None] - starts[None, :], 0, page_len)
    counts = jnp.sum(jnp.where(matches, left[None], 0), axis=(1, 2))
    owners = jnp.any(matches[:, 1], axis=1).astype(jnp.int32)

    groups = 4
    parts, queries, key_square = pl.pallas_call(
        pages_kernel,
        out_shape=(
            jax.ShapeDtypeStruct((mp_count, tree_size + 8, LANES), bf16),
            jax.ShapeDtypeStruct((HEADS, rows, HEAD_DIM), bf16),
            jax.ShapeDtypeStruct((8, LANES), f32),
        ),
        in_specs=[SMEM, SMEM, *vmem(4), pl.BlockSpec(memory_space=pltpu.HBM)],
        out_specs=tuple(vmem(3)),
        scratch_shapes=[
            pltpu.VMEM(kv_cache.shape, bf16),
            pltpu.VMEM((mp_count, tree_size, LANES), f32),
            pltpu.SemaphoreType.DMA((groups,)),
        ],
        compiler_params=pltpu.CompilerParams(vmem_limit_bytes=16 * 2**20),
        cost_estimate=pl.CostEstimate(
            flops=4 * page_count * page_len * LANES * model_width,
            bytes_accessed=kv_cache.size * 2,
            transcendentals=page_count * page_len * tree_size * HEADS,
        ),
        name="pages",
    )(counts, owners, gathered, twice[0], cosine, sine, kv_cache)
    arrived = lax.all_to_all(parts, "mp", 0, 0)

    path, tree_mixed, tree_stats = pl.pallas_call(
        tree_kernel,
        out_shape=(
            jax.ShapeDtypeStruct((2, 8, LANES), f32),
            jax.ShapeDtypeStruct((tree_size, LANES), f32),
            jax.ShapeDtypeStruct((2, LANES), f32),
        ),
        in_specs=[SMEM, SMEM, *vmem(10)],
        out_specs=tuple(vmem(3)),
        compiler_params=pltpu.CompilerParams(vmem_limit_bytes=8 * 2**20),
        cost_estimate=pl.CostEstimate(flops=2**24, bytes_accessed=2**20, transcendentals=2**13),
        name="tree",
    )(
        mp_place.reshape(1),
        accepted_node,
        queries,
        own[1],
        other_key,
        own[2],
        key_square,
        twice[1],
        cosine,
        sine,
        ancestry,
        node_depth,
    )
    accepted_kv = jnp.transpose(
        path[:, :draft_count].reshape(2, draft_count, req_local, slab), (2, 1, 0, 3)
    ).astype(bf16)

    ride = half_count // 2
    first_ride, second_ride = drafted[:ride], drafted[ride:]
    out_twice = jnp.concatenate([out_weight.T, out_weight.T], axis=0)
    attended_copies = pl.pallas_call(
        merge_kernel,
        out_shape=jax.ShapeDtypeStruct((mp_count, tree_size + ride, LANES), bf16),
        in_specs=vmem(4),
        out_specs=vmem(1)[0],
        compiler_params=pltpu.CompilerParams(vmem_limit_bytes=8 * 2**20),
        name="merge",
    )(arrived, tree_mixed, tree_stats, first_ride)
    attended_copies, out_twice, second_ride, accepted_kv = lax.optimization_barrier(
        (attended_copies, out_twice, second_ride, accepted_kv)
    )
    attended = lax.all_to_all(attended_copies, "mp", 0, 0)
    out_copies = pl.pallas_call(
        out_kernel,
        out_shape=jax.ShapeDtypeStruct((mp_count, tree_size + ride, LANES), bf16),
        in_specs=vmem(3),
        out_specs=vmem(1)[0],
        compiler_params=pltpu.CompilerParams(vmem_limit_bytes=8 * 2**20),
        name="out_columns",
    )(attended, out_twice, second_ride)
    projected_out = lax.all_to_all(out_copies, "mp", 0, 0)
    residual = pl.pallas_call(
        residual_kernel,
        out_shape=jax.ShapeDtypeStruct((rows, model_width), bf16),
        in_specs=vmem(3),
        out_specs=vmem(1)[0],
        compiler_params=pltpu.CompilerParams(vmem_limit_bytes=8 * 2**20),
        name="residual",
    )(projected_out, gain_rows[2:3], tree_inputs)
    gate_up = jnp.einsum("td,dce->tce", residual, gate_up_weight, preferred_element_type=f32)
    hidden = (jax.nn.silu(gate_up[:, 0]) * gate_up[:, 1]).astype(bf16)
    row_share = rows // mp_count
    partial = jnp.dot(hidden, down_weight, preferred_element_type=f32).astype(bf16)
    shares = lax.all_to_all(partial.reshape(mp_count, row_share, model_width), "mp", 0, 0)

    riders = jnp.concatenate([attended[:, tree_size:], projected_out[:, tree_size:]], axis=1)
    riders = jnp.transpose(riders.reshape(mp_count, half_count, 2, slab), (2, 1, 0, 3))
    draft_logits = lax.dot_general(
        riders.reshape(2 * half_count, model_width),
        vocab_weight,
        (((1,), (1,)), ((), ())),
        preferred_element_type=f32,
    ).reshape(req_count * req_local, draft_count, vocab_local)
    residual_rows = lax.dynamic_slice_in_dim(residual, mp_place * row_share, row_share, 0)
    own_rows = jnp.sum(shares.astype(f32), axis=0)
    row_square = jnp.mean(own_rows * own_rows, axis=-1, keepdims=True)
    layer_out = (
        residual_rows.astype(f32)
        + own_rows * lax.rsqrt(row_square + norm_epsilon) * gain_rows[3]
    ).astype(bf16)
    return (draft_logits, layer_out, accepted_kv)


def solution(mesh):
    placed = (
        P("req", None),
        P(None, None, "mp"),
        P(("req", "mp"), None),
        P("req", None),
        P("req", None),
        P("req"),
        P("req", None),
        P(("req", "mp"), None, None, None),
        P("req"),
        P(None, None, "mp"),
        P(),
        P(None, "mp"),
        P(None, None, "mp"),
        P("mp", None),
    )
    return jax.shard_map(
        per_device,
        mesh=mesh,
        in_specs=placed,
        out_specs=(
            P(None, None, ("req", "mp")),
            P(("req", "mp"), None),
            P("req", None, None, "mp"),
        ),
        check_vma=False,
    )
```

```python
import functools

import jax
import jax.numpy as jnp
from jax import lax
from jax.experimental import pallas as pl
from jax.experimental.pallas import tpu as pltpu
from jax.sharding import PartitionSpec as P

HEADS = 16
HEAD_DIM = 128
HALF = HEAD_DIM // 2
LANES = 128
SIDE = 4

rope_base = 500000.0
norm_epsilon = 1e-06
masked_score = -1e30


def tree_shape(parents):
    node_count = parents.shape[-1]
    step_one = (
        parents[..., :, None] == jnp.arange(node_count, dtype=jnp.int32)[None, None, :]
    ).astype(jnp.float32)
    step_two = jnp.einsum("rij,rjk->rik", step_one, step_one, precision=lax.Precision.HIGHEST)
    step_three = jnp.einsum("rij,rjk->rik", step_two, step_one, precision=lax.Precision.HIGHEST)
    ancestry = jnp.eye(node_count, dtype=jnp.float32)[None] + step_one + step_two + step_three
    return (ancestry, jnp.sum(ancestry, axis=-1))


def split_three(value):
    top = value.astype(jnp.bfloat16).astype(jnp.float32)
    rest = value - top
    middle = rest.astype(jnp.bfloat16).astype(jnp.float32)
    return top, middle, (rest - middle).astype(jnp.bfloat16).astype(jnp.float32)


def in_first(rows):
    return lax.broadcasted_iota(jnp.int32, (rows, LANES), 1) < HALF


def paired(left, right):
    first = in_first(left.shape[0])
    return (
        jnp.where(first, left, pltpu.roll(right, HALF, 1)),
        jnp.where(first, pltpu.roll(left, HALF, 1), right),
    )


def packed_inverse(squares, width):
    first = in_first(squares.shape[0])
    zero = jnp.zeros_like(squares)
    left = jnp.sum(jnp.where(first, squares, zero), axis=1, keepdims=True)
    right = jnp.sum(jnp.where(first, zero, squares), axis=1, keepdims=True)
    return lax.rsqrt(jnp.where(first, left, right) / width + norm_epsilon)


def spot_of(place):
    return place % SIDE * (2 * HEADS // SIDE) + place // SIDE


def columns_to_rows(columns):
    rest = LANES - columns.shape[0]
    return jnp.concatenate([columns, jnp.zeros((rest, LANES), jnp.float32)], axis=0).T


def project_kernel(inputs, weights, copies, own_key, own_value, rows, columns, sems):
    nodes = own_key.shape[0]
    fetches = [pltpu.make_async_copy(inputs, rows, sems.at[0])]
    for kind in range(3):
        fetches.append(pltpu.make_async_copy(weights.at[kind], columns.at[kind], sems.at[1 + kind]))
    for fetch in fetches:
        fetch.start()
    fetches[0].wait()
    first = in_first(nodes)

    def projected(kind):
        fetches[1 + kind].wait()
        weight = columns[kind]
        product = lax.dot_general(
            rows[...],
            jnp.concatenate([weight, weight], axis=0),
            (((1,), (1,)), ((), ())),
            preferred_element_type=jnp.float32,
        )
        return jnp.where(first, product[:nodes], product[nodes:]).astype(jnp.bfloat16)

    query = projected(0)
    key = projected(1)
    own_key[...] = key
    squares = key.astype(jnp.float32)
    squares = squares * squares
    zero = jnp.zeros_like(squares)
    lane = lax.broadcasted_iota(jnp.int32, (nodes, LANES), 1)
    left = jnp.sum(jnp.where(first, squares, zero), axis=1, keepdims=True)
    right = jnp.sum(jnp.where(first, zero, squares), axis=1, keepdims=True)
    turned = columns_to_rows(jnp.where(lane == 0, left, jnp.where(lane == 1, right, zero)))
    sums = jnp.where(in_first(1), turned[0:1], pltpu.roll(turned[1:2], HALF, 1))
    tail = jnp.concatenate([*split_three(sums), jnp.zeros((5, LANES), jnp.float32)], axis=0)
    chunk = jnp.concatenate([query.astype(jnp.float32), tail], axis=0).astype(jnp.bfloat16)
    for target in range(copies.shape[0]):
        copies[target] = chunk
    own_value[...] = projected(2)


def pages_kernel(counts, gathered, gains, cosine, sine, cache, out, queries, key_square, kv, held, sems):
    pages, _, page_len, width = cache.shape
    nodes = cosine.shape[0]
    groups = sems.shape[0]
    group_width = width // groups

    def fetch(group):
        columns = pl.ds(group * group_width, group_width)
        return pltpu.make_async_copy(
            cache.at[:, :, :, columns], kv.at[:, :, :, columns], sems.at[group]
        )

    for group in range(groups):
        fetch(group).start()
    squares = jnp.zeros((nodes, LANES), jnp.float32)
    extra = jnp.zeros((8, LANES), jnp.float32)
    for source in range(2 * HEADS):
        chunk = gathered[source].astype(jnp.float32)
        squares = squares + chunk[:nodes] * chunk[:nodes]
        extra = extra + chunk[nodes : nodes + 8]
    inverse = packed_inverse(squares, width)
    key_square[...] = extra
    token = lax.broadcasted_iota(jnp.int32, (nodes, page_len), 1)
    bias = []
    for page in range(pages):
        halves = [
            jnp.where(token < counts[2 * page + request : 2 * page + request + 1], 0.0, masked_score)
            for request in range(2)
        ]
        bias.append(jnp.concatenate(halves, axis=0))
    scale = HEAD_DIM ** (-0.5)
    cos_rows = cosine[...]
    sin_rows = sine[...]
    lane = lax.broadcasted_iota(jnp.int32, (2 * nodes, LANES), 1)
    stats = jnp.zeros((2 * nodes, LANES), jnp.float32)
    for head in range(HEADS):
        if head % (HEADS // groups) == 0:
            fetch(head // (HEADS // groups)).wait()
        base = head * HEAD_DIM
        front = gathered[spot_of(2 * head)][:nodes].astype(jnp.float32)
        back = gathered[spot_of(2 * head + 1)][:nodes].astype(jnp.float32)
        front = front * inverse * gains[2 * head : 2 * head + 1]
        back = back * inverse * gains[2 * head + 1 : 2 * head + 2]
        front, back = rotated(front, back, cos_rows, sin_rows)
        query = jnp.concatenate(paired(front, back), axis=0).astype(jnp.bfloat16)
        queries[head] = query
        keys = kv[:, 0, :, base : base + HEAD_DIM].reshape(pages * page_len, HEAD_DIM)
        scores = lax.dot_general(
            query, keys, (((1,), (1,)), ((), ())), preferred_element_type=jnp.float32
        )
        scores = [
            scores[:, page * page_len : (page + 1) * page_len] * scale + bias[page]
            for page in range(pages)
        ]
        top = jnp.max(functools.reduce(jnp.maximum, scores), axis=1, keepdims=True)
        weights = [jnp.exp(score - top) for score in scores]
        total = jnp.sum(functools.reduce(jnp.add, weights), axis=1, keepdims=True)
        values = kv[:, 1, :, base : base + HEAD_DIM].reshape(pages * page_len, HEAD_DIM)
        mixed = jnp.dot(
            jnp.concatenate(weights, axis=1).astype(jnp.bfloat16),
            values,
            preferred_element_type=jnp.float32,
        )
        stats = jnp.where(lane == head, top, stats)
        stats = jnp.where(lane == HEADS + head, total, stats)
        left, right = paired(mixed[:nodes], mixed[nodes:])
        held[2 * head] = left
        held[2 * head + 1] = right
    turned = columns_to_rows(stats)
    shifted = pltpu.roll(turned, HALF - nodes, 1)
    turned = jnp.where(in_first(LANES), turned, shifted)
    rows = [*split_three(turned[:HEADS]), *split_three(turned[HEADS : 2 * HEADS])]
    rows += [jnp.zeros_like(rows[0])] * 2
    for head in range(HEADS):
        tail = jnp.concatenate([row[head : head + 1] for row in rows], axis=0)
        for half in range(2):
            block = jnp.concatenate([held[2 * head + half], tail], axis=0)
            out[spot_of(2 * head + half)] = block.astype(jnp.bfloat16)


def tree_kernel(
    place,
    accepted,
    queries,
    own_key,
    other_key,
    own_value,
    key_square,
    gains,
    cosine,
    sine,
    ancestry,
    depth,
    ride,
    large,
    path_out,
    tree_out,
    large_out,
    sem,
):
    copy = pltpu.make_async_copy(large, large_out, sem)
    copy.start()
    width = 2 * HEADS * HALF
    requests, nodes, _ = ancestry.shape
    head = place[0] // 2
    even = jnp.full((nodes, LANES), place[0] % 2, jnp.int32) == 0
    first = in_first(nodes)
    sums = (key_square[0:1] + key_square[1:2]) + key_square[2:3]
    square = jnp.broadcast_to(sums, (LANES, LANES)).T
    square = jnp.where(first, square[:nodes], square[HALF : HALF + nodes])
    inverse = lax.rsqrt(square / width + norm_epsilon)
    own = own_key[...].astype(jnp.float32)
    other = other_key[...].astype(jnp.float32)
    front = jnp.where(even, own, other) * inverse * gains[pl.ds(2 * head, 1)]
    back = jnp.where(even, other, own) * inverse * gains[pl.ds(2 * head + 1, 1)]
    front, back = rotated(front, back, cosine[...], sine[...])
    kept = jnp.where(even, front, back).astype(jnp.bfloat16)
    keys = paired(front, back)
    value = own_value[...]
    query = queries[head]
    lane = lax.broadcasted_iota(jnp.int32, (nodes, LANES), 1)
    stats = jnp.zeros((nodes, LANES), jnp.float32)
    mixed = []
    pickers = []
    for request in range(requests):
        line = ancestry[request]
        scores = lax.dot_general(
            query[request * nodes : (request + 1) * nodes],
            keys[request].astype(jnp.bfloat16),
            (((1,), (1,)), ((), ())),
            preferred_element_type=jnp.float32,
        ) * (HEAD_DIM ** (-0.5))
        visible = line > 0.5
        scores = jnp.where(visible, scores, masked_score)
        top = jnp.max(scores, axis=1, keepdims=True)
        weights = jnp.where(visible, jnp.exp(scores - top), 0.0)
        total = jnp.sum(weights, axis=1, keepdims=True)
        mixed.append(jnp.dot(weights.astype(jnp.bfloat16), value, preferred_element_type=jnp.float32))
        stats = jnp.where(lane == request, top, stats)
        stats = jnp.where(lane == request + 2, total, stats)
        on_path = ancestry[request, pl.ds(accepted[request], 1), :]
        levels = depth[pl.ds(request, 1), :]
        wanted = (lax.broadcasted_iota(jnp.int32, (8, nodes), 0) + 1).astype(jnp.float32)
        picker = jnp.where(wanted == levels, on_path, 0.0).astype(jnp.bfloat16)
        pickers.append(picker)
    turned = columns_to_rows(stats)
    row = in_first(1)
    tail = [
        jnp.where(row, turned[0:1], pltpu.roll(turned[1:2], HALF, 1)),
        jnp.where(row, turned[2:3], pltpu.roll(turned[3:4], HALF, 1)),
        jnp.zeros((6, LANES), jnp.float32),
    ]
    tree_out[...] = jnp.concatenate(
        [jnp.where(first, mixed[0], mixed[1]), *tail, ride[...].astype(jnp.float32)], axis=0
    )
    for kind, block in enumerate((kept, value)):
        picked = [
            jnp.dot(picker, block, preferred_element_type=jnp.float32) for picker in pickers
        ]
        path_out[kind] = jnp.where(in_first(8), picked[0], picked[1])
    copy.wait()


def merge_kernel(parts, tree, out):
    count = parts.shape[0]
    nodes = parts.shape[1] - 8
    top_tree = tree[nodes : nodes + 1]
    tops = []
    totals = []
    for source in range(count):
        tail = parts[source].astype(jnp.float32)[nodes : nodes + 8]
        tops.append((tail[0:1] + tail[1:2]) + tail[2:3])
        totals.append((tail[3:4] + tail[4:5]) + tail[5:6])
    tops = jnp.concatenate(tops, axis=0)
    totals = jnp.concatenate(totals, axis=0)
    top = jnp.maximum(jnp.max(tops, axis=0, keepdims=True), top_tree)
    factors = jnp.exp(tops - top)
    factor_tree = jnp.exp(top_tree - top)
    total = jnp.sum(factors * totals, axis=0, keepdims=True) + factor_tree * tree[nodes + 1 : nodes + 2]
    shares = jnp.concatenate([factors / total, factor_tree / total], axis=0)
    turned = columns_to_rows(shares)
    first = in_first(nodes)

    def spread(source):
        return jnp.where(
            first,
            turned[0:nodes, source : source + 1],
            turned[HALF : HALF + nodes, source : source + 1],
        )

    mixed = spread(count) * tree[:nodes]
    for source in range(count):
        mixed = mixed + spread(source) * parts[source].astype(jnp.float32)[:nodes]
    result = jnp.concatenate([mixed, tree[nodes + 8 :]], axis=0).astype(jnp.bfloat16)
    for target in range(count):
        out[target] = result


def out_kernel(gathered, weight, drafted, out):
    count = gathered.shape[0]
    nodes = gathered.shape[1] - drafted.shape[0]
    total = jnp.zeros((2 * nodes, LANES), jnp.float32)
    for head in range(count // 2):
        both = paired(
            gathered[spot_of(2 * head)][:nodes].astype(jnp.float32),
            gathered[spot_of(2 * head + 1)][:nodes].astype(jnp.float32),
        )
        block = jnp.concatenate(both, axis=0).astype(jnp.bfloat16)
        total = total + lax.dot_general(
            block,
            weight[:, head * HEAD_DIM : (head + 1) * HEAD_DIM],
            (((1,), (1,)), ((), ())),
            preferred_element_type=jnp.float32,
        )
    packed = jnp.where(in_first(nodes), total[:nodes], total[nodes:])
    result = jnp.concatenate([packed, drafted[...].astype(jnp.float32)], axis=0).astype(jnp.bfloat16)
    for target in range(count):
        out[target] = result


def residual_kernel(gathered, gain, inputs, out, rows, sem):
    fetch = pltpu.make_async_copy(inputs, rows, sem)
    fetch.start()
    count = gathered.shape[0]
    nodes = rows.shape[0] // 2
    squares = jnp.zeros((nodes, LANES), jnp.float32)
    for source in range(count):
        chunk = gathered[source].astype(jnp.float32)[:nodes]
        squares = squares + chunk * chunk
    inverse = packed_inverse(squares, count * HALF)
    fetch.wait()
    for head in range(count // 2):
        both = paired(
            gathered[spot_of(2 * head)].astype(jnp.float32)[:nodes] * inverse,
            gathered[spot_of(2 * head + 1)].astype(jnp.float32)[:nodes] * inverse,
        )
        columns = slice(head * HEAD_DIM, (head + 1) * HEAD_DIM)
        block = jnp.concatenate(both, axis=0) * gain[:, columns]
        out[:, columns] = (rows[:, columns].astype(jnp.float32) + block).astype(jnp.bfloat16)


def down_kernel(hidden, weight, out, held):
    count, chunk_rows, _ = out.shape
    total_rows = hidden.shape[0]
    share = total_rows // count
    line = lax.broadcasted_iota(jnp.int32, (total_rows, total_rows), 0)
    column = lax.broadcasted_iota(jnp.int32, (total_rows, total_rows), 1)
    spot = line % count
    depth = count // SIDE
    owner = spot % depth * SIDE + spot // depth
    turn = (column == owner * share + line // count).astype(jnp.bfloat16)
    rows = jnp.dot(turn, hidden[...], preferred_element_type=jnp.float32).astype(jnp.bfloat16)
    for block in range(chunk_rows // share):
        sums = jnp.dot(
            rows,
            weight[:, block * LANES : (block + 1) * LANES],
            preferred_element_type=jnp.float32,
        )
        for row in range(share):
            held[pl.ds(block * share + row, count, stride=chunk_rows), :] = sums[
                row * count : (row + 1) * count
            ]
    for target in range(count):
        out[target] = held[target * chunk_rows : (target + 1) * chunk_rows].astype(jnp.bfloat16)


def last_kernel(shares, residual, gain, out):
    count, chunk_rows, _ = shares.shape
    share = out.shape[0]
    blocks = chunk_rows // share
    sums = jnp.zeros((chunk_rows, LANES), jnp.float32)
    for source in range(count):
        sums = sums + shares[source].astype(jnp.float32)
    parts = [sums[block * share : (block + 1) * share] for block in range(blocks)]
    squares = functools.reduce(jnp.add, [part * part for part in parts])
    square = jnp.sum(squares, axis=1, keepdims=True) / (blocks * LANES)
    inverse = lax.rsqrt(square + norm_epsilon)
    for block, part in enumerate(parts):
        columns = slice(block * LANES, (block + 1) * LANES)
        grown = residual[:, columns].astype(jnp.float32) + part * inverse * gain[:, columns]
        out[:, columns] = grown.astype(jnp.bfloat16)


def logits_kernel(early, late, vocab, out, table, drafted, sem):
    fetch = pltpu.make_async_copy(vocab, table, sem)
    fetch.start()
    count = early.shape[0]
    start = early.shape[1] - drafted.shape[0] // 4
    for head in range(count // 2):
        left = [part[spot_of(2 * head)].astype(jnp.float32)[start:] for part in (early, late)]
        right = [part[spot_of(2 * head + 1)].astype(jnp.float32)[start:] for part in (early, late)]
        both = paired(jnp.concatenate(left, axis=0), jnp.concatenate(right, axis=0))
        drafted[:, head * HEAD_DIM : (head + 1) * HEAD_DIM] = jnp.concatenate(both, axis=0).astype(
            jnp.bfloat16
        )
    fetch.wait()
    logits = lax.dot_general(
        drafted[...], table[...], (((1,), (1,)), ((), ())), preferred_element_type=jnp.float32
    )
    requests, drafts, _ = out.shape
    for request in range(requests):
        out[request] = logits[request * drafts : (request + 1) * drafts]


def rotated(front, back, cosine, sine):
    return front * cosine - back * sine, back * cosine + front * sine


def vmem(count):
    return [pl.BlockSpec(memory_space=pltpu.VMEM)] * count


SMEM = pl.BlockSpec(memory_space=pltpu.SMEM)


HBM = pl.BlockSpec(memory_space=pltpu.HBM)
MP = ("z", "x")
REQ = ("y", "c")
TURN = ("x", "z")


def limit(mib):
    return pltpu.CompilerParams(vmem_limit_bytes=mib * 2**20)


def exchange(chunks):
    return lax.all_to_all(chunks, TURN, 0, 0)


def per_device(
    draft_hidden,
    draft_weight,
    vocab_weight,
    tree_inputs,
    tree_parent,
    cache_len,
    page_table,
    kv_cache,
    accepted_node,
    qkv_weight,
    norm_gains,
    out_weight,
    gate_up_weight,
    down_weight,
):
    mp_count = lax.axis_size(MP)
    req_count = lax.axis_size(REQ)
    mp_place = lax.axis_index(MP)
    req_place = lax.axis_index(REQ)
    req_local, model_width = draft_hidden.shape
    draft_count = draft_weight.shape[0]
    slab = draft_weight.shape[2]
    vocab_local = vocab_weight.shape[0]
    rows = tree_inputs.shape[0]
    tree_size = tree_parent.shape[1]
    page_count, _, page_len, _ = kv_cache.shape
    table_width = page_table.shape[1]
    bf16 = jnp.bfloat16
    f32 = jnp.float32

    query_copies, own_key, own_value = pl.pallas_call(
        project_kernel,
        out_shape=(
            jax.ShapeDtypeStruct((mp_count, tree_size + 8, LANES), bf16),
            jax.ShapeDtypeStruct((tree_size, LANES), bf16),
            jax.ShapeDtypeStruct((tree_size, LANES), bf16),
        ),
        in_specs=[HBM, HBM],
        out_specs=tuple(vmem(3)),
        scratch_shapes=[
            pltpu.VMEM((rows, model_width), bf16),
            pltpu.VMEM((3, slab, model_width), bf16),
            pltpu.SemaphoreType.DMA((4,)),
        ],
        compiler_params=limit(8),
        name="project",
    )(tree_inputs, jnp.transpose(qkv_weight, (1, 2, 0)))
    gathered = exchange(query_copies)
    other_key = lax.ppermute(own_key, "x", [(i, i ^ 1) for i in range(SIDE)])

    pair = lax.ppermute(draft_hidden, "c", [(0, 1), (1, 0)])
    both = jnp.concatenate([draft_hidden, pair], axis=0)
    turns = req_count // 2
    hidden_parts = [both] + [
        lax.ppermute(both, "y", [(i, (i + k) % turns) for i in range(turns)])
        for k in range(1, turns)
    ]
    hidden_all = jnp.concatenate(hidden_parts, axis=0)
    spot = jnp.arange(req_count * req_local, dtype=jnp.int32)
    turn = spot // (2 * req_local)
    side = (spot // req_local) % 2
    holder = 2 * ((req_place // 2 - turn) % turns) + ((req_place % 2) ^ side)
    origin = holder * req_local + spot % req_local
    order = (origin[None, :] == spot[:, None]).astype(bf16)
    hidden_all = jnp.dot(order, hidden_all, preferred_element_type=f32).astype(bf16)
    draft_raw = jnp.einsum("rd,kde->rke", hidden_all, draft_weight, preferred_element_type=f32)
    own_columns = lax.dynamic_slice_in_dim(hidden_all, mp_place * slab, slab, 1).astype(f32)
    drafted = (own_columns[:, None, :] + jax.nn.silu(draft_raw)).astype(bf16)
    half_count = req_count * req_local * draft_count // 2
    drafted = drafted.reshape(2, half_count, slab)
    drafted = jnp.concatenate([drafted[0], drafted[1]], axis=1)

    ancestry, node_depth = tree_shape(tree_parent)
    positions = cache_len[:, None].astype(f32) + node_depth - 1.0
    freqs = rope_base ** (-jnp.arange(HALF, dtype=f32) * 2.0 / HEAD_DIM)
    angles = positions.T[:, :, None] * freqs[None, None, :]
    angles = angles.reshape(tree_size, LANES)
    cosine = jnp.cos(angles)
    sine = jnp.sin(angles)
    gain_rows = norm_gains.astype(f32)
    twice = gain_rows[:2].reshape(2, mp_count, slab)
    twice = jnp.concatenate([twice, twice], axis=2)

    slots = (req_place * mp_count + mp_place) * page_count + jnp.arange(page_count, dtype=jnp.int32)
    matches = page_table[None, :, :] == slots[:, None, None]
    starts = jnp.arange(table_width, dtype=jnp.int32) * page_len
    left = jnp.clip(cache_len[:, None] - starts[None, :], 0, page_len)
    counts = jnp.sum(jnp.where(matches, left[None], 0), axis=2).reshape(page_count * req_local, 1)
    counts = jnp.broadcast_to(counts, (page_count * req_local, LANES))

    groups = 4
    parts, queries, key_square = pl.pallas_call(
        pages_kernel,
        out_shape=(
            jax.ShapeDtypeStruct((mp_count, tree_size + 8, LANES), bf16),
            jax.ShapeDtypeStruct((HEADS, rows, HEAD_DIM), bf16),
            jax.ShapeDtypeStruct((8, LANES), f32),
        ),
        in_specs=[*vmem(5), HBM],
        out_specs=tuple(vmem(3)),
        scratch_shapes=[
            pltpu.VMEM(kv_cache.shape, bf16),
            pltpu.VMEM((mp_count, tree_size, LANES), f32),
            pltpu.SemaphoreType.DMA((groups,)),
        ],
        compiler_params=limit(60),
        cost_estimate=pl.CostEstimate(
            flops=4 * page_count * page_len * LANES * model_width,
            bytes_accessed=kv_cache.size * 2,
            transcendentals=page_count * page_len * tree_size * HEADS,
        ),
        name="pages",
    )(counts, gathered, twice[0], cosine, sine, kv_cache)
    arrived = exchange(parts)

    ride = half_count // 2
    first_ride, second_ride = drafted[:ride], drafted[ride:]
    path, tree, gate_up_copy = pl.pallas_call(
        tree_kernel,
        out_shape=(
            jax.ShapeDtypeStruct((2, 8, LANES), f32),
            jax.ShapeDtypeStruct((tree_size + 8 + ride, LANES), f32),
            jax.ShapeDtypeStruct(gate_up_weight.shape, bf16),
        ),
        in_specs=[SMEM, SMEM, *vmem(11), HBM],
        out_specs=(*vmem(2), HBM),
        scratch_shapes=[pltpu.SemaphoreType.DMA],
        compiler_params=limit(8),
        cost_estimate=pl.CostEstimate(flops=2**24, bytes_accessed=2**22, transcendentals=2**13),
        name="tree",
    )(
        mp_place.reshape(1),
        accepted_node,
        queries,
        own_key,
        other_key,
        own_value,
        key_square,
        twice[1],
        cosine,
        sine,
        ancestry,
        node_depth,
        first_ride,
        gate_up_weight,
    )
    accepted_kv = jnp.transpose(
        path[:, :draft_count].reshape(2, draft_count, req_local, slab), (2, 1, 0, 3)
    ).astype(bf16)

    out_twice = jnp.concatenate([out_weight.T, out_weight.T], axis=0)
    attended_copies = pl.pallas_call(
        merge_kernel,
        out_shape=jax.ShapeDtypeStruct((mp_count, tree_size + ride, LANES), bf16),
        in_specs=vmem(2),
        out_specs=vmem(1)[0],
        compiler_params=limit(8),
        name="merge",
    )(arrived, tree)
    out_gain = gain_rows[2:3]
    last_gain = gain_rows[3:4]
    attended_copies, out_twice, second_ride, accepted_kv, out_gain, last_gain = (
        lax.optimization_barrier(
            (attended_copies, out_twice, second_ride, accepted_kv, out_gain, last_gain)
        )
    )
    attended = exchange(attended_copies)
    out_copies = pl.pallas_call(
        out_kernel,
        out_shape=jax.ShapeDtypeStruct((mp_count, tree_size + ride, LANES), bf16),
        in_specs=vmem(3),
        out_specs=vmem(1)[0],
        compiler_params=limit(8),
        name="out_columns",
    )(attended, out_twice, second_ride)
    projected_out = exchange(out_copies)
    residual = pl.pallas_call(
        residual_kernel,
        out_shape=jax.ShapeDtypeStruct((rows, model_width), bf16),
        in_specs=[*vmem(2), HBM],
        out_specs=vmem(1)[0],
        scratch_shapes=[pltpu.VMEM((rows, model_width), bf16), pltpu.SemaphoreType.DMA],
        compiler_params=limit(8),
        name="residual",
    )(projected_out, out_gain, tree_inputs)
    gate_up = jnp.einsum("td,dce->tce", residual, gate_up_copy, preferred_element_type=f32)
    hidden = (jax.nn.silu(gate_up[:, 0]) * gate_up[:, 1]).astype(bf16)
    row_share = rows // mp_count
    chunk_rows = row_share * model_width // LANES
    partial = pl.pallas_call(
        down_kernel,
        out_shape=jax.ShapeDtypeStruct((mp_count, chunk_rows, LANES), bf16),
        in_specs=vmem(2),
        out_specs=vmem(1)[0],
        scratch_shapes=[pltpu.VMEM((mp_count * chunk_rows, LANES), f32)],
        compiler_params=limit(8),
        name="down",
    )(hidden, down_weight)
    shares = exchange(partial)

    draft_logits = pl.pallas_call(
        logits_kernel,
        out_shape=jax.ShapeDtypeStruct((req_count * req_local, draft_count, vocab_local), f32),
        in_specs=[*vmem(2), HBM],
        out_specs=vmem(1)[0],
        scratch_shapes=[
            pltpu.VMEM(vocab_weight.shape, bf16),
            pltpu.VMEM((req_count * req_local * draft_count, model_width), bf16),
            pltpu.SemaphoreType.DMA,
        ],
        compiler_params=limit(12),
        cost_estimate=pl.CostEstimate(flops=2**27, bytes_accessed=2**21, transcendentals=0),
        name="logits",
    )(attended, projected_out, vocab_weight)
    residual_rows = lax.dynamic_slice_in_dim(residual, mp_place * row_share, row_share, 0)
    layer_out = pl.pallas_call(
        last_kernel,
        out_shape=jax.ShapeDtypeStruct((row_share, model_width), bf16),
        in_specs=vmem(3),
        out_specs=vmem(1)[0],
        compiler_params=limit(8),
        name="last",
    )(shares, residual_rows, last_gain)
    return (draft_logits, layer_out, accepted_kv)


def solution(mesh):
    chips = mesh.devices.reshape(-1, 2, mesh.devices.shape[1] // SIDE, SIDE)
    mesh = jax.sharding.Mesh(chips, (*REQ, *MP))
    both = (*REQ, *MP)
    placed = (
        P(REQ, None),
        P(None, None, MP),
        P(both, None),
        P(REQ, None),
        P(REQ, None),
        P(REQ),
        P(REQ, None),
        P(both, None, None, None),
        P(REQ),
        P(None, None, MP),
        P(),
        P(None, MP),
        P(None, None, MP),
        P(MP, None),
    )
    return jax.shard_map(
        per_device,
        mesh=mesh,
        in_specs=placed,
        out_specs=(P(None, None, both), P(both, None), P(REQ, None, None, MP)),
        check_vma=False,
    )
```

```python
import functools

import jax
import jax.numpy as jnp
from jax import lax
from jax.experimental import pallas as pl
from jax.experimental.pallas import tpu as pltpu
from jax.sharding import PartitionSpec as P

HEADS = 16
HEAD_DIM = 128
HALF = HEAD_DIM // 2
LANES = 128
SIDE = 4

rope_base = 500000.0
norm_epsilon = 1e-06
masked_score = -1e30


def tree_shape(parents):
    node_count = parents.shape[-1]
    step_one = (
        parents[..., :, None] == jnp.arange(node_count, dtype=jnp.int32)[None, None, :]
    ).astype(jnp.float32)
    step_two = jnp.einsum("rij,rjk->rik", step_one, step_one, precision=lax.Precision.HIGHEST)
    step_three = jnp.einsum("rij,rjk->rik", step_two, step_one, precision=lax.Precision.HIGHEST)
    ancestry = jnp.eye(node_count, dtype=jnp.float32)[None] + step_one + step_two + step_three
    return (ancestry, jnp.sum(ancestry, axis=-1))


def split_three(value):
    top = value.astype(jnp.bfloat16).astype(jnp.float32)
    rest = value - top
    middle = rest.astype(jnp.bfloat16).astype(jnp.float32)
    return top, middle, (rest - middle).astype(jnp.bfloat16).astype(jnp.float32)


def in_first(rows):
    return lax.broadcasted_iota(jnp.int32, (rows, LANES), 1) < HALF


def paired(left, right):
    first = in_first(left.shape[0])
    return (
        jnp.where(first, left, pltpu.roll(right, HALF, 1)),
        jnp.where(first, pltpu.roll(left, HALF, 1), right),
    )


def packed_inverse(squares, width):
    first = in_first(squares.shape[0])
    zero = jnp.zeros_like(squares)
    left = jnp.sum(jnp.where(first, squares, zero), axis=1, keepdims=True)
    right = jnp.sum(jnp.where(first, zero, squares), axis=1, keepdims=True)
    return lax.rsqrt(jnp.where(first, left, right) / width + norm_epsilon)


def spot_of(place):
    return place % SIDE * (2 * HEADS // SIDE) + place // SIDE


def columns_to_rows(columns):
    rest = LANES - columns.shape[0]
    return jnp.concatenate([columns, jnp.zeros((rest, LANES), jnp.float32)], axis=0).T


def project_kernel(
    place, hidden, inputs, weights, draft_weights, copies, own_key, own_value, rows, columns, heads, sems
):
    nodes = own_key.shape[0]
    fetches = [pltpu.make_async_copy(inputs, rows, sems.at[0])]
    for kind in range(3):
        fetches.append(pltpu.make_async_copy(weights.at[kind], columns.at[kind], sems.at[1 + kind]))
    fetches.append(pltpu.make_async_copy(draft_weights, heads, sems.at[4]))
    for fetch in fetches:
        fetch.start()
    fetches[0].wait()
    first = in_first(nodes)

    def projected(kind):
        fetches[1 + kind].wait()
        weight = columns[kind]
        product = lax.dot_general(
            rows[...],
            jnp.concatenate([weight, weight], axis=0),
            (((1,), (1,)), ((), ())),
            preferred_element_type=jnp.float32,
        )
        return jnp.where(first, product[:nodes], product[nodes:]).astype(jnp.bfloat16)

    query = projected(0)
    key = projected(1)
    own_key[...] = key
    squares = key.astype(jnp.float32)
    squares = squares * squares
    zero = jnp.zeros_like(squares)
    lane = lax.broadcasted_iota(jnp.int32, (nodes, LANES), 1)
    left = jnp.sum(jnp.where(first, squares, zero), axis=1, keepdims=True)
    right = jnp.sum(jnp.where(first, zero, squares), axis=1, keepdims=True)
    turned = columns_to_rows(jnp.where(lane == 0, left, jnp.where(lane == 1, right, zero)))
    sums = jnp.where(in_first(1), turned[0:1], pltpu.roll(turned[1:2], HALF, 1))
    fetches[4].wait()
    states = hidden[...]
    start = pl.multiple_of(place[0] // 2 * LANES, LANES)
    own = hidden[:, pl.ds(start, LANES)].astype(jnp.float32)
    swapped = pltpu.roll(own, HALF, 1)
    here = jnp.full(own.shape, place[0] % 2, jnp.int32) == lax.broadcasted_iota(jnp.int32, own.shape, 1) // HALF
    own = jnp.where(here, own, swapped)
    pairs = []
    for pair in range(heads.shape[0] // LANES):
        raw = lax.dot_general(
            states,
            heads[pair * LANES : (pair + 1) * LANES],
            (((1,), (1,)), ((), ())),
            preferred_element_type=jnp.float32,
        )
        pairs.append(own + raw / (1.0 + jnp.exp(-raw)))
    drafted = [part[r : r + 1] for r in range(states.shape[0]) for part in pairs]
    tail = jnp.concatenate([*split_three(sums), *drafted, jnp.zeros_like(sums)], axis=0)
    chunk = jnp.concatenate([query.astype(jnp.float32), tail], axis=0).astype(jnp.bfloat16)
    for target in range(copies.shape[0]):
        copies[target] = chunk
    own_value[...] = projected(2)


def pages_kernel(
    counts, gathered, gains, cosine, sine, cache, out, queries, key_square, drafts, kv, held, sems
):
    pages, _, page_len, width = cache.shape
    nodes = cosine.shape[0]
    groups = sems.shape[0]
    group_width = width // groups

    def fetch(group):
        columns = pl.ds(group * group_width, group_width)
        return pltpu.make_async_copy(
            cache.at[:, :, :, columns], kv.at[:, :, :, columns], sems.at[group]
        )

    for group in range(groups):
        fetch(group).start()
    squares = jnp.zeros((nodes, LANES), jnp.float32)
    extra = jnp.zeros((8, LANES), jnp.float32)
    for source in range(2 * HEADS):
        chunk = gathered[source].astype(jnp.float32)
        squares = squares + chunk[:nodes] * chunk[:nodes]
        extra = extra + chunk[nodes : nodes + 8]
    inverse = packed_inverse(squares, width)
    key_square[...] = extra
    for head in range(HEADS):
        tails = [gathered[spot_of(2 * head + side)].astype(jnp.float32)[nodes:] for side in range(2)]
        even, odd = paired(*tails)
        lines = [part[row : row + 1] for row in range(3, 7) for part in (even, odd)]
        drafts[:, head * HEAD_DIM : (head + 1) * HEAD_DIM] = jnp.concatenate(lines, axis=0).astype(
            jnp.bfloat16
        )
    token = lax.broadcasted_iota(jnp.int32, (nodes, page_len), 1)
    bias = []
    for page in range(pages):
        halves = [
            jnp.where(token < counts[2 * page + request : 2 * page + request + 1], 0.0, masked_score)
            for request in range(2)
        ]
        bias.append(jnp.concatenate(halves, axis=0))
    scale = HEAD_DIM ** (-0.5)
    cos_rows = cosine[...]
    sin_rows = sine[...]
    lane = lax.broadcasted_iota(jnp.int32, (2 * nodes, LANES), 1)
    stats = jnp.zeros((2 * nodes, LANES), jnp.float32)
    for head in range(HEADS):
        if head % (HEADS // groups) == 0:
            fetch(head // (HEADS // groups)).wait()
        base = head * HEAD_DIM
        front = gathered[spot_of(2 * head)][:nodes].astype(jnp.float32)
        back = gathered[spot_of(2 * head + 1)][:nodes].astype(jnp.float32)
        front = front * inverse * gains[2 * head : 2 * head + 1]
        back = back * inverse * gains[2 * head + 1 : 2 * head + 2]
        front, back = rotated(front, back, cos_rows, sin_rows)
        query = jnp.concatenate(paired(front, back), axis=0).astype(jnp.bfloat16)
        queries[head] = query
        keys = kv[:, 0, :, base : base + HEAD_DIM].reshape(pages * page_len, HEAD_DIM)
        scores = lax.dot_general(
            query, keys, (((1,), (1,)), ((), ())), preferred_element_type=jnp.float32
        )
        scores = [
            scores[:, page * page_len : (page + 1) * page_len] * scale + bias[page]
            for page in range(pages)
        ]
        top = jnp.max(functools.reduce(jnp.maximum, scores), axis=1, keepdims=True)
        weights = [jnp.exp(score - top) for score in scores]
        total = jnp.sum(functools.reduce(jnp.add, weights), axis=1, keepdims=True)
        values = kv[:, 1, :, base : base + HEAD_DIM].reshape(pages * page_len, HEAD_DIM)
        mixed = jnp.dot(
            jnp.concatenate(weights, axis=1).astype(jnp.bfloat16),
            values,
            preferred_element_type=jnp.float32,
        )
        stats = jnp.where(lane == head, top, stats)
        stats = jnp.where(lane == HEADS + head, total, stats)
        left, right = paired(mixed[:nodes], mixed[nodes:])
        held[2 * head] = left
        held[2 * head + 1] = right
    turned = columns_to_rows(stats)
    shifted = pltpu.roll(turned, HALF - nodes, 1)
    turned = jnp.where(in_first(LANES), turned, shifted)
    rows = [*split_three(turned[:HEADS]), *split_three(turned[HEADS : 2 * HEADS])]
    rows += [jnp.zeros_like(rows[0])] * 2
    for head in range(HEADS):
        tail = jnp.concatenate([row[head : head + 1] for row in rows], axis=0)
        for half in range(2):
            block = jnp.concatenate([held[2 * head + half], tail], axis=0)
            out[spot_of(2 * head + half)] = block.astype(jnp.bfloat16)


def tree_kernel(
    place,
    accepted,
    queries,
    own_key,
    other_key,
    own_value,
    key_square,
    gains,
    cosine,
    sine,
    ancestry,
    depth,
    large,
    path_out,
    tree_out,
    large_out,
    sem,
):
    copy = pltpu.make_async_copy(large, large_out, sem)
    copy.start()
    width = 2 * HEADS * HALF
    requests, nodes, _ = ancestry.shape
    head = place[0] // 2
    even = jnp.full((nodes, LANES), place[0] % 2, jnp.int32) == 0
    first = in_first(nodes)
    sums = (key_square[0:1] + key_square[1:2]) + key_square[2:3]
    square = jnp.broadcast_to(sums, (LANES, LANES)).T
    square = jnp.where(first, square[:nodes], square[HALF : HALF + nodes])
    inverse = lax.rsqrt(square / width + norm_epsilon)
    own = own_key[...].astype(jnp.float32)
    other = other_key[...].astype(jnp.float32)
    front = jnp.where(even, own, other) * inverse * gains[pl.ds(2 * head, 1)]
    back = jnp.where(even, other, own) * inverse * gains[pl.ds(2 * head + 1, 1)]
    front, back = rotated(front, back, cosine[...], sine[...])
    kept = jnp.where(even, front, back).astype(jnp.bfloat16)
    keys = paired(front, back)
    value = own_value[...]
    query = queries[head]
    lane = lax.broadcasted_iota(jnp.int32, (nodes, LANES), 1)
    stats = jnp.zeros((nodes, LANES), jnp.float32)
    mixed = []
    pickers = []
    for request in range(requests):
        line = ancestry[request]
        scores = lax.dot_general(
            query[request * nodes : (request + 1) * nodes],
            keys[request].astype(jnp.bfloat16),
            (((1,), (1,)), ((), ())),
            preferred_element_type=jnp.float32,
        ) * (HEAD_DIM ** (-0.5))
        visible = line > 0.5
        scores = jnp.where(visible, scores, masked_score)
        top = jnp.max(scores, axis=1, keepdims=True)
        weights = jnp.where(visible, jnp.exp(scores - top), 0.0)
        total = jnp.sum(weights, axis=1, keepdims=True)
        mixed.append(jnp.dot(weights.astype(jnp.bfloat16), value, preferred_element_type=jnp.float32))
        stats = jnp.where(lane == request, top, stats)
        stats = jnp.where(lane == request + 2, total, stats)
        on_path = ancestry[request, pl.ds(accepted[request], 1), :]
        levels = depth[pl.ds(request, 1), :]
        wanted = (lax.broadcasted_iota(jnp.int32, (8, nodes), 0) + 1).astype(jnp.float32)
        picker = jnp.where(wanted == levels, on_path, 0.0).astype(jnp.bfloat16)
        pickers.append(picker)
    turned = columns_to_rows(stats)
    row = in_first(1)
    tail = [
        jnp.where(row, turned[0:1], pltpu.roll(turned[1:2], HALF, 1)),
        jnp.where(row, turned[2:3], pltpu.roll(turned[3:4], HALF, 1)),
        jnp.zeros((6, LANES), jnp.float32),
    ]
    tree_out[...] = jnp.concatenate(
        [jnp.where(first, mixed[0], mixed[1]), *tail], axis=0
    )
    for kind, block in enumerate((kept, value)):
        picked = [
            jnp.dot(picker, block, preferred_element_type=jnp.float32) for picker in pickers
        ]
        path_out[kind] = jnp.where(in_first(8), picked[0], picked[1])
    copy.wait()


def merge_kernel(parts, tree, out):
    count = parts.shape[0]
    nodes = parts.shape[1] - 8
    top_tree = tree[nodes : nodes + 1]
    tops = []
    totals = []
    for source in range(count):
        tail = parts[source].astype(jnp.float32)[nodes : nodes + 8]
        tops.append((tail[0:1] + tail[1:2]) + tail[2:3])
        totals.append((tail[3:4] + tail[4:5]) + tail[5:6])
    tops = jnp.concatenate(tops, axis=0)
    totals = jnp.concatenate(totals, axis=0)
    top = jnp.maximum(jnp.max(tops, axis=0, keepdims=True), top_tree)
    factors = jnp.exp(tops - top)
    factor_tree = jnp.exp(top_tree - top)
    total = jnp.sum(factors * totals, axis=0, keepdims=True) + factor_tree * tree[nodes + 1 : nodes + 2]
    shares = jnp.concatenate([factors / total, factor_tree / total], axis=0)
    turned = columns_to_rows(shares)
    first = in_first(nodes)

    def spread(source):
        return jnp.where(
            first,
            turned[0:nodes, source : source + 1],
            turned[HALF : HALF + nodes, source : source + 1],
        )

    mixed = spread(count) * tree[:nodes]
    for source in range(count):
        mixed = mixed + spread(source) * parts[source].astype(jnp.float32)[:nodes]
    result = mixed.astype(jnp.bfloat16)
    for target in range(count):
        out[target] = result


def out_kernel(gathered, weight, out):
    count = gathered.shape[0]
    nodes = gathered.shape[1]
    total = jnp.zeros((2 * nodes, LANES), jnp.float32)
    for head in range(count // 2):
        both = paired(
            gathered[spot_of(2 * head)][:nodes].astype(jnp.float32),
            gathered[spot_of(2 * head + 1)][:nodes].astype(jnp.float32),
        )
        block = jnp.concatenate(both, axis=0).astype(jnp.bfloat16)
        total = total + lax.dot_general(
            block,
            weight[:, head * HEAD_DIM : (head + 1) * HEAD_DIM],
            (((1,), (1,)), ((), ())),
            preferred_element_type=jnp.float32,
        )
    result = jnp.where(in_first(nodes), total[:nodes], total[nodes:]).astype(jnp.bfloat16)
    for target in range(count):
        out[target] = result


def residual_kernel(gathered, gain, inputs, out, rows, sem):
    fetch = pltpu.make_async_copy(inputs, rows, sem)
    fetch.start()
    count = gathered.shape[0]
    nodes = rows.shape[0] // 2
    squares = jnp.zeros((nodes, LANES), jnp.float32)
    for source in range(count):
        chunk = gathered[source].astype(jnp.float32)[:nodes]
        squares = squares + chunk * chunk
    inverse = packed_inverse(squares, count * HALF)
    fetch.wait()
    for head in range(count // 2):
        both = paired(
            gathered[spot_of(2 * head)].astype(jnp.float32)[:nodes] * inverse,
            gathered[spot_of(2 * head + 1)].astype(jnp.float32)[:nodes] * inverse,
        )
        columns = slice(head * HEAD_DIM, (head + 1) * HEAD_DIM)
        block = jnp.concatenate(both, axis=0) * gain[:, columns]
        out[:, columns] = (rows[:, columns].astype(jnp.float32) + block).astype(jnp.bfloat16)


def down_kernel(hidden, weight, out, held):
    count, chunk_rows, _ = out.shape
    total_rows = hidden.shape[0]
    share = total_rows // count
    line = lax.broadcasted_iota(jnp.int32, (total_rows, total_rows), 0)
    column = lax.broadcasted_iota(jnp.int32, (total_rows, total_rows), 1)
    spot = line % count
    depth = count // SIDE
    owner = spot % depth * SIDE + spot // depth
    turn = (column == owner * share + line // count).astype(jnp.bfloat16)
    rows = jnp.dot(turn, hidden[...], preferred_element_type=jnp.float32).astype(jnp.bfloat16)
    for block in range(chunk_rows // share):
        sums = jnp.dot(
            rows,
            weight[:, block * LANES : (block + 1) * LANES],
            preferred_element_type=jnp.float32,
        )
        for row in range(share):
            held[pl.ds(block * share + row, count, stride=chunk_rows), :] = sums[
                row * count : (row + 1) * count
            ]
    for target in range(count):
        out[target] = held[target * chunk_rows : (target + 1) * chunk_rows].astype(jnp.bfloat16)


def last_kernel(shares, residual, gain, out):
    count, chunk_rows, _ = shares.shape
    share = out.shape[0]
    blocks = chunk_rows // share
    sums = jnp.zeros((chunk_rows, LANES), jnp.float32)
    for source in range(count):
        sums = sums + shares[source].astype(jnp.float32)
    parts = [sums[block * share : (block + 1) * share] for block in range(blocks)]
    squares = functools.reduce(jnp.add, [part * part for part in parts])
    square = jnp.sum(squares, axis=1, keepdims=True) / (blocks * LANES)
    inverse = lax.rsqrt(square + norm_epsilon)
    for block, part in enumerate(parts):
        columns = slice(block * LANES, (block + 1) * LANES)
        grown = residual[:, columns].astype(jnp.float32) + part * inverse * gain[:, columns]
        out[:, columns] = grown.astype(jnp.bfloat16)


def logits_kernel(origins, drafts, vocab, out, table, sem):
    fetch = pltpu.make_async_copy(vocab, table, sem)
    fetch.start()
    requests, levels, _ = out.shape
    vectors = drafts[...]
    fetch.wait()
    logits = lax.dot_general(
        vectors, table[...], (((1,), (1,)), ((), ())), preferred_element_type=jnp.float32
    )
    for spot in range(requests):
        out[pl.ds(origins[spot], 1)] = logits[spot * levels : (spot + 1) * levels][None]


def rotated(front, back, cosine, sine):
    return front * cosine - back * sine, back * cosine + front * sine


def vmem(count):
    return [pl.BlockSpec(memory_space=pltpu.VMEM)] * count


SMEM = pl.BlockSpec(memory_space=pltpu.SMEM)


HBM = pl.BlockSpec(memory_space=pltpu.HBM)
MP = ("z", "x")
REQ = ("y", "c")
TURN = ("x", "z")


def limit(mib):
    return pltpu.CompilerParams(vmem_limit_bytes=mib * 2**20)


def exchange(chunks):
    return lax.all_to_all(chunks, TURN, 0, 0)


def per_device(
    draft_hidden,
    draft_weight,
    vocab_weight,
    tree_inputs,
    tree_parent,
    cache_len,
    page_table,
    kv_cache,
    accepted_node,
    qkv_weight,
    norm_gains,
    out_weight,
    gate_up_weight,
    down_weight,
):
    mp_count = lax.axis_size(MP)
    req_count = lax.axis_size(REQ)
    mp_place = lax.axis_index(MP)
    req_place = lax.axis_index(REQ)
    req_local, model_width = draft_hidden.shape
    draft_count = draft_weight.shape[0]
    slab = draft_weight.shape[2]
    vocab_local = vocab_weight.shape[0]
    rows = tree_inputs.shape[0]
    tree_size = tree_parent.shape[1]
    page_count, _, page_len, _ = kv_cache.shape
    table_width = page_table.shape[1]
    bf16 = jnp.bfloat16
    f32 = jnp.float32

    query_copies, own_key, own_value = pl.pallas_call(
        project_kernel,
        out_shape=(
            jax.ShapeDtypeStruct((mp_count, tree_size + 8, LANES), bf16),
            jax.ShapeDtypeStruct((tree_size, LANES), bf16),
            jax.ShapeDtypeStruct((tree_size, LANES), bf16),
        ),
        in_specs=[SMEM, *vmem(1), HBM, HBM, HBM],
        out_specs=tuple(vmem(3)),
        scratch_shapes=[
            pltpu.VMEM((rows, model_width), bf16),
            pltpu.VMEM((3, slab, model_width), bf16),
            pltpu.VMEM((draft_count * slab, model_width), bf16),
            pltpu.SemaphoreType.DMA((5,)),
        ],
        compiler_params=limit(60),
        cost_estimate=pl.CostEstimate(flops=2**32, bytes_accessed=0, transcendentals=0),
        name="project",
    )(
        mp_place.reshape(1),
        draft_hidden,
        tree_inputs,
        jnp.transpose(qkv_weight, (1, 2, 0)),
        jnp.transpose(draft_weight, (0, 2, 1)).reshape(draft_count * slab, model_width),
    )
    gathered = exchange(query_copies)
    other_key = lax.ppermute(own_key, "x", [(i, i ^ 1) for i in range(SIDE)])

    ancestry, node_depth = tree_shape(tree_parent)
    positions = cache_len[:, None].astype(f32) + node_depth - 1.0
    freqs = rope_base ** (-jnp.arange(HALF, dtype=f32) * 2.0 / HEAD_DIM)
    angles = positions.T[:, :, None] * freqs[None, None, :]
    angles = angles.reshape(tree_size, LANES)
    cosine = jnp.cos(angles)
    sine = jnp.sin(angles)
    gain_rows = norm_gains.astype(f32)
    twice = gain_rows[:2].reshape(2, mp_count, slab)
    twice = jnp.concatenate([twice, twice], axis=2)

    slots = (req_place * mp_count + mp_place) * page_count + jnp.arange(page_count, dtype=jnp.int32)
    matches = page_table[None, :, :] == slots[:, None, None]
    starts = jnp.arange(table_width, dtype=jnp.int32) * page_len
    left = jnp.clip(cache_len[:, None] - starts[None, :], 0, page_len)
    counts = jnp.sum(jnp.where(matches, left[None], 0), axis=2).reshape(page_count * req_local, 1)

    groups = 4
    parts, queries, key_square, drafts = pl.pallas_call(
        pages_kernel,
        out_shape=(
            jax.ShapeDtypeStruct((mp_count, tree_size + 8, LANES), bf16),
            jax.ShapeDtypeStruct((HEADS, rows, HEAD_DIM), bf16),
            jax.ShapeDtypeStruct((8, LANES), f32),
            jax.ShapeDtypeStruct((req_local * draft_count, model_width), bf16),
        ),
        in_specs=[*vmem(5), HBM],
        out_specs=tuple(vmem(4)),
        scratch_shapes=[
            pltpu.VMEM(kv_cache.shape, bf16),
            pltpu.VMEM((mp_count, tree_size, LANES), f32),
            pltpu.SemaphoreType.DMA((groups,)),
        ],
        compiler_params=limit(52),
        cost_estimate=pl.CostEstimate(flops=2**33, bytes_accessed=0, transcendentals=0),
        name="pages",
    )(counts, gathered, twice[0], cosine, sine, kv_cache)
    arrived = exchange(parts)

    pair = lax.ppermute(drafts, "c", [(0, 1), (1, 0)])
    both = jnp.concatenate([drafts, pair], axis=0)
    turns = req_count // 2
    drafted = [both] + [
        lax.ppermute(both, "y", [(i, (i + k) % turns) for i in range(turns)])
        for k in range(1, turns)
    ]
    drafted = jnp.concatenate(drafted, axis=0)
    spot = jnp.arange(req_count * req_local, dtype=jnp.int32)
    turn = spot // (2 * req_local)
    side = (spot // req_local) % 2
    holder = 2 * ((req_place // 2 - turn) % turns) + ((req_place % 2) ^ side)
    origins = holder * req_local + spot % req_local

    path, tree, gate_up_copy = pl.pallas_call(
        tree_kernel,
        out_shape=(
            jax.ShapeDtypeStruct((2, 8, LANES), f32),
            jax.ShapeDtypeStruct((tree_size + 8, LANES), f32),
            jax.ShapeDtypeStruct(gate_up_weight.shape, bf16),
        ),
        in_specs=[SMEM, SMEM, *vmem(10), HBM],
        out_specs=(*vmem(2), HBM),
        scratch_shapes=[pltpu.SemaphoreType.DMA],
        compiler_params=limit(60),
        cost_estimate=pl.CostEstimate(flops=2**31, bytes_accessed=0, transcendentals=2**13),
        name="tree",
    )(
        mp_place.reshape(1),
        accepted_node,
        queries,
        own_key,
        other_key,
        own_value,
        key_square,
        twice[1],
        cosine,
        sine,
        ancestry,
        node_depth,
        gate_up_weight,
    )
    accepted_kv = jnp.transpose(
        path[:, :draft_count].reshape(2, draft_count, req_local, slab), (2, 1, 0, 3)
    ).astype(bf16)

    out_twice = jnp.concatenate([out_weight.T, out_weight.T], axis=0)
    attended_copies = pl.pallas_call(
        merge_kernel,
        out_shape=jax.ShapeDtypeStruct((mp_count, tree_size, LANES), bf16),
        in_specs=vmem(2),
        out_specs=vmem(1)[0],
        compiler_params=limit(8),
        name="merge",
    )(arrived, tree)
    out_gain = gain_rows[2:3]
    last_gain = gain_rows[3:4]
    attended_copies, out_twice, accepted_kv, out_gain, last_gain, drafted, origins = (
        lax.optimization_barrier(
            (attended_copies, out_twice, accepted_kv, out_gain, last_gain, drafted, origins)
        )
    )
    attended = exchange(attended_copies)
    out_copies = pl.pallas_call(
        out_kernel,
        out_shape=jax.ShapeDtypeStruct((mp_count, tree_size, LANES), bf16),
        in_specs=vmem(2),
        out_specs=vmem(1)[0],
        compiler_params=limit(8),
        name="out_columns",
    )(attended, out_twice)
    projected_out = exchange(out_copies)
    projected_out, drafted, origins = lax.optimization_barrier((projected_out, drafted, origins))
    residual = pl.pallas_call(
        residual_kernel,
        out_shape=jax.ShapeDtypeStruct((rows, model_width), bf16),
        in_specs=[*vmem(2), HBM],
        out_specs=vmem(1)[0],
        scratch_shapes=[pltpu.VMEM((rows, model_width), bf16), pltpu.SemaphoreType.DMA],
        compiler_params=limit(8),
        name="residual",
    )(projected_out, out_gain, tree_inputs)
    gate_up = jnp.einsum("td,dce->tce", residual, gate_up_copy, preferred_element_type=f32)
    hidden = (jax.nn.silu(gate_up[:, 0]) * gate_up[:, 1]).astype(bf16)
    row_share = rows // mp_count
    chunk_rows = row_share * model_width // LANES
    partial = pl.pallas_call(
        down_kernel,
        out_shape=jax.ShapeDtypeStruct((mp_count, chunk_rows, LANES), bf16),
        in_specs=vmem(2),
        out_specs=vmem(1)[0],
        scratch_shapes=[pltpu.VMEM((mp_count * chunk_rows, LANES), f32)],
        compiler_params=limit(8),
        name="down",
    )(hidden, down_weight)
    shares = exchange(partial)

    draft_logits = pl.pallas_call(
        logits_kernel,
        out_shape=jax.ShapeDtypeStruct((req_count * req_local, draft_count, vocab_local), f32),
        in_specs=[SMEM, *vmem(1), HBM],
        out_specs=vmem(1)[0],
        scratch_shapes=[pltpu.VMEM(vocab_weight.shape, bf16), pltpu.SemaphoreType.DMA],
        compiler_params=limit(60),
        cost_estimate=pl.CostEstimate(flops=2**31, bytes_accessed=0, transcendentals=0),
        name="logits",
    )(origins, drafted, vocab_weight)
    residual_rows = lax.dynamic_slice_in_dim(residual, mp_place * row_share, row_share, 0)
    layer_out = pl.pallas_call(
        last_kernel,
        out_shape=jax.ShapeDtypeStruct((row_share, model_width), bf16),
        in_specs=vmem(3),
        out_specs=vmem(1)[0],
        compiler_params=limit(8),
        name="last",
    )(shares, residual_rows, last_gain)
    return (draft_logits, layer_out, accepted_kv)


def solution(mesh):
    chips = mesh.devices.reshape(-1, 2, mesh.devices.shape[1] // SIDE, SIDE)
    mesh = jax.sharding.Mesh(chips, (*REQ, *MP))
    both = (*REQ, *MP)
    placed = (
        P(REQ, None),
        P(None, None, MP),
        P(both, None),
        P(REQ, None),
        P(REQ, None),
        P(REQ),
        P(REQ, None),
        P(both, None, None, None),
        P(REQ),
        P(None, None, MP),
        P(),
        P(None, MP),
        P(None, None, MP),
        P(MP, None),
    )
    return jax.shard_map(
        per_device,
        mesh=mesh,
        in_specs=placed,
        out_specs=(P(None, None, both), P(both, None), P(REQ, None, None, MP)),
        check_vma=False,
    )
```

```python
import functools

import jax
import jax.numpy as jnp
from jax import lax
from jax.experimental import pallas as pl
from jax.experimental.pallas import tpu as pltpu
from jax.sharding import PartitionSpec as P

HEADS = 16
HEAD_DIM = 128
HALF = HEAD_DIM // 2
LANES = 128
SIDE = 4

rope_base = 500000.0
norm_epsilon = 1e-06
masked_score = -1e30


def tree_shape(parents):
    node_count = parents.shape[-1]
    step_one = (
        parents[..., :, None] == jnp.arange(node_count, dtype=jnp.int32)[None, None, :]
    ).astype(jnp.float32)
    step_two = jnp.einsum("rij,rjk->rik", step_one, step_one, precision=lax.Precision.HIGHEST)
    step_three = jnp.einsum("rij,rjk->rik", step_two, step_one, precision=lax.Precision.HIGHEST)
    ancestry = jnp.eye(node_count, dtype=jnp.float32)[None] + step_one + step_two + step_three
    return (ancestry, jnp.sum(ancestry, axis=-1))


def split_three(value):
    top = value.astype(jnp.bfloat16).astype(jnp.float32)
    rest = value - top
    middle = rest.astype(jnp.bfloat16).astype(jnp.float32)
    return top, middle, (rest - middle).astype(jnp.bfloat16).astype(jnp.float32)


def in_first(rows):
    return lax.broadcasted_iota(jnp.int32, (rows, LANES), 1) < HALF


def paired(left, right):
    first = in_first(left.shape[0])
    return (
        jnp.where(first, left, pltpu.roll(right, HALF, 1)),
        jnp.where(first, pltpu.roll(left, HALF, 1), right),
    )


def packed_inverse(squares, width):
    first = in_first(squares.shape[0])
    zero = jnp.zeros_like(squares)
    left = jnp.sum(jnp.where(first, squares, zero), axis=1, keepdims=True)
    right = jnp.sum(jnp.where(first, zero, squares), axis=1, keepdims=True)
    return lax.rsqrt(jnp.where(first, left, right) / width + norm_epsilon)


def spot_of(place):
    return place % SIDE * (2 * HEADS // SIDE) + place // SIDE


def columns_to_rows(columns):
    rest = LANES - columns.shape[0]
    return jnp.concatenate([columns, jnp.zeros((rest, LANES), jnp.float32)], axis=0).T


def project_kernel(
    place, hidden, inputs, weights, draft_weights, copies, own_key, own_value, rows, columns, heads, sems
):
    nodes = own_key.shape[0]
    fetches = [pltpu.make_async_copy(inputs, rows, sems.at[0])]
    for place_of, kind in enumerate((0, 1, 2, 2)):
        block = columns.at[pl.ds(place_of * HALF, HALF)]
        fetches.append(pltpu.make_async_copy(weights.at[kind], block, sems.at[1 + place_of]))
    fetches.append(pltpu.make_async_copy(draft_weights, heads, sems.at[5]))
    for fetch in fetches:
        fetch.start()
    for fetch in fetches[:5]:
        fetch.wait()
    first = in_first(nodes)
    product = lax.dot_general(
        rows[...], columns[...], (((1,), (1,)), ((), ())), preferred_element_type=jnp.float32
    )
    query, key = paired(product[:nodes, :LANES], product[nodes:, :LANES])
    key = key.astype(jnp.bfloat16)
    query = query.astype(jnp.bfloat16)
    own_key[...] = key
    own_value[...] = jnp.where(first, product[:nodes, LANES:], product[nodes:, LANES:]).astype(
        jnp.bfloat16
    )
    squares = key.astype(jnp.float32)
    squares = squares * squares
    zero = jnp.zeros_like(squares)
    lane = lax.broadcasted_iota(jnp.int32, (nodes, LANES), 1)
    left = jnp.sum(jnp.where(first, squares, zero), axis=1, keepdims=True)
    right = jnp.sum(jnp.where(first, zero, squares), axis=1, keepdims=True)
    turned = columns_to_rows(jnp.where(lane == 0, left, jnp.where(lane == 1, right, zero)))
    sums = jnp.where(in_first(1), turned[0:1], pltpu.roll(turned[1:2], HALF, 1))
    fetches[5].wait()
    states = hidden[...]
    start = pl.multiple_of(place[0] // 2 * LANES, LANES)
    own = hidden[:, pl.ds(start, LANES)].astype(jnp.float32)
    swapped = pltpu.roll(own, HALF, 1)
    here = jnp.full(own.shape, place[0] % 2, jnp.int32) == lax.broadcasted_iota(jnp.int32, own.shape, 1) // HALF
    own = jnp.where(here, own, swapped)
    raw = lax.dot_general(
        states, heads[...], (((1,), (1,)), ((), ())), preferred_element_type=jnp.float32
    )
    raw = raw / (1.0 + jnp.exp(-raw))
    pairs = [own + raw[:, side * LANES : (side + 1) * LANES] for side in range(raw.shape[1] // LANES)]
    drafted = [part[r : r + 1] for r in range(states.shape[0]) for part in pairs]
    tail = jnp.concatenate([*split_three(sums), *drafted, jnp.zeros_like(sums)], axis=0)
    chunk = jnp.concatenate([query.astype(jnp.float32), tail], axis=0).astype(jnp.bfloat16)
    for target in range(copies.shape[0]):
        copies[target] = chunk


def pages_kernel(
    counts, gathered, gains, cosine, sine, cache, out, queries, key_square, drafts, kv, held, sems
):
    pages, _, page_len, width = cache.shape
    nodes = cosine.shape[0]
    groups = sems.shape[0]
    group_width = width // groups

    def fetch(group):
        columns = pl.ds(group * group_width, group_width)
        return pltpu.make_async_copy(
            cache.at[:, :, :, columns], kv.at[:, :, :, columns], sems.at[group]
        )

    for group in range(groups):
        fetch(group).start()
    squares = jnp.zeros((nodes, LANES), jnp.float32)
    extra = jnp.zeros((8, LANES), jnp.float32)
    for source in range(2 * HEADS):
        chunk = gathered[source].astype(jnp.float32)
        squares = squares + chunk[:nodes] * chunk[:nodes]
        extra = extra + chunk[nodes : nodes + 8]
    inverse = packed_inverse(squares, width)
    key_square[...] = extra
    for head in range(HEADS):
        tails = [gathered[spot_of(2 * head + side)].astype(jnp.float32)[nodes:] for side in range(2)]
        even, odd = paired(*tails)
        lines = [part[row : row + 1] for row in range(3, 7) for part in (even, odd)]
        drafts[:, head * HEAD_DIM : (head + 1) * HEAD_DIM] = jnp.concatenate(lines, axis=0).astype(
            jnp.bfloat16
        )
    token = lax.broadcasted_iota(jnp.int32, (nodes, page_len), 1)
    bias = []
    for page in range(pages):
        halves = [
            jnp.where(token < counts[2 * page + request : 2 * page + request + 1], 0.0, masked_score)
            for request in range(2)
        ]
        bias.append(jnp.concatenate(halves, axis=0))
    scale = HEAD_DIM ** (-0.5)
    cos_rows = cosine[...]
    sin_rows = sine[...]
    lane = lax.broadcasted_iota(jnp.int32, (2 * nodes, LANES), 1)
    stats = jnp.zeros((2 * nodes, LANES), jnp.float32)

    def scored(head):
        if head % (HEADS // groups) == 0:
            fetch(head // (HEADS // groups)).wait()
        front = gathered[spot_of(2 * head)][:nodes].astype(jnp.float32)
        back = gathered[spot_of(2 * head + 1)][:nodes].astype(jnp.float32)
        front = front * inverse * gains[2 * head : 2 * head + 1]
        back = back * inverse * gains[2 * head + 1 : 2 * head + 2]
        front, back = rotated(front, back, cos_rows, sin_rows)
        query = jnp.concatenate(paired(front, back), axis=0).astype(jnp.bfloat16)
        queries[head] = query
        keys = kv[:, 0, :, head * HEAD_DIM : (head + 1) * HEAD_DIM]
        return lax.dot_general(
            query,
            keys.reshape(pages * page_len, HEAD_DIM),
            (((1,), (1,)), ((), ())),
            preferred_element_type=jnp.float32,
        )

    ahead = 3
    waiting = [scored(head) for head in range(ahead)]
    for head in range(HEADS):
        scores = waiting.pop(0)
        if head + ahead < HEADS:
            waiting.append(scored(head + ahead))
        base = head * HEAD_DIM
        scores = [
            scores[:, page * page_len : (page + 1) * page_len] * scale + bias[page]
            for page in range(pages)
        ]
        top = jnp.max(functools.reduce(jnp.maximum, scores), axis=1, keepdims=True)
        weights = [jnp.exp(score - top) for score in scores]
        total = jnp.sum(functools.reduce(jnp.add, weights), axis=1, keepdims=True)
        values = kv[:, 1, :, base : base + HEAD_DIM].reshape(pages * page_len, HEAD_DIM)
        mixed = jnp.dot(
            jnp.concatenate(weights, axis=1).astype(jnp.bfloat16),
            values,
            preferred_element_type=jnp.float32,
        )
        stats = jnp.where(lane == head, top, stats)
        stats = jnp.where(lane == HEADS + head, total, stats)
        left, right = paired(mixed[:nodes], mixed[nodes:])
        held[2 * head] = left
        held[2 * head + 1] = right
    turned = columns_to_rows(stats)
    shifted = pltpu.roll(turned, HALF - nodes, 1)
    turned = jnp.where(in_first(LANES), turned, shifted)
    rows = [*split_three(turned[:HEADS]), *split_three(turned[HEADS : 2 * HEADS])]
    rows += [jnp.zeros_like(rows[0])] * 2
    for head in range(HEADS):
        tail = jnp.concatenate([row[head : head + 1] for row in rows], axis=0)
        for half in range(2):
            block = jnp.concatenate([held[2 * head + half], tail], axis=0)
            out[spot_of(2 * head + half)] = block.astype(jnp.bfloat16)


def tree_kernel(
    place,
    accepted,
    queries,
    own_key,
    other_key,
    own_value,
    key_square,
    gains,
    cosine,
    sine,
    ancestry,
    depth,
    large,
    path_out,
    tree_out,
    large_out,
    sem,
):
    copy = pltpu.make_async_copy(large, large_out, sem)
    copy.start()
    width = 2 * HEADS * HALF
    requests, nodes, _ = ancestry.shape
    head = place[0] // 2
    even = jnp.full((nodes, LANES), place[0] % 2, jnp.int32) == 0
    first = in_first(nodes)
    sums = (key_square[0:1] + key_square[1:2]) + key_square[2:3]
    square = jnp.broadcast_to(sums, (LANES, LANES)).T
    square = jnp.where(first, square[:nodes], square[HALF : HALF + nodes])
    inverse = lax.rsqrt(square / width + norm_epsilon)
    own = own_key[...].astype(jnp.float32)
    other = other_key[...].astype(jnp.float32)
    front = jnp.where(even, own, other) * inverse * gains[pl.ds(2 * head, 1)]
    back = jnp.where(even, other, own) * inverse * gains[pl.ds(2 * head + 1, 1)]
    front, back = rotated(front, back, cosine[...], sine[...])
    kept = jnp.where(even, front, back).astype(jnp.bfloat16)
    keys = paired(front, back)
    value = own_value[...]
    query = queries[head]
    lane = lax.broadcasted_iota(jnp.int32, (nodes, LANES), 1)
    stats = jnp.zeros((nodes, LANES), jnp.float32)
    mixed = []
    pickers = []
    for request in range(requests):
        line = ancestry[request]
        scores = lax.dot_general(
            query[request * nodes : (request + 1) * nodes],
            keys[request].astype(jnp.bfloat16),
            (((1,), (1,)), ((), ())),
            preferred_element_type=jnp.float32,
        ) * (HEAD_DIM ** (-0.5))
        visible = line > 0.5
        scores = jnp.where(visible, scores, masked_score)
        top = jnp.max(scores, axis=1, keepdims=True)
        weights = jnp.where(visible, jnp.exp(scores - top), 0.0)
        total = jnp.sum(weights, axis=1, keepdims=True)
        mixed.append(jnp.dot(weights.astype(jnp.bfloat16), value, preferred_element_type=jnp.float32))
        stats = jnp.where(lane == request, top, stats)
        stats = jnp.where(lane == request + 2, total, stats)
        on_path = ancestry[request, pl.ds(accepted[request], 1), :]
        levels = depth[pl.ds(request, 1), :]
        wanted = (lax.broadcasted_iota(jnp.int32, (8, nodes), 0) + 1).astype(jnp.float32)
        picker = jnp.where(wanted == levels, on_path, 0.0).astype(jnp.bfloat16)
        pickers.append(picker)
    turned = columns_to_rows(stats)
    row = in_first(1)
    tail = [
        jnp.where(row, turned[0:1], pltpu.roll(turned[1:2], HALF, 1)),
        jnp.where(row, turned[2:3], pltpu.roll(turned[3:4], HALF, 1)),
        jnp.zeros((6, LANES), jnp.float32),
    ]
    tree_out[...] = jnp.concatenate(
        [jnp.where(first, mixed[0], mixed[1]), *tail], axis=0
    )
    for kind, block in enumerate((kept, value)):
        picked = [
            jnp.dot(picker, block, preferred_element_type=jnp.float32) for picker in pickers
        ]
        path_out[kind] = jnp.where(in_first(8), picked[0], picked[1])
    copy.wait()


def merge_kernel(parts, tree_part, out, tree, sem):
    count = parts.shape[0]
    nodes = parts.shape[1] - 8
    fetch = pltpu.make_async_copy(tree_part, tree, sem)
    fetch.start()
    tops = []
    totals = []
    for source in range(count):
        tail = parts[source].astype(jnp.float32)[nodes : nodes + 8]
        tops.append((tail[0:1] + tail[1:2]) + tail[2:3])
        totals.append((tail[3:4] + tail[4:5]) + tail[5:6])
    tops = jnp.concatenate(tops, axis=0)
    totals = jnp.concatenate(totals, axis=0)
    fetch.wait()
    top_tree = tree[nodes : nodes + 1]
    top = jnp.maximum(jnp.max(tops, axis=0, keepdims=True), top_tree)
    factors = jnp.exp(tops - top)
    factor_tree = jnp.exp(top_tree - top)
    total = jnp.sum(factors * totals, axis=0, keepdims=True) + factor_tree * tree[nodes + 1 : nodes + 2]
    shares = jnp.concatenate([factors / total, factor_tree / total], axis=0)
    turned = columns_to_rows(shares)
    first = in_first(nodes)

    def spread(source):
        return jnp.where(
            first,
            turned[0:nodes, source : source + 1],
            turned[HALF : HALF + nodes, source : source + 1],
        )

    mixed = spread(count) * tree[:nodes]
    for source in range(count):
        mixed = mixed + spread(source) * parts[source].astype(jnp.float32)[:nodes]
    result = mixed.astype(jnp.bfloat16)
    for target in range(count):
        out[target] = result


def out_kernel(gathered, weight, out):
    count = gathered.shape[0]
    nodes = gathered.shape[1]
    total = jnp.zeros((2 * nodes, LANES), jnp.float32)
    for head in range(count // 2):
        both = paired(
            gathered[spot_of(2 * head)][:nodes].astype(jnp.float32),
            gathered[spot_of(2 * head + 1)][:nodes].astype(jnp.float32),
        )
        block = jnp.concatenate(both, axis=0).astype(jnp.bfloat16)
        total = total + lax.dot_general(
            block,
            weight[:, head * HEAD_DIM : (head + 1) * HEAD_DIM],
            (((1,), (1,)), ((), ())),
            preferred_element_type=jnp.float32,
        )
    result = jnp.where(in_first(nodes), total[:nodes], total[nodes:]).astype(jnp.bfloat16)
    for target in range(count):
        out[target] = result


def residual_kernel(gathered, gain, inputs, out, rows, sem):
    fetch = pltpu.make_async_copy(inputs, rows, sem)
    fetch.start()
    count = gathered.shape[0]
    nodes = rows.shape[0] // 2
    squares = jnp.zeros((nodes, LANES), jnp.float32)
    for source in range(count):
        chunk = gathered[source].astype(jnp.float32)[:nodes]
        squares = squares + chunk * chunk
    inverse = packed_inverse(squares, count * HALF)
    fetch.wait()
    for head in range(count // 2):
        both = paired(
            gathered[spot_of(2 * head)].astype(jnp.float32)[:nodes] * inverse,
            gathered[spot_of(2 * head + 1)].astype(jnp.float32)[:nodes] * inverse,
        )
        columns = slice(head * HEAD_DIM, (head + 1) * HEAD_DIM)
        block = jnp.concatenate(both, axis=0) * gain[:, columns]
        out[:, columns] = (rows[:, columns].astype(jnp.float32) + block).astype(jnp.bfloat16)


def down_kernel(hidden, weight, out, held):
    count, chunk_rows, _ = out.shape
    total_rows = hidden.shape[0]
    share = total_rows // count
    line = lax.broadcasted_iota(jnp.int32, (total_rows, total_rows), 0)
    column = lax.broadcasted_iota(jnp.int32, (total_rows, total_rows), 1)
    spot = line % count
    depth = count // SIDE
    owner = spot % depth * SIDE + spot // depth
    turn = (column == owner * share + line // count).astype(jnp.bfloat16)
    rows = jnp.dot(turn, hidden[...], preferred_element_type=jnp.float32).astype(jnp.bfloat16)
    for block in range(chunk_rows // share):
        sums = jnp.dot(
            rows,
            weight[:, block * LANES : (block + 1) * LANES],
            preferred_element_type=jnp.float32,
        )
        for row in range(share):
            held[pl.ds(block * share + row, count, stride=chunk_rows), :] = sums[
                row * count : (row + 1) * count
            ]
    for target in range(count):
        out[target] = held[target * chunk_rows : (target + 1) * chunk_rows].astype(jnp.bfloat16)


def last_kernel(shares, residual, gain, out):
    count, chunk_rows, _ = shares.shape
    share = out.shape[0]
    blocks = chunk_rows // share
    sums = jnp.zeros((chunk_rows, LANES), jnp.float32)
    for source in range(count):
        sums = sums + shares[source].astype(jnp.float32)
    parts = [sums[block * share : (block + 1) * share] for block in range(blocks)]
    squares = functools.reduce(jnp.add, [part * part for part in parts])
    square = jnp.sum(squares, axis=1, keepdims=True) / (blocks * LANES)
    inverse = lax.rsqrt(square + norm_epsilon)
    for block, part in enumerate(parts):
        columns = slice(block * LANES, (block + 1) * LANES)
        grown = residual[:, columns].astype(jnp.float32) + part * inverse * gain[:, columns]
        out[:, columns] = grown.astype(jnp.bfloat16)


def logits_kernel(origins, drafts, vocab, out, table, sem):
    fetch = pltpu.make_async_copy(vocab, table, sem)
    fetch.start()
    requests, levels, _ = out.shape
    vectors = drafts[...]
    fetch.wait()
    logits = lax.dot_general(
        vectors, table[...], (((1,), (1,)), ((), ())), preferred_element_type=jnp.float32
    )
    for spot in range(requests):
        out[pl.ds(origins[spot], 1)] = logits[spot * levels : (spot + 1) * levels][None]


def rotated(front, back, cosine, sine):
    return front * cosine - back * sine, back * cosine + front * sine


def vmem(count):
    return [pl.BlockSpec(memory_space=pltpu.VMEM)] * count


SMEM = pl.BlockSpec(memory_space=pltpu.SMEM)


HBM = pl.BlockSpec(memory_space=pltpu.HBM)
MP = ("z", "x")
REQ = ("y", "c")
TURN = ("x", "z")


def limit(mib):
    return pltpu.CompilerParams(vmem_limit_bytes=mib * 2**20)


def exchange(chunks):
    return lax.all_to_all(chunks, TURN, 0, 0)


def per_device(
    draft_hidden,
    draft_weight,
    vocab_weight,
    tree_inputs,
    tree_parent,
    cache_len,
    page_table,
    kv_cache,
    accepted_node,
    qkv_weight,
    norm_gains,
    out_weight,
    gate_up_weight,
    down_weight,
):
    mp_count = lax.axis_size(MP)
    req_count = lax.axis_size(REQ)
    mp_place = lax.axis_index(MP)
    req_place = lax.axis_index(REQ)
    req_local, model_width = draft_hidden.shape
    draft_count = draft_weight.shape[0]
    slab = draft_weight.shape[2]
    vocab_local = vocab_weight.shape[0]
    rows = tree_inputs.shape[0]
    tree_size = tree_parent.shape[1]
    page_count, _, page_len, _ = kv_cache.shape
    table_width = page_table.shape[1]
    bf16 = jnp.bfloat16
    f32 = jnp.float32

    query_copies, own_key, own_value = pl.pallas_call(
        project_kernel,
        out_shape=(
            jax.ShapeDtypeStruct((mp_count, tree_size + 8, LANES), bf16),
            jax.ShapeDtypeStruct((tree_size, LANES), bf16),
            jax.ShapeDtypeStruct((tree_size, LANES), bf16),
        ),
        in_specs=[SMEM, *vmem(1), HBM, HBM, HBM],
        out_specs=tuple(vmem(3)),
        scratch_shapes=[
            pltpu.VMEM((rows, model_width), bf16),
            pltpu.VMEM((4 * slab, model_width), bf16),
            pltpu.VMEM((draft_count * slab, model_width), bf16),
            pltpu.SemaphoreType.DMA((6,)),
        ],
        compiler_params=limit(60),
        cost_estimate=pl.CostEstimate(flops=2**32, bytes_accessed=0, transcendentals=0),
        name="project",
    )(
        mp_place.reshape(1),
        draft_hidden,
        tree_inputs,
        jnp.transpose(qkv_weight, (1, 2, 0)),
        jnp.transpose(draft_weight, (0, 2, 1)).reshape(draft_count * slab, model_width),
    )
    gathered = exchange(query_copies)
    other_key = lax.ppermute(own_key, "x", [(i, i ^ 1) for i in range(SIDE)])

    ancestry, node_depth = tree_shape(tree_parent)
    positions = cache_len[:, None].astype(f32) + node_depth - 1.0
    freqs = rope_base ** (-jnp.arange(HALF, dtype=f32) * 2.0 / HEAD_DIM)
    angles = positions.T[:, :, None] * freqs[None, None, :]
    angles = angles.reshape(tree_size, LANES)
    cosine = jnp.cos(angles)
    sine = jnp.sin(angles)
    gain_rows = norm_gains.astype(f32)
    twice = gain_rows[:2].reshape(2, mp_count, slab)
    twice = jnp.concatenate([twice, twice], axis=2)

    slots = (req_place * mp_count + mp_place) * page_count + jnp.arange(page_count, dtype=jnp.int32)
    matches = page_table[None, :, :] == slots[:, None, None]
    starts = jnp.arange(table_width, dtype=jnp.int32) * page_len
    left = jnp.clip(cache_len[:, None] - starts[None, :], 0, page_len)
    counts = jnp.sum(jnp.where(matches, left[None], 0), axis=2).reshape(page_count * req_local, 1)

    groups = 4
    parts, queries, key_square, drafts = pl.pallas_call(
        pages_kernel,
        out_shape=(
            jax.ShapeDtypeStruct((mp_count, tree_size + 8, LANES), bf16),
            jax.ShapeDtypeStruct((HEADS, rows, HEAD_DIM), bf16),
            jax.ShapeDtypeStruct((8, LANES), f32),
            jax.ShapeDtypeStruct((req_local * draft_count, model_width), bf16),
        ),
        in_specs=[*vmem(5), HBM],
        out_specs=tuple(vmem(4)),
        scratch_shapes=[
            pltpu.VMEM(kv_cache.shape, bf16),
            pltpu.VMEM((mp_count, tree_size, LANES), f32),
            pltpu.SemaphoreType.DMA((groups,)),
        ],
        compiler_params=limit(52),
        cost_estimate=pl.CostEstimate(flops=2**33, bytes_accessed=0, transcendentals=0),
        name="pages",
    )(counts, gathered, twice[0], cosine, sine, kv_cache)
    arrived = exchange(parts)

    path, tree, gate_up_copy = pl.pallas_call(
        tree_kernel,
        out_shape=(
            jax.ShapeDtypeStruct((2, 8, LANES), f32),
            jax.ShapeDtypeStruct((tree_size + 8, LANES), f32),
            jax.ShapeDtypeStruct(gate_up_weight.shape, bf16),
        ),
        in_specs=[SMEM, SMEM, *vmem(10), HBM],
        out_specs=tuple(vmem(3)),
        scratch_shapes=[pltpu.SemaphoreType.DMA],
        compiler_params=limit(52),
        cost_estimate=pl.CostEstimate(flops=2**31, bytes_accessed=0, transcendentals=2**13),
        name="tree",
    )(
        mp_place.reshape(1),
        accepted_node,
        queries,
        own_key,
        other_key,
        own_value,
        key_square,
        twice[1],
        cosine,
        sine,
        ancestry,
        node_depth,
        gate_up_weight,
    )
    pair = lax.ppermute(drafts, "c", [(0, 1), (1, 0)])
    both = jnp.concatenate([drafts, pair], axis=0)
    turns = req_count // 2
    drafted = [both] + [
        lax.ppermute(both, "y", [(i, (i + k) % turns) for i in range(turns)])
        for k in range(1, turns)
    ]
    drafted = jnp.concatenate(drafted, axis=0)
    spot = jnp.arange(req_count * req_local, dtype=jnp.int32)
    turn = spot // (2 * req_local)
    side = (spot // req_local) % 2
    holder = 2 * ((req_place // 2 - turn) % turns) + ((req_place % 2) ^ side)
    origins = holder * req_local + spot % req_local

    accepted_kv = jnp.transpose(
        path[:, :draft_count].reshape(2, draft_count, req_local, slab), (2, 1, 0, 3)
    ).astype(bf16)

    out_twice = jnp.concatenate([out_weight.T, out_weight.T], axis=0)
    attended_copies = pl.pallas_call(
        merge_kernel,
        out_shape=jax.ShapeDtypeStruct((mp_count, tree_size, LANES), bf16),
        in_specs=[*vmem(1), HBM],
        out_specs=vmem(1)[0],
        scratch_shapes=[pltpu.VMEM((tree_size + 8, LANES), f32), pltpu.SemaphoreType.DMA],
        compiler_params=limit(8),
        cost_estimate=pl.CostEstimate(flops=2**31, bytes_accessed=0, transcendentals=0),
        name="merge",
    )(arrived, tree)
    out_gain = gain_rows[2:3]
    last_gain = gain_rows[3:4]
    attended_copies, out_twice, accepted_kv, out_gain, last_gain, drafted, origins = (
        lax.optimization_barrier(
            (attended_copies, out_twice, accepted_kv, out_gain, last_gain, drafted, origins)
        )
    )
    attended = exchange(attended_copies)
    out_copies = pl.pallas_call(
        out_kernel,
        out_shape=jax.ShapeDtypeStruct((mp_count, tree_size, LANES), bf16),
        in_specs=vmem(2),
        out_specs=vmem(1)[0],
        compiler_params=limit(8),
        name="out_columns",
    )(attended, out_twice)
    projected_out = exchange(out_copies)
    projected_out, drafted, origins = lax.optimization_barrier((projected_out, drafted, origins))
    residual = pl.pallas_call(
        residual_kernel,
        out_shape=jax.ShapeDtypeStruct((rows, model_width), bf16),
        in_specs=[*vmem(2), HBM],
        out_specs=vmem(1)[0],
        scratch_shapes=[pltpu.VMEM((rows, model_width), bf16), pltpu.SemaphoreType.DMA],
        compiler_params=limit(8),
        name="residual",
    )(projected_out, out_gain, tree_inputs)
    gate_up = jnp.einsum("td,dce->tce", residual, gate_up_copy, preferred_element_type=f32)
    hidden = (jax.nn.silu(gate_up[:, 0]) * gate_up[:, 1]).astype(bf16)
    row_share = rows // mp_count
    chunk_rows = row_share * model_width // LANES
    partial = pl.pallas_call(
        down_kernel,
        out_shape=jax.ShapeDtypeStruct((mp_count, chunk_rows, LANES), bf16),
        in_specs=vmem(2),
        out_specs=vmem(1)[0],
        scratch_shapes=[pltpu.VMEM((mp_count * chunk_rows, LANES), f32)],
        compiler_params=limit(8),
        name="down",
    )(hidden, down_weight)
    shares = exchange(partial)

    draft_logits = pl.pallas_call(
        logits_kernel,
        out_shape=jax.ShapeDtypeStruct((req_count * req_local, draft_count, vocab_local), f32),
        in_specs=[SMEM, *vmem(1), HBM],
        out_specs=vmem(1)[0],
        scratch_shapes=[pltpu.VMEM(vocab_weight.shape, bf16), pltpu.SemaphoreType.DMA],
        compiler_params=limit(60),
        cost_estimate=pl.CostEstimate(flops=2**31, bytes_accessed=0, transcendentals=0),
        name="logits",
    )(origins, drafted, vocab_weight)
    residual_rows = lax.dynamic_slice_in_dim(residual, mp_place * row_share, row_share, 0)
    layer_out = pl.pallas_call(
        last_kernel,
        out_shape=jax.ShapeDtypeStruct((row_share, model_width), bf16),
        in_specs=vmem(3),
        out_specs=vmem(1)[0],
        compiler_params=limit(8),
        name="last",
    )(shares, residual_rows, last_gain)
    return (draft_logits, layer_out, accepted_kv)


def solution(mesh):
    chips = mesh.devices.reshape(-1, 2, mesh.devices.shape[1] // SIDE, SIDE)
    mesh = jax.sharding.Mesh(chips, (*REQ, *MP))
    both = (*REQ, *MP)
    placed = (
        P(REQ, None),
        P(None, None, MP),
        P(both, None),
        P(REQ, None),
        P(REQ, None),
        P(REQ),
        P(REQ, None),
        P(both, None, None, None),
        P(REQ),
        P(None, None, MP),
        P(),
        P(None, MP),
        P(None, None, MP),
        P(MP, None),
    )
    return jax.shard_map(
        per_device,
        mesh=mesh,
        in_specs=placed,
        out_specs=(P(None, None, both), P(both, None), P(REQ, None, None, MP)),
        check_vma=False,
    )
```

```python
import functools

import jax
import jax.numpy as jnp
from jax import lax
from jax.experimental import pallas as pl
from jax.experimental.pallas import tpu as pltpu
from jax.sharding import PartitionSpec as P

HEADS = 16
HEAD_DIM = 128
HALF = HEAD_DIM // 2
LANES = 128
SIDE = 4

rope_base = 500000.0
norm_epsilon = 1e-06
masked_score = -1e30


def tree_shape(parents):
    node_count = parents.shape[-1]
    step_one = (
        parents[..., :, None] == jnp.arange(node_count, dtype=jnp.int32)[None, None, :]
    ).astype(jnp.float32)
    step_two = jnp.einsum("rij,rjk->rik", step_one, step_one, precision=lax.Precision.HIGHEST)
    step_three = jnp.einsum("rij,rjk->rik", step_two, step_one, precision=lax.Precision.HIGHEST)
    ancestry = jnp.eye(node_count, dtype=jnp.float32)[None] + step_one + step_two + step_three
    return (ancestry, jnp.sum(ancestry, axis=-1))


def split_three(value):
    top = value.astype(jnp.bfloat16).astype(jnp.float32)
    rest = value - top
    middle = rest.astype(jnp.bfloat16).astype(jnp.float32)
    return top, middle, (rest - middle).astype(jnp.bfloat16).astype(jnp.float32)


def in_first(rows):
    return lax.broadcasted_iota(jnp.int32, (rows, LANES), 1) < HALF


def paired(left, right):
    first = in_first(left.shape[0])
    return (
        jnp.where(first, left, pltpu.roll(right, HALF, 1)),
        jnp.where(first, pltpu.roll(left, HALF, 1), right),
    )


def packed_inverse(squares, width):
    first = in_first(squares.shape[0])
    zero = jnp.zeros_like(squares)
    left = jnp.sum(jnp.where(first, squares, zero), axis=1, keepdims=True)
    right = jnp.sum(jnp.where(first, zero, squares), axis=1, keepdims=True)
    return lax.rsqrt(jnp.where(first, left, right) / width + norm_epsilon)


def spot_of(place):
    return place % SIDE * (2 * HEADS // SIDE) + place // SIDE


def columns_to_rows(columns):
    rest = LANES - columns.shape[0]
    return jnp.concatenate([columns, jnp.zeros((rest, LANES), jnp.float32)], axis=0).T


def project_kernel(
    place, hidden, inputs, weights, draft_weights, copies, own_key, own_value, rows, columns, heads, sems
):
    nodes = own_key.shape[0]
    fetches = [pltpu.make_async_copy(inputs, rows, sems.at[0])]
    for place_of, kind in enumerate((0, 1, 2, 2)):
        block = columns.at[pl.ds(place_of * HALF, HALF)]
        fetches.append(pltpu.make_async_copy(weights.at[kind], block, sems.at[1 + place_of]))
    fetches.append(pltpu.make_async_copy(draft_weights, heads, sems.at[5]))
    for fetch in fetches:
        fetch.start()
    for fetch in fetches[:5]:
        fetch.wait()
    first = in_first(nodes)
    product = lax.dot_general(
        columns[...], rows[...], (((1,), (1,)), ((), ())), preferred_element_type=jnp.float32
    ).T
    query, key = paired(product[:nodes, :LANES], product[nodes:, :LANES])
    key = key.astype(jnp.bfloat16)
    query = query.astype(jnp.bfloat16)
    own_key[...] = key
    own_value[...] = jnp.where(first, product[:nodes, LANES:], product[nodes:, LANES:]).astype(
        jnp.bfloat16
    )
    squares = key.astype(jnp.float32)
    squares = squares * squares
    zero = jnp.zeros_like(squares)
    lane = lax.broadcasted_iota(jnp.int32, (nodes, LANES), 1)
    left = jnp.sum(jnp.where(first, squares, zero), axis=1, keepdims=True)
    right = jnp.sum(jnp.where(first, zero, squares), axis=1, keepdims=True)
    turned = columns_to_rows(jnp.where(lane == 0, left, jnp.where(lane == 1, right, zero)))
    sums = jnp.where(in_first(1), turned[0:1], pltpu.roll(turned[1:2], HALF, 1))
    fetches[5].wait()
    states = hidden[...]
    start = pl.multiple_of(place[0] // 2 * LANES, LANES)
    own = hidden[:, pl.ds(start, LANES)].astype(jnp.float32)
    swapped = pltpu.roll(own, HALF, 1)
    here = jnp.full(own.shape, place[0] % 2, jnp.int32) == lax.broadcasted_iota(jnp.int32, own.shape, 1) // HALF
    own = jnp.where(here, own, swapped)
    raw = lax.dot_general(
        heads[...], states, (((1,), (1,)), ((), ())), preferred_element_type=jnp.float32
    ).T
    raw = raw / (1.0 + jnp.exp(-raw))
    pairs = [own + raw[:, side * LANES : (side + 1) * LANES] for side in range(raw.shape[1] // LANES)]
    drafted = [part[r : r + 1] for r in range(states.shape[0]) for part in pairs]
    tail = jnp.concatenate([*split_three(sums), *drafted, jnp.zeros_like(sums)], axis=0)
    chunk = jnp.concatenate([query.astype(jnp.float32), tail], axis=0).astype(jnp.bfloat16)
    for target in range(copies.shape[0]):
        copies[target] = chunk


def tree_part(place, query, own_key, other_key, own_value, sums, gains, cosine, sine, ancestry):
    requests, nodes, _ = ancestry.shape
    width = 2 * HEADS * HALF
    head = place[0] // 2
    parity = jnp.full((nodes, LANES), place[0] % 2, jnp.int32)
    even = parity == 0
    side = lax.broadcasted_iota(jnp.int32, (nodes, LANES), 1) // HALF
    first = in_first(nodes)
    square = jnp.broadcast_to(sums, (LANES, LANES)).T
    square = jnp.where(first, square[:nodes], square[HALF : HALF + nodes])
    inverse = lax.rsqrt(square / width + norm_epsilon)
    own = own_key[...].astype(jnp.float32)
    other = other_key[...].astype(jnp.float32)
    front = jnp.where(even, own, other) * inverse * gains[pl.ds(2 * head, 1)]
    back = jnp.where(even, other, own) * inverse * gains[pl.ds(2 * head + 1, 1)]
    front, back = rotated(front, back, cosine[...], sine[...])
    kept = jnp.where(even, front, back).astype(jnp.bfloat16)
    keys = paired(front, back)
    value = own_value[...]
    tops, totals, mixed = [], [], []
    for request in range(requests):
        scores = lax.dot_general(
            query[request * nodes : (request + 1) * nodes],
            keys[request].astype(jnp.bfloat16),
            (((1,), (1,)), ((), ())),
            preferred_element_type=jnp.float32,
        ) * (HEAD_DIM ** (-0.5))
        visible = ancestry[request] > 0.5
        scores = jnp.where(visible, scores, masked_score)
        top = jnp.max(scores, axis=1, keepdims=True)
        weights = jnp.where(visible, jnp.exp(scores - top), 0.0)
        tops.append(top)
        totals.append(jnp.sum(weights, axis=1, keepdims=True))
        found = jnp.dot(weights.astype(jnp.bfloat16), value, preferred_element_type=jnp.float32)
        turned = pltpu.roll(found, HALF, 1)
        lined = jnp.where(parity == request, found, turned)
        mixed.append(jnp.where(side == parity, lined, 0.0))
    return (
        jnp.concatenate(tops, axis=0),
        jnp.concatenate(totals, axis=0),
        jnp.concatenate(mixed, axis=0),
        kept,
    )


def pages_kernel(
    place,
    counts,
    gathered,
    gains,
    key_gains,
    cosine,
    sine,
    own_key,
    other_key,
    own_value,
    ancestry,
    cache,
    out,
    drafts,
    kept_out,
    kv,
    held,
    queries,
    sems,
):
    pages, _, page_len, width = cache.shape
    nodes = cosine.shape[0]
    groups = sems.shape[0]
    group_width = width // groups

    def fetch(group):
        columns = pl.ds(group * group_width, group_width)
        return pltpu.make_async_copy(
            cache.at[:, :, :, columns], kv.at[:, :, :, columns], sems.at[group]
        )

    for group in range(groups):
        fetch(group).start()
    squares = jnp.zeros((nodes, LANES), jnp.float32)
    extra = jnp.zeros((8, LANES), jnp.float32)
    for source in range(2 * HEADS):
        chunk = gathered[source].astype(jnp.float32)
        squares = squares + chunk[:nodes] * chunk[:nodes]
        extra = extra + chunk[nodes : nodes + 8]
    inverse = packed_inverse(squares, width)
    sums = (extra[0:1] + extra[1:2]) + extra[2:3]
    for head in range(HEADS):
        tails = [gathered[spot_of(2 * head + side)].astype(jnp.float32)[nodes:] for side in range(2)]
        even, odd = paired(*tails)
        lines = [part[row : row + 1] for row in range(3, 7) for part in (even, odd)]
        drafts[:, head * HEAD_DIM : (head + 1) * HEAD_DIM] = jnp.concatenate(lines, axis=0).astype(
            jnp.bfloat16
        )
    token = lax.broadcasted_iota(jnp.int32, (nodes, page_len), 1)
    bias = []
    for page in range(pages):
        halves = [
            jnp.where(token < counts[2 * page + request : 2 * page + request + 1], 0.0, masked_score)
            for request in range(2)
        ]
        bias.append(jnp.concatenate(halves, axis=0))
    scale = HEAD_DIM ** (-0.5)
    cos_rows = cosine[...]
    sin_rows = sine[...]
    lane = lax.broadcasted_iota(jnp.int32, (2 * nodes, LANES), 1)
    stats = jnp.zeros((2 * nodes, LANES), jnp.float32)
    count = out.shape[0]
    share = 2 * nodes // count
    chunk_rows = share * HEADS

    def scored(head):
        if head % (HEADS // groups) == 0:
            fetch(head // (HEADS // groups)).wait()
        front = gathered[spot_of(2 * head)][:nodes].astype(jnp.float32)
        back = gathered[spot_of(2 * head + 1)][:nodes].astype(jnp.float32)
        front = front * inverse * gains[2 * head : 2 * head + 1]
        back = back * inverse * gains[2 * head + 1 : 2 * head + 2]
        front, back = rotated(front, back, cos_rows, sin_rows)
        query = jnp.concatenate(paired(front, back), axis=0).astype(jnp.bfloat16)
        queries[head] = query
        keys = kv[:, 0, :, head * HEAD_DIM : (head + 1) * HEAD_DIM]
        return lax.dot_general(
            query,
            keys.reshape(pages * page_len, HEAD_DIM),
            (((1,), (1,)), ((), ())),
            preferred_element_type=jnp.float32,
        )

    ahead = 3
    waiting = [scored(head) for head in range(ahead)]
    for head in range(HEADS):
        scores = waiting.pop(0)
        if head + ahead < HEADS:
            waiting.append(scored(head + ahead))
        base = head * HEAD_DIM
        scores = [
            scores[:, page * page_len : (page + 1) * page_len] * scale + bias[page]
            for page in range(pages)
        ]
        top = jnp.max(functools.reduce(jnp.maximum, scores), axis=1, keepdims=True)
        weights = [jnp.exp(score - top) for score in scores]
        total = jnp.sum(functools.reduce(jnp.add, weights), axis=1, keepdims=True)
        values = kv[:, 1, :, base : base + HEAD_DIM].reshape(pages * page_len, HEAD_DIM)
        mixed = jnp.dot(
            jnp.concatenate(weights, axis=1).astype(jnp.bfloat16),
            values,
            preferred_element_type=jnp.float32,
        )
        stats = jnp.where(lane == head, top, stats)
        stats = jnp.where(lane == HEADS + head, total, stats)
        for row in range(share):
            held[pl.ds(row * HEADS + head, count, stride=chunk_rows), :] = mixed[
                row * count : (row + 1) * count
            ]
    own_head = place[0] // 2
    tree_top, tree_total, tree_mixed, kept = tree_part(
        place, queries[own_head], own_key, other_key, own_value, sums, key_gains, cosine, sine, ancestry
    )
    kept_out[...] = kept
    is_top = lane == own_head
    is_total = lane == HEADS + own_head
    top = jnp.sum(jnp.where(is_top, stats, 0.0), axis=1, keepdims=True)
    total = jnp.sum(jnp.where(is_total, stats, 0.0), axis=1, keepdims=True)
    both_top = jnp.maximum(top, tree_top)
    page_factor = jnp.exp(top - both_top)
    tree_factor = jnp.exp(tree_top - both_top)
    adds = (1 - place[0] % 2).astype(jnp.float32)
    stats = jnp.where(is_top, both_top, stats)
    stats = jnp.where(is_total, total * page_factor + tree_total * tree_factor * adds, stats)
    tree_mixed = tree_mixed * tree_factor
    for row in range(share):
        spot = pl.ds(row * HEADS + own_head, count, stride=chunk_rows)
        lines = slice(row * count, (row + 1) * count)
        held[spot, :] = held[spot, :] * page_factor[lines] + tree_mixed[lines]
    spread = lax.broadcasted_iota(jnp.int32, (count, LANES), 1) // HEADS

    def by_device(kind):
        found = jnp.zeros((count, LANES), jnp.float32)
        for row in range(share):
            turned = pltpu.roll(
                stats[row * count : (row + 1) * count], (row - kind) * HEADS % LANES, 1
            )
            found = jnp.where(spread == row, turned, found)
        return found

    rows = [*split_three(by_device(0)), *split_three(by_device(1))]
    rows += [jnp.zeros_like(rows[0])] * 2
    for target in range(count):
        tail = jnp.concatenate([row[target : target + 1] for row in rows], axis=0)
        block = jnp.concatenate(
            [held[target * chunk_rows : (target + 1) * chunk_rows], tail], axis=0
        )
        out[target] = block.astype(jnp.bfloat16)


def path_kernel(accepted, kept, own_value, ancestry, depth, out):
    requests, nodes, _ = ancestry.shape
    pickers = []
    for request in range(requests):
        on_path = ancestry[request, pl.ds(accepted[request], 1), :]
        levels = depth[pl.ds(request, 1), :]
        wanted = (lax.broadcasted_iota(jnp.int32, (8, nodes), 0) + 1).astype(jnp.float32)
        pickers.append(jnp.where(wanted == levels, on_path, 0.0).astype(jnp.bfloat16))
    for kind, block in enumerate((kept[...], own_value[...])):
        picked = [
            jnp.dot(picker, block, preferred_element_type=jnp.float32) for picker in pickers
        ]
        out[kind] = jnp.where(in_first(8), picked[0], picked[1])


def order_kernel(side, own, *rest):
    *others, out = rest
    for turn, block in enumerate((own, *others)):
        out[pl.ds((side[0] + SIDE - turn) % SIDE, 1)] = block[...][None]


def held_kernel(large, out, sem):
    copy = pltpu.make_async_copy(large, out, sem)
    copy.start()
    copy.wait()


def merge_kernel(parts, out):
    count = parts.shape[0]
    rows = parts.shape[1] - 8
    tops = []
    totals = []
    for source in range(count):
        tail = parts[source].astype(jnp.float32)[rows:]
        tops.append((tail[0:1] + tail[1:2]) + tail[2:3])
        totals.append((tail[3:4] + tail[4:5]) + tail[5:6])
    tops = jnp.concatenate(tops, axis=0)
    totals = jnp.concatenate(totals, axis=0)
    factors = jnp.exp(tops - jnp.max(tops, axis=0, keepdims=True))
    shares = factors / jnp.sum(factors * totals, axis=0, keepdims=True)
    turned = columns_to_rows(shares)
    mixed = jnp.zeros((rows, LANES), jnp.float32)
    for source in range(count):
        mixed = mixed + turned[:rows, source : source + 1] * parts[source].astype(jnp.float32)[:rows]
    result = mixed.astype(jnp.bfloat16)
    for target in range(out.shape[0]):
        out[target] = result


def out_kernel(gathered, weight, out, wide, rows):
    depth, chunk_rows, _ = gathered.shape
    for source in range(depth):
        wide[source * chunk_rows : (source + 1) * chunk_rows] = gathered[source].astype(jnp.float32)
    for head in range(HEADS):
        lines = [
            wide[pl.ds(row * HEADS + head, depth, stride=chunk_rows), :]
            for row in range(chunk_rows // HEADS)
        ]
        rows[:, head * HEAD_DIM : (head + 1) * HEAD_DIM] = jnp.concatenate(lines, axis=0)
    product = lax.dot_general(
        rows[...].astype(jnp.bfloat16),
        weight[...],
        (((1,), (1,)), ((), ())),
        preferred_element_type=jnp.float32,
    )
    result = jnp.concatenate([product[:, :LANES], product[:, LANES:]], axis=0).astype(jnp.bfloat16)
    for target in range(out.shape[0]):
        out[target] = result


def residual_kernel(gathered, gain, inputs, out, rows, sem):
    fetch = pltpu.make_async_copy(inputs, rows, sem)
    fetch.start()
    count, chunk_rows, _ = gathered.shape
    depth = count // SIDE
    lines = chunk_rows // 2
    width = out.shape[1]
    eight = lines // 3

    def block(side, place, half):
        chunk = gathered[side * depth + place].astype(jnp.float32)
        return chunk[half * lines : (half + 1) * lines]

    def in_order(parts):
        return jnp.concatenate(
            [parts[side][row * eight : (row + 1) * eight] for row in range(3) for side in range(SIDE)],
            axis=0,
        )

    inverses = []
    for side in range(SIDE):
        squares = jnp.zeros((lines, LANES), jnp.float32)
        for place in range(depth):
            for half in range(2):
                found = block(side, place, half)
                squares = squares + found * found
        square = jnp.sum(squares, axis=1, keepdims=True) / width
        inverses.append(jnp.broadcast_to(lax.rsqrt(square + norm_epsilon), (lines, LANES)))
    inverse = in_order(inverses)
    fetch.wait()
    for place in range(depth):
        for half in range(2):
            start = (2 * place + half) * LANES
            columns = slice(start, start + LANES)
            found = in_order([block(side, place, half) for side in range(SIDE)])
            grown = rows[:, columns].astype(jnp.float32) + found * inverse * gain[:, columns]
            out[:, columns] = grown.astype(jnp.bfloat16)


def down_kernel(hidden, weight, out, held):
    count, chunk_rows, _ = out.shape
    total_rows = hidden.shape[0]
    share = total_rows // count
    line = lax.broadcasted_iota(jnp.int32, (total_rows, total_rows), 0)
    column = lax.broadcasted_iota(jnp.int32, (total_rows, total_rows), 1)
    spot = line % count
    depth = count // SIDE
    owner = spot % depth * SIDE + spot // depth
    turn = (column == owner * share + line // count).astype(jnp.bfloat16)
    rows = jnp.dot(turn, hidden[...], preferred_element_type=jnp.float32).astype(jnp.bfloat16)
    for block in range(chunk_rows // share):
        sums = jnp.dot(
            rows,
            weight[:, block * LANES : (block + 1) * LANES],
            preferred_element_type=jnp.float32,
        )
        for row in range(share):
            held[pl.ds(block * share + row, count, stride=chunk_rows), :] = sums[
                row * count : (row + 1) * count
            ]
    for target in range(count):
        out[target] = held[target * chunk_rows : (target + 1) * chunk_rows].astype(jnp.bfloat16)


def last_kernel(shares, residual, gain, out):
    count, chunk_rows, _ = shares.shape
    share = out.shape[0]
    blocks = chunk_rows // share
    sums = jnp.zeros((chunk_rows, LANES), jnp.float32)
    for source in range(count):
        sums = sums + shares[source].astype(jnp.float32)
    parts = [sums[block * share : (block + 1) * share] for block in range(blocks)]
    squares = functools.reduce(jnp.add, [part * part for part in parts])
    square = jnp.sum(squares, axis=1, keepdims=True) / (blocks * LANES)
    inverse = lax.rsqrt(square + norm_epsilon)
    for block, part in enumerate(parts):
        columns = slice(block * LANES, (block + 1) * LANES)
        grown = residual[:, columns].astype(jnp.float32) + part * inverse * gain[:, columns]
        out[:, columns] = grown.astype(jnp.bfloat16)


def logits_kernel(origins, drafts, vocab, out, table, sem):
    fetch = pltpu.make_async_copy(vocab, table, sem)
    fetch.start()
    requests, levels, _ = out.shape
    vectors = drafts[...]
    fetch.wait()
    logits = lax.dot_general(
        table[...], vectors, (((1,), (1,)), ((), ())), preferred_element_type=jnp.float32
    ).T
    for spot in range(requests):
        out[pl.ds(origins[spot], 1)] = logits[spot * levels : (spot + 1) * levels][None]


def rotated(front, back, cosine, sine):
    return front * cosine - back * sine, back * cosine + front * sine


def vmem(count):
    return [pl.BlockSpec(memory_space=pltpu.VMEM)] * count


SMEM = pl.BlockSpec(memory_space=pltpu.SMEM)


HBM = pl.BlockSpec(memory_space=pltpu.HBM)
MP = ("z", "x")
REQ = ("y", "c")
TURN = ("x", "z")


def limit(mib):
    return pltpu.CompilerParams(vmem_limit_bytes=mib * 2**20)


def exchange(chunks):
    return lax.all_to_all(chunks, TURN, 0, 0)


def per_device(
    draft_hidden,
    draft_weight,
    vocab_weight,
    tree_inputs,
    tree_parent,
    cache_len,
    page_table,
    kv_cache,
    accepted_node,
    qkv_weight,
    norm_gains,
    out_weight,
    gate_up_weight,
    down_weight,
):
    mp_count = lax.axis_size(MP)
    req_count = lax.axis_size(REQ)
    mp_place = lax.axis_index(MP)
    req_place = lax.axis_index(REQ)
    req_local, model_width = draft_hidden.shape
    draft_count = draft_weight.shape[0]
    slab = draft_weight.shape[2]
    vocab_local = vocab_weight.shape[0]
    rows = tree_inputs.shape[0]
    tree_size = tree_parent.shape[1]
    page_count, _, page_len, _ = kv_cache.shape
    table_width = page_table.shape[1]
    bf16 = jnp.bfloat16
    f32 = jnp.float32

    query_copies, own_key, own_value = pl.pallas_call(
        project_kernel,
        out_shape=(
            jax.ShapeDtypeStruct((mp_count, tree_size + 8, LANES), bf16),
            jax.ShapeDtypeStruct((tree_size, LANES), bf16),
            jax.ShapeDtypeStruct((tree_size, LANES), bf16),
        ),
        in_specs=[SMEM, *vmem(1), HBM, HBM, HBM],
        out_specs=tuple(vmem(3)),
        scratch_shapes=[
            pltpu.VMEM((rows, model_width), bf16),
            pltpu.VMEM((4 * slab, model_width), bf16),
            pltpu.VMEM((draft_count * slab, model_width), bf16),
            pltpu.SemaphoreType.DMA((6,)),
        ],
        compiler_params=limit(60),
        cost_estimate=pl.CostEstimate(flops=2**32, bytes_accessed=0, transcendentals=0),
        name="project",
    )(
        mp_place.reshape(1),
        draft_hidden,
        tree_inputs,
        jnp.transpose(qkv_weight, (1, 2, 0)),
        jnp.transpose(draft_weight, (0, 2, 1)).reshape(draft_count * slab, model_width),
    )
    gathered = exchange(query_copies)
    gate_up_copy = pl.pallas_call(
        held_kernel,
        out_shape=jax.ShapeDtypeStruct(gate_up_weight.shape, bf16),
        in_specs=[HBM],
        out_specs=vmem(1)[0],
        scratch_shapes=[pltpu.SemaphoreType.DMA],
        compiler_params=limit(52),
        cost_estimate=pl.CostEstimate(flops=2**31, bytes_accessed=0, transcendentals=0),
        name="held",
    )(gate_up_weight)
    gathered, gate_up_copy = lax.optimization_barrier((gathered, gate_up_copy))
    other_key = lax.ppermute(own_key, "x", [(i, i ^ 1) for i in range(SIDE)])
    out_own, other_key = lax.optimization_barrier((out_weight.T, other_key))
    out_parts = [out_own] + [
        lax.ppermute(out_own, "x", [(i, (i + k) % SIDE) for i in range(SIDE)]) for k in range(1, SIDE)
    ]

    ancestry, node_depth = tree_shape(tree_parent)
    positions = cache_len[:, None].astype(f32) + node_depth - 1.0
    freqs = rope_base ** (-jnp.arange(HALF, dtype=f32) * 2.0 / HEAD_DIM)
    angles = positions.T[:, :, None] * freqs[None, None, :]
    angles = angles.reshape(tree_size, LANES)
    cosine = jnp.cos(angles)
    sine = jnp.sin(angles)
    gain_rows = norm_gains.astype(f32)
    twice = gain_rows[:2].reshape(2, mp_count, slab)
    twice = jnp.concatenate([twice, twice], axis=2)

    slots = (req_place * mp_count + mp_place) * page_count + jnp.arange(page_count, dtype=jnp.int32)
    matches = page_table[None, :, :] == slots[:, None, None]
    starts = jnp.arange(table_width, dtype=jnp.int32) * page_len
    left = jnp.clip(cache_len[:, None] - starts[None, :], 0, page_len)
    counts = jnp.sum(jnp.where(matches, left[None], 0), axis=2).reshape(page_count * req_local, 1)

    groups = 4
    parts, drafts, kept = pl.pallas_call(
        pages_kernel,
        out_shape=(
            jax.ShapeDtypeStruct((mp_count, tree_size + 8, LANES), bf16),
            jax.ShapeDtypeStruct((req_local * draft_count, model_width), bf16),
            jax.ShapeDtypeStruct((tree_size, LANES), bf16),
        ),
        in_specs=[SMEM, *vmem(10), HBM],
        out_specs=tuple(vmem(3)),
        scratch_shapes=[
            pltpu.VMEM(kv_cache.shape, bf16),
            pltpu.VMEM((mp_count * tree_size, LANES), f32),
            pltpu.VMEM((HEADS, rows, HEAD_DIM), bf16),
            pltpu.SemaphoreType.DMA((groups,)),
        ],
        compiler_params=limit(52),
        cost_estimate=pl.CostEstimate(flops=2**33, bytes_accessed=0, transcendentals=0),
        name="pages",
    )(
        mp_place.reshape(1),
        counts,
        gathered,
        twice[0],
        twice[1],
        cosine,
        sine,
        own_key,
        other_key,
        own_value,
        ancestry,
        kv_cache,
    )
    arrived = exchange(parts)

    path = pl.pallas_call(
        path_kernel,
        out_shape=jax.ShapeDtypeStruct((2, 8, LANES), f32),
        in_specs=[SMEM, *vmem(4)],
        out_specs=vmem(1)[0],
        compiler_params=limit(8),
        name="path",
    )(accepted_node, kept, own_value, ancestry, node_depth)
    side_place = lax.axis_index("x").reshape(1)
    out_wide = pl.pallas_call(
        order_kernel,
        out_shape=jax.ShapeDtypeStruct((SIDE, slab, model_width), bf16),
        in_specs=[SMEM, *vmem(SIDE)],
        out_specs=vmem(1)[0],
        compiler_params=limit(12),
        name="order",
    )(side_place, *out_parts).reshape(SIDE * slab, model_width)

    pair = lax.ppermute(drafts, "c", [(0, 1), (1, 0)])
    both = jnp.concatenate([drafts, pair], axis=0)
    turns = req_count // 2
    drafted = [both] + [
        lax.ppermute(both, "y", [(i, (i + k) % turns) for i in range(turns)])
        for k in range(1, turns)
    ]
    drafted = jnp.concatenate(drafted, axis=0)
    spot = jnp.arange(req_count * req_local, dtype=jnp.int32)
    turn = spot // (2 * req_local)
    side = (spot // req_local) % 2
    holder = 2 * ((req_place // 2 - turn) % turns) + ((req_place % 2) ^ side)
    origins = holder * req_local + spot % req_local

    accepted_kv = jnp.transpose(
        path[:, :draft_count].reshape(2, draft_count, req_local, slab), (2, 1, 0, 3)
    ).astype(bf16)

    attended_copies = pl.pallas_call(
        merge_kernel,
        out_shape=jax.ShapeDtypeStruct((mp_count // SIDE, tree_size, LANES), bf16),
        in_specs=vmem(1),
        out_specs=vmem(1)[0],
        compiler_params=limit(8),
        name="merge",
    )(arrived)
    out_gain = gain_rows[2:3]
    last_gain = gain_rows[3:4]
    attended_copies, out_wide, accepted_kv, out_gain, last_gain, drafted, origins = (
        lax.optimization_barrier(
            (attended_copies, out_wide, accepted_kv, out_gain, last_gain, drafted, origins)
        )
    )
    attended = lax.all_to_all(attended_copies, "z", 0, 0)
    out_copies = pl.pallas_call(
        out_kernel,
        out_shape=jax.ShapeDtypeStruct((mp_count, tree_size, LANES), bf16),
        in_specs=vmem(2),
        out_specs=vmem(1)[0],
        scratch_shapes=[
            pltpu.VMEM((mp_count // SIDE * tree_size, LANES), f32),
            pltpu.VMEM((rows // SIDE, model_width), f32),
        ],
        compiler_params=limit(8),
        name="out_columns",
    )(attended, out_wide)
    projected_out = exchange(out_copies)
    projected_out, drafted, origins = lax.optimization_barrier((projected_out, drafted, origins))
    residual = pl.pallas_call(
        residual_kernel,
        out_shape=jax.ShapeDtypeStruct((rows, model_width), bf16),
        in_specs=[*vmem(2), HBM],
        out_specs=vmem(1)[0],
        scratch_shapes=[pltpu.VMEM((rows, model_width), bf16), pltpu.SemaphoreType.DMA],
        compiler_params=limit(8),
        name="residual",
    )(projected_out, out_gain, tree_inputs)
    gate_up = jnp.einsum("td,dce->tce", residual, gate_up_copy, preferred_element_type=f32)
    hidden = (jax.nn.silu(gate_up[:, 0]) * gate_up[:, 1]).astype(bf16)
    row_share = rows // mp_count
    chunk_rows = row_share * model_width // LANES
    partial = pl.pallas_call(
        down_kernel,
        out_shape=jax.ShapeDtypeStruct((mp_count, chunk_rows, LANES), bf16),
        in_specs=vmem(2),
        out_specs=vmem(1)[0],
        scratch_shapes=[pltpu.VMEM((mp_count * chunk_rows, LANES), f32)],
        compiler_params=limit(8),
        name="down",
    )(hidden, down_weight)
    shares = exchange(partial)

    draft_logits = pl.pallas_call(
        logits_kernel,
        out_shape=jax.ShapeDtypeStruct((req_count * req_local, draft_count, vocab_local), f32),
        in_specs=[SMEM, *vmem(1), HBM],
        out_specs=vmem(1)[0],
        scratch_shapes=[pltpu.VMEM(vocab_weight.shape, bf16), pltpu.SemaphoreType.DMA],
        compiler_params=limit(60),
        cost_estimate=pl.CostEstimate(flops=2**31, bytes_accessed=0, transcendentals=0),
        name="logits",
    )(origins, drafted, vocab_weight)
    residual_rows = lax.dynamic_slice_in_dim(residual, mp_place * row_share, row_share, 0)
    layer_out = pl.pallas_call(
        last_kernel,
        out_shape=jax.ShapeDtypeStruct((row_share, model_width), bf16),
        in_specs=vmem(3),
        out_specs=vmem(1)[0],
        compiler_params=limit(8),
        name="last",
    )(shares, residual_rows, last_gain)
    return (draft_logits, layer_out, accepted_kv)


def solution(mesh):
    chips = mesh.devices.reshape(-1, 2, mesh.devices.shape[1] // SIDE, SIDE)
    mesh = jax.sharding.Mesh(chips, (*REQ, *MP))
    both = (*REQ, *MP)
    placed = (
        P(REQ, None),
        P(None, None, MP),
        P(both, None),
        P(REQ, None),
        P(REQ, None),
        P(REQ),
        P(REQ, None),
        P(both, None, None, None),
        P(REQ),
        P(None, None, MP),
        P(),
        P(None, MP),
        P(None, None, MP),
        P(MP, None),
    )
    return jax.shard_map(
        per_device,
        mesh=mesh,
        in_specs=placed,
        out_specs=(P(None, None, both), P(both, None), P(REQ, None, None, MP)),
        check_vma=False,
    )
```

```python
import functools

import jax
import jax.numpy as jnp
from jax import lax
from jax.experimental import pallas as pl
from jax.experimental.pallas import tpu as pltpu
from jax.sharding import PartitionSpec as P

HEADS = 16
HEAD_DIM = 128
HALF = HEAD_DIM // 2
LANES = 128
SIDE = 4

rope_base = 500000.0
norm_epsilon = 1e-06
masked_score = -1e30


def tree_shape(parents):
    node_count = parents.shape[-1]
    step_one = (
        parents[..., :, None] == jnp.arange(node_count, dtype=jnp.int32)[None, None, :]
    ).astype(jnp.float32)
    step_two = jnp.einsum("rij,rjk->rik", step_one, step_one, precision=lax.Precision.HIGHEST)
    step_three = jnp.einsum("rij,rjk->rik", step_two, step_one, precision=lax.Precision.HIGHEST)
    ancestry = jnp.eye(node_count, dtype=jnp.float32)[None] + step_one + step_two + step_three
    return (ancestry, jnp.sum(ancestry, axis=-1))


def split_three(value):
    top = value.astype(jnp.bfloat16).astype(jnp.float32)
    rest = value - top
    middle = rest.astype(jnp.bfloat16).astype(jnp.float32)
    return top, middle, (rest - middle).astype(jnp.bfloat16).astype(jnp.float32)


def in_first(rows):
    return lax.broadcasted_iota(jnp.int32, (rows, LANES), 1) < HALF


def paired(left, right):
    first = in_first(left.shape[0])
    return (
        jnp.where(first, left, pltpu.roll(right, HALF, 1)),
        jnp.where(first, pltpu.roll(left, HALF, 1), right),
    )


def packed_inverse(squares, width):
    first = in_first(squares.shape[0])
    zero = jnp.zeros_like(squares)
    left = jnp.sum(jnp.where(first, squares, zero), axis=1, keepdims=True)
    right = jnp.sum(jnp.where(first, zero, squares), axis=1, keepdims=True)
    return lax.rsqrt(jnp.where(first, left, right) / width + norm_epsilon)


def spot_of(place):
    return place % SIDE * (2 * HEADS // SIDE) + place // SIDE


def columns_to_rows(columns):
    rest = LANES - columns.shape[0]
    return jnp.concatenate([columns, jnp.zeros((rest, LANES), jnp.float32)], axis=0).T


def project_kernel(
    place, hidden, inputs, weights, draft_weights, copies, own_key, own_value, rows, columns, heads, sems
):
    nodes = own_key.shape[0]
    pieces = sems.shape[0] - 1
    depth = rows.shape[1] // pieces
    fetches = []
    for piece in range(pieces):
        part = pl.ds(piece * depth, depth)
        fetches.append(
            [pltpu.make_async_copy(inputs.at[:, part], rows.at[:, part], sems.at[piece, 0])]
            + [
                pltpu.make_async_copy(
                    weights.at[kind, :, part],
                    columns.at[pl.ds(kind * HALF, HALF), part],
                    sems.at[piece, 1 + kind],
                )
                for kind in range(3)
            ]
        )
    drafting = pltpu.make_async_copy(draft_weights, heads, sems.at[pieces, 0])
    for group in fetches:
        for fetch in group:
            fetch.start()
    drafting.start()
    first = in_first(nodes)
    product = jnp.zeros((rows.shape[0], 2 * LANES), jnp.float32)
    for piece, group in enumerate(fetches):
        for fetch in group:
            fetch.wait()
        part = slice(piece * depth, (piece + 1) * depth)
        weight = jnp.concatenate([columns[:, part], columns[2 * HALF :, part]], axis=0)
        product = product + lax.dot_general(
            rows[:, part], weight, (((1,), (1,)), ((), ())), preferred_element_type=jnp.float32
        )
    query, key = paired(product[:nodes, :LANES], product[nodes:, :LANES])
    key = key.astype(jnp.bfloat16)
    query = query.astype(jnp.bfloat16)
    own_key[...] = key
    own_value[...] = jnp.where(first, product[:nodes, LANES:], product[nodes:, LANES:]).astype(
        jnp.bfloat16
    )
    squares = key.astype(jnp.float32)
    squares = squares * squares
    zero = jnp.zeros_like(squares)
    lane = lax.broadcasted_iota(jnp.int32, (nodes, LANES), 1)
    left = jnp.sum(jnp.where(first, squares, zero), axis=1, keepdims=True)
    right = jnp.sum(jnp.where(first, zero, squares), axis=1, keepdims=True)
    turned = columns_to_rows(jnp.where(lane == 0, left, jnp.where(lane == 1, right, zero)))
    sums = jnp.where(in_first(1), turned[0:1], pltpu.roll(turned[1:2], HALF, 1))
    drafting.wait()
    states = hidden[...]
    start = pl.multiple_of(place[0] // 2 * LANES, LANES)
    own = hidden[:, pl.ds(start, LANES)].astype(jnp.float32)
    swapped = pltpu.roll(own, HALF, 1)
    here = jnp.full(own.shape, place[0] % 2, jnp.int32) == lax.broadcasted_iota(jnp.int32, own.shape, 1) // HALF
    own = jnp.where(here, own, swapped)
    raw = lax.dot_general(
        heads[...], states, (((1,), (1,)), ((), ())), preferred_element_type=jnp.float32
    ).T
    raw = raw / (1.0 + jnp.exp(-raw))
    pairs = [own + raw[:, side * LANES : (side + 1) * LANES] for side in range(raw.shape[1] // LANES)]
    drafted = [part[r : r + 1] for r in range(states.shape[0]) for part in pairs]
    tail = jnp.concatenate([*split_three(sums), *drafted, jnp.zeros_like(sums)], axis=0)
    chunk = jnp.concatenate([query.astype(jnp.float32), tail], axis=0).astype(jnp.bfloat16)
    for target in range(copies.shape[0]):
        copies[target] = chunk


def tree_part(place, query, own_key, other_key, own_value, sums, gains, cosine, sine, ancestry):
    requests, nodes, _ = ancestry.shape
    width = 2 * HEADS * HALF
    head = place[0] // 2
    parity = jnp.full((nodes, LANES), place[0] % 2, jnp.int32)
    even = parity == 0
    side = lax.broadcasted_iota(jnp.int32, (nodes, LANES), 1) // HALF
    first = in_first(nodes)
    square = jnp.broadcast_to(sums, (LANES, LANES)).T
    square = jnp.where(first, square[:nodes], square[HALF : HALF + nodes])
    inverse = lax.rsqrt(square / width + norm_epsilon)
    own = own_key[...].astype(jnp.float32)
    other = other_key[...].astype(jnp.float32)
    front = jnp.where(even, own, other) * inverse * gains[pl.ds(2 * head, 1)]
    back = jnp.where(even, other, own) * inverse * gains[pl.ds(2 * head + 1, 1)]
    front, back = rotated(front, back, cosine[...], sine[...])
    kept = jnp.where(even, front, back).astype(jnp.bfloat16)
    keys = paired(front, back)
    value = own_value[...]
    tops, totals, mixed = [], [], []
    for request in range(requests):
        scores = lax.dot_general(
            query[request * nodes : (request + 1) * nodes],
            keys[request].astype(jnp.bfloat16),
            (((1,), (1,)), ((), ())),
            preferred_element_type=jnp.float32,
        ) * (HEAD_DIM ** (-0.5))
        visible = ancestry[request] > 0.5
        scores = jnp.where(visible, scores, masked_score)
        top = jnp.max(scores, axis=1, keepdims=True)
        weights = jnp.where(visible, jnp.exp(scores - top), 0.0)
        tops.append(top)
        totals.append(jnp.sum(weights, axis=1, keepdims=True))
        found = jnp.dot(weights.astype(jnp.bfloat16), value, preferred_element_type=jnp.float32)
        turned = pltpu.roll(found, HALF, 1)
        lined = jnp.where(parity == request, found, turned)
        mixed.append(jnp.where(side == parity, lined, 0.0))
    return (
        jnp.concatenate(tops, axis=0),
        jnp.concatenate(totals, axis=0),
        jnp.concatenate(mixed, axis=0),
        kept,
    )


def pages_kernel(
    place,
    counts,
    gathered,
    gains,
    key_gains,
    cosine,
    sine,
    own_key,
    other_key,
    own_value,
    ancestry,
    cache,
    out,
    drafts,
    kept_out,
    kv,
    held,
    queries,
    sems,
):
    pages, _, page_len, width = cache.shape
    nodes = cosine.shape[0]
    groups = sems.shape[0]
    group_width = width // groups

    def fetch(group):
        columns = pl.ds(group * group_width, group_width)
        return pltpu.make_async_copy(
            cache.at[:, :, :, columns], kv.at[:, :, :, columns], sems.at[group]
        )

    for group in range(groups):
        fetch(group).start()
    squares = jnp.zeros((nodes, LANES), jnp.float32)
    extra = jnp.zeros((8, LANES), jnp.float32)
    for source in range(2 * HEADS):
        chunk = gathered[source].astype(jnp.float32)
        squares = squares + chunk[:nodes] * chunk[:nodes]
        extra = extra + chunk[nodes : nodes + 8]
    inverse = packed_inverse(squares, width)
    sums = (extra[0:1] + extra[1:2]) + extra[2:3]
    for head in range(HEADS):
        tails = [gathered[spot_of(2 * head + side)].astype(jnp.float32)[nodes:] for side in range(2)]
        even, odd = paired(*tails)
        lines = [part[row : row + 1] for row in range(3, 7) for part in (even, odd)]
        drafts[:, head * HEAD_DIM : (head + 1) * HEAD_DIM] = jnp.concatenate(lines, axis=0).astype(
            jnp.bfloat16
        )
    token = lax.broadcasted_iota(jnp.int32, (nodes, page_len), 1)
    bias = []
    for page in range(pages):
        halves = [
            jnp.where(token < counts[2 * page + request : 2 * page + request + 1], 0.0, masked_score)
            for request in range(2)
        ]
        bias.append(jnp.concatenate(halves, axis=0))
    scale = HEAD_DIM ** (-0.5)
    cos_rows = cosine[...]
    sin_rows = sine[...]
    lane = lax.broadcasted_iota(jnp.int32, (2 * nodes, LANES), 1)
    stats = jnp.zeros((2 * nodes, LANES), jnp.float32)
    count = out.shape[0]
    share = 2 * nodes // count
    chunk_rows = share * HEADS

    def scored(head):
        if head % (HEADS // groups) == 0:
            fetch(head // (HEADS // groups)).wait()
        front = gathered[spot_of(2 * head)][:nodes].astype(jnp.float32)
        back = gathered[spot_of(2 * head + 1)][:nodes].astype(jnp.float32)
        front = front * inverse * gains[2 * head : 2 * head + 1]
        back = back * inverse * gains[2 * head + 1 : 2 * head + 2]
        front, back = rotated(front, back, cos_rows, sin_rows)
        query = jnp.concatenate(paired(front, back), axis=0).astype(jnp.bfloat16)
        queries[head] = query
        keys = kv[:, 0, :, head * HEAD_DIM : (head + 1) * HEAD_DIM]
        return lax.dot_general(
            query,
            keys.reshape(pages * page_len, HEAD_DIM),
            (((1,), (1,)), ((), ())),
            preferred_element_type=jnp.float32,
        )

    ahead = 4
    waiting = [scored(head) for head in range(ahead)]
    for head in range(HEADS):
        scores = waiting.pop(0)
        if head + ahead < HEADS:
            waiting.append(scored(head + ahead))
        base = head * HEAD_DIM
        scores = [
            scores[:, page * page_len : (page + 1) * page_len] * scale + bias[page]
            for page in range(pages)
        ]
        top = jnp.max(functools.reduce(jnp.maximum, scores), axis=1, keepdims=True)
        weights = [jnp.exp(score - top) for score in scores]
        total = jnp.sum(functools.reduce(jnp.add, weights), axis=1, keepdims=True)
        values = kv[:, 1, :, base : base + HEAD_DIM].reshape(pages * page_len, HEAD_DIM)
        mixed = jnp.dot(
            jnp.concatenate(weights, axis=1).astype(jnp.bfloat16),
            values,
            preferred_element_type=jnp.float32,
        )
        stats = jnp.where(lane == head, top, stats)
        stats = jnp.where(lane == HEADS + head, total, stats)
        for row in range(share):
            held[pl.ds(row * HEADS + head, count, stride=chunk_rows), :] = mixed[
                row * count : (row + 1) * count
            ]
    own_head = place[0] // 2
    tree_top, tree_total, tree_mixed, kept = tree_part(
        place, queries[own_head], own_key, other_key, own_value, sums, key_gains, cosine, sine, ancestry
    )
    kept_out[...] = kept
    is_top = lane == own_head
    is_total = lane == HEADS + own_head
    top = jnp.sum(jnp.where(is_top, stats, 0.0), axis=1, keepdims=True)
    total = jnp.sum(jnp.where(is_total, stats, 0.0), axis=1, keepdims=True)
    both_top = jnp.maximum(top, tree_top)
    page_factor = jnp.exp(top - both_top)
    tree_factor = jnp.exp(tree_top - both_top)
    adds = (1 - place[0] % 2).astype(jnp.float32)
    stats = jnp.where(is_top, both_top, stats)
    stats = jnp.where(is_total, total * page_factor + tree_total * tree_factor * adds, stats)
    tree_mixed = tree_mixed * tree_factor
    for row in range(share):
        spot = pl.ds(row * HEADS + own_head, count, stride=chunk_rows)
        lines = slice(row * count, (row + 1) * count)
        held[spot, :] = held[spot, :] * page_factor[lines] + tree_mixed[lines]
    spread = lax.broadcasted_iota(jnp.int32, (count, LANES), 1) // HEADS

    def by_device(kind):
        found = jnp.zeros((count, LANES), jnp.float32)
        for row in range(share):
            turned = pltpu.roll(
                stats[row * count : (row + 1) * count], (row - kind) * HEADS % LANES, 1
            )
            found = jnp.where(spread == row, turned, found)
        return found

    rows = [*split_three(by_device(0)), *split_three(by_device(1))]
    rows += [jnp.zeros_like(rows[0])] * 2
    for target in range(count):
        tail = jnp.concatenate([row[target : target + 1] for row in rows], axis=0)
        block = jnp.concatenate(
            [held[target * chunk_rows : (target + 1) * chunk_rows], tail], axis=0
        )
        out[target] = block.astype(jnp.bfloat16)


def path_kernel(accepted, kept, own_value, ancestry, depth, out):
    requests, nodes, _ = ancestry.shape
    pickers = []
    for request in range(requests):
        on_path = ancestry[request, pl.ds(accepted[request], 1), :]
        levels = depth[pl.ds(request, 1), :]
        wanted = (lax.broadcasted_iota(jnp.int32, (8, nodes), 0) + 1).astype(jnp.float32)
        pickers.append(jnp.where(wanted == levels, on_path, 0.0).astype(jnp.bfloat16))
    for kind, block in enumerate((kept[...], own_value[...])):
        picked = [
            jnp.dot(picker, block, preferred_element_type=jnp.float32) for picker in pickers
        ]
        out[kind] = jnp.where(in_first(8), picked[0], picked[1])


def order_kernel(side, own, *rest):
    *others, out = rest
    for turn, block in enumerate((own, *others)):
        out[pl.ds((side[0] + SIDE - turn) % SIDE, 1)] = block[...][None]


def held_kernel(large, out, sem):
    copy = pltpu.make_async_copy(large, out, sem)
    copy.start()
    copy.wait()


def merge_kernel(parts, out):
    count = parts.shape[0]
    rows = parts.shape[1] - 8
    tops = []
    totals = []
    for source in range(count):
        tail = parts[source].astype(jnp.float32)[rows:]
        tops.append((tail[0:1] + tail[1:2]) + tail[2:3])
        totals.append((tail[3:4] + tail[4:5]) + tail[5:6])
    tops = jnp.concatenate(tops, axis=0)
    totals = jnp.concatenate(totals, axis=0)
    factors = jnp.exp(tops - jnp.max(tops, axis=0, keepdims=True))
    shares = factors / jnp.sum(factors * totals, axis=0, keepdims=True)
    turned = columns_to_rows(shares)
    mixed = jnp.zeros((rows, LANES), jnp.float32)
    for source in range(count):
        mixed = mixed + turned[:rows, source : source + 1] * parts[source].astype(jnp.float32)[:rows]
    result = mixed.astype(jnp.bfloat16)
    for target in range(out.shape[0]):
        out[target] = result


def out_kernel(gathered, weight, out, wide, rows):
    depth, chunk_rows, _ = gathered.shape
    for source in range(depth):
        wide[source * chunk_rows : (source + 1) * chunk_rows] = gathered[source].astype(jnp.float32)
    for head in range(HEADS):
        lines = [
            wide[pl.ds(row * HEADS + head, depth, stride=chunk_rows), :]
            for row in range(chunk_rows // HEADS)
        ]
        rows[:, head * HEAD_DIM : (head + 1) * HEAD_DIM] = jnp.concatenate(lines, axis=0)
    product = lax.dot_general(
        rows[...].astype(jnp.bfloat16),
        weight[...],
        (((1,), (1,)), ((), ())),
        preferred_element_type=jnp.float32,
    )
    result = jnp.concatenate([product[:, :LANES], product[:, LANES:]], axis=0).astype(jnp.bfloat16)
    for target in range(out.shape[0]):
        out[target] = result


def residual_kernel(gathered, gain, inputs, out, rows, sem):
    fetch = pltpu.make_async_copy(inputs, rows, sem)
    fetch.start()
    count, chunk_rows, _ = gathered.shape
    depth = count // SIDE
    lines = chunk_rows // 2
    width = out.shape[1]
    eight = lines // 3

    def block(side, place, half):
        chunk = gathered[side * depth + place].astype(jnp.float32)
        return chunk[half * lines : (half + 1) * lines]

    def in_order(parts):
        return jnp.concatenate(
            [parts[side][row * eight : (row + 1) * eight] for row in range(3) for side in range(SIDE)],
            axis=0,
        )

    inverses = []
    for side in range(SIDE):
        squares = jnp.zeros((lines, LANES), jnp.float32)
        for place in range(depth):
            for half in range(2):
                found = block(side, place, half)
                squares = squares + found * found
        square = jnp.sum(squares, axis=1, keepdims=True) / width
        inverses.append(jnp.broadcast_to(lax.rsqrt(square + norm_epsilon), (lines, LANES)))
    inverse = in_order(inverses)
    fetch.wait()
    for place in range(depth):
        for half in range(2):
            start = (2 * place + half) * LANES
            columns = slice(start, start + LANES)
            found = in_order([block(side, place, half) for side in range(SIDE)])
            grown = rows[:, columns].astype(jnp.float32) + found * inverse * gain[:, columns]
            out[:, columns] = grown.astype(jnp.bfloat16)


def down_kernel(hidden, weight, out, held):
    count, chunk_rows, _ = out.shape
    total_rows = hidden.shape[0]
    share = total_rows // count
    line = lax.broadcasted_iota(jnp.int32, (total_rows, total_rows), 0)
    column = lax.broadcasted_iota(jnp.int32, (total_rows, total_rows), 1)
    spot = line % count
    depth = count // SIDE
    owner = spot % depth * SIDE + spot // depth
    turn = (column == owner * share + line // count).astype(jnp.bfloat16)
    rows = jnp.dot(turn, hidden[...], preferred_element_type=jnp.float32).astype(jnp.bfloat16)
    for block in range(chunk_rows // share):
        sums = jnp.dot(
            rows,
            weight[:, block * LANES : (block + 1) * LANES],
            preferred_element_type=jnp.float32,
        )
        for row in range(share):
            held[pl.ds(block * share + row, count, stride=chunk_rows), :] = sums[
                row * count : (row + 1) * count
            ]
    for target in range(count):
        out[target] = held[target * chunk_rows : (target + 1) * chunk_rows].astype(jnp.bfloat16)


def last_kernel(shares, residual, gain, out):
    count, chunk_rows, _ = shares.shape
    share = out.shape[0]
    blocks = chunk_rows // share
    sums = jnp.zeros((chunk_rows, LANES), jnp.float32)
    for source in range(count):
        sums = sums + shares[source].astype(jnp.float32)
    parts = [sums[block * share : (block + 1) * share] for block in range(blocks)]
    squares = functools.reduce(jnp.add, [part * part for part in parts])
    square = jnp.sum(squares, axis=1, keepdims=True) / (blocks * LANES)
    inverse = lax.rsqrt(square + norm_epsilon)
    for block, part in enumerate(parts):
        columns = slice(block * LANES, (block + 1) * LANES)
        grown = residual[:, columns].astype(jnp.float32) + part * inverse * gain[:, columns]
        out[:, columns] = grown.astype(jnp.bfloat16)


def logits_kernel(origins, drafts, vocab, out, table, sem):
    fetch = pltpu.make_async_copy(vocab, table, sem)
    fetch.start()
    requests, levels, _ = out.shape
    vectors = drafts[...]
    fetch.wait()
    logits = lax.dot_general(
        table[...], vectors, (((1,), (1,)), ((), ())), preferred_element_type=jnp.float32
    ).T
    for spot in range(requests):
        out[pl.ds(origins[spot], 1)] = logits[spot * levels : (spot + 1) * levels][None]


def rotated(front, back, cosine, sine):
    return front * cosine - back * sine, back * cosine + front * sine


def vmem(count):
    return [pl.BlockSpec(memory_space=pltpu.VMEM)] * count


SMEM = pl.BlockSpec(memory_space=pltpu.SMEM)


HBM = pl.BlockSpec(memory_space=pltpu.HBM)
MP = ("z", "x")
REQ = ("y", "c")
TURN = ("x", "z")


def limit(mib):
    return pltpu.CompilerParams(vmem_limit_bytes=mib * 2**20)


def exchange(chunks):
    return lax.all_to_all(chunks, TURN, 0, 0)


def per_device(
    draft_hidden,
    draft_weight,
    vocab_weight,
    tree_inputs,
    tree_parent,
    cache_len,
    page_table,
    kv_cache,
    accepted_node,
    qkv_weight,
    norm_gains,
    out_weight,
    gate_up_weight,
    down_weight,
):
    mp_count = lax.axis_size(MP)
    req_count = lax.axis_size(REQ)
    mp_place = lax.axis_index(MP)
    req_place = lax.axis_index(REQ)
    req_local, model_width = draft_hidden.shape
    draft_count = draft_weight.shape[0]
    slab = draft_weight.shape[2]
    vocab_local = vocab_weight.shape[0]
    rows = tree_inputs.shape[0]
    tree_size = tree_parent.shape[1]
    page_count, _, page_len, _ = kv_cache.shape
    table_width = page_table.shape[1]
    bf16 = jnp.bfloat16
    f32 = jnp.float32

    query_copies, own_key, own_value = pl.pallas_call(
        project_kernel,
        out_shape=(
            jax.ShapeDtypeStruct((mp_count, tree_size + 8, LANES), bf16),
            jax.ShapeDtypeStruct((tree_size, LANES), bf16),
            jax.ShapeDtypeStruct((tree_size, LANES), bf16),
        ),
        in_specs=[SMEM, *vmem(1), HBM, HBM, HBM],
        out_specs=tuple(vmem(3)),
        scratch_shapes=[
            pltpu.VMEM((rows, model_width), bf16),
            pltpu.VMEM((3 * slab, model_width), bf16),
            pltpu.VMEM((draft_count * slab, model_width), bf16),
            pltpu.SemaphoreType.DMA((3, 4)),
        ],
        compiler_params=limit(60),
        cost_estimate=pl.CostEstimate(flops=2**32, bytes_accessed=0, transcendentals=0),
        name="project",
    )(
        mp_place.reshape(1),
        draft_hidden,
        tree_inputs,
        jnp.transpose(qkv_weight, (1, 2, 0)),
        jnp.transpose(draft_weight, (0, 2, 1)).reshape(draft_count * slab, model_width),
    )
    gathered = exchange(query_copies)
    gate_up_copy = pl.pallas_call(
        held_kernel,
        out_shape=jax.ShapeDtypeStruct(gate_up_weight.shape, bf16),
        in_specs=[HBM],
        out_specs=vmem(1)[0],
        scratch_shapes=[pltpu.SemaphoreType.DMA],
        compiler_params=limit(52),
        cost_estimate=pl.CostEstimate(flops=2**31, bytes_accessed=0, transcendentals=0),
        name="held",
    )(gate_up_weight)
    gathered, gate_up_copy = lax.optimization_barrier((gathered, gate_up_copy))
    other_key = lax.ppermute(own_key, "x", [(i, i ^ 1) for i in range(SIDE)])
    out_own, other_key = lax.optimization_barrier((out_weight.T, other_key))
    out_parts = [out_own] + [
        lax.ppermute(out_own, "x", [(i, (i + k) % SIDE) for i in range(SIDE)]) for k in range(1, SIDE)
    ]

    ancestry, node_depth = tree_shape(tree_parent)
    positions = cache_len[:, None].astype(f32) + node_depth - 1.0
    freqs = rope_base ** (-jnp.arange(HALF, dtype=f32) * 2.0 / HEAD_DIM)
    angles = positions.T[:, :, None] * freqs[None, None, :]
    angles = angles.reshape(tree_size, LANES)
    cosine = jnp.cos(angles)
    sine = jnp.sin(angles)
    gain_rows = norm_gains.astype(f32)
    twice = gain_rows[:2].reshape(2, mp_count, slab)
    twice = jnp.concatenate([twice, twice], axis=2)

    slots = (req_place * mp_count + mp_place) * page_count + jnp.arange(page_count, dtype=jnp.int32)
    matches = page_table[None, :, :] == slots[:, None, None]
    starts = jnp.arange(table_width, dtype=jnp.int32) * page_len
    left = jnp.clip(cache_len[:, None] - starts[None, :], 0, page_len)
    counts = jnp.sum(jnp.where(matches, left[None], 0), axis=2).reshape(page_count * req_local, 1)

    groups = 4
    parts, drafts, kept = pl.pallas_call(
        pages_kernel,
        out_shape=(
            jax.ShapeDtypeStruct((mp_count, tree_size + 8, LANES), bf16),
            jax.ShapeDtypeStruct((req_local * draft_count, model_width), bf16),
            jax.ShapeDtypeStruct((tree_size, LANES), bf16),
        ),
        in_specs=[SMEM, *vmem(10), HBM],
        out_specs=tuple(vmem(3)),
        scratch_shapes=[
            pltpu.VMEM(kv_cache.shape, bf16),
            pltpu.VMEM((mp_count * tree_size, LANES), f32),
            pltpu.VMEM((HEADS, rows, HEAD_DIM), bf16),
            pltpu.SemaphoreType.DMA((groups,)),
        ],
        compiler_params=limit(52),
        cost_estimate=pl.CostEstimate(flops=2**33, bytes_accessed=0, transcendentals=0),
        name="pages",
    )(
        mp_place.reshape(1),
        counts,
        gathered,
        twice[0],
        twice[1],
        cosine,
        sine,
        own_key,
        other_key,
        own_value,
        ancestry,
        kv_cache,
    )
    arrived = exchange(parts)

    path = pl.pallas_call(
        path_kernel,
        out_shape=jax.ShapeDtypeStruct((2, 8, LANES), f32),
        in_specs=[SMEM, *vmem(4)],
        out_specs=vmem(1)[0],
        compiler_params=limit(8),
        name="path",
    )(accepted_node, kept, own_value, ancestry, node_depth)
    side_place = lax.axis_index("x").reshape(1)
    out_wide = pl.pallas_call(
        order_kernel,
        out_shape=jax.ShapeDtypeStruct((SIDE, slab, model_width), bf16),
        in_specs=[SMEM, *vmem(SIDE)],
        out_specs=vmem(1)[0],
        compiler_params=limit(12),
        name="order",
    )(side_place, *out_parts).reshape(SIDE * slab, model_width)

    pair = lax.ppermute(drafts, "c", [(0, 1), (1, 0)])
    both = jnp.concatenate([drafts, pair], axis=0)
    turns = req_count // 2
    drafted = [both] + [
        lax.ppermute(both, "y", [(i, (i + k) % turns) for i in range(turns)])
        for k in range(1, turns)
    ]
    drafted = jnp.concatenate(drafted, axis=0)
    spot = jnp.arange(req_count * req_local, dtype=jnp.int32)
    turn = spot // (2 * req_local)
    side = (spot // req_local) % 2
    holder = 2 * ((req_place // 2 - turn) % turns) + ((req_place % 2) ^ side)
    origins = holder * req_local + spot % req_local

    accepted_kv = jnp.transpose(
        path[:, :draft_count].reshape(2, draft_count, req_local, slab), (2, 1, 0, 3)
    ).astype(bf16)

    attended_copies = pl.pallas_call(
        merge_kernel,
        out_shape=jax.ShapeDtypeStruct((mp_count // SIDE, tree_size, LANES), bf16),
        in_specs=vmem(1),
        out_specs=vmem(1)[0],
        compiler_params=limit(8),
        name="merge",
    )(arrived)
    out_gain = gain_rows[2:3]
    last_gain = gain_rows[3:4]
    attended_copies, out_wide, accepted_kv, out_gain, last_gain, drafted, origins = (
        lax.optimization_barrier(
            (attended_copies, out_wide, accepted_kv, out_gain, last_gain, drafted, origins)
        )
    )
    attended = lax.all_to_all(attended_copies, "z", 0, 0)
    out_copies = pl.pallas_call(
        out_kernel,
        out_shape=jax.ShapeDtypeStruct((mp_count, tree_size, LANES), bf16),
        in_specs=vmem(2),
        out_specs=vmem(1)[0],
        scratch_shapes=[
            pltpu.VMEM((mp_count // SIDE * tree_size, LANES), f32),
            pltpu.VMEM((rows // SIDE, model_width), f32),
        ],
        compiler_params=limit(8),
        name="out_columns",
    )(attended, out_wide)
    projected_out = exchange(out_copies)
    projected_out, drafted, origins = lax.optimization_barrier((projected_out, drafted, origins))
    residual = pl.pallas_call(
        residual_kernel,
        out_shape=jax.ShapeDtypeStruct((rows, model_width), bf16),
        in_specs=[*vmem(2), HBM],
        out_specs=vmem(1)[0],
        scratch_shapes=[pltpu.VMEM((rows, model_width), bf16), pltpu.SemaphoreType.DMA],
        compiler_params=limit(8),
        name="residual",
    )(projected_out, out_gain, tree_inputs)
    gate_up = jnp.einsum("td,dce->tce", residual, gate_up_copy, preferred_element_type=f32)
    hidden = (jax.nn.silu(gate_up[:, 0]) * gate_up[:, 1]).astype(bf16)
    row_share = rows // mp_count
    chunk_rows = row_share * model_width // LANES
    partial = pl.pallas_call(
        down_kernel,
        out_shape=jax.ShapeDtypeStruct((mp_count, chunk_rows, LANES), bf16),
        in_specs=vmem(2),
        out_specs=vmem(1)[0],
        scratch_shapes=[pltpu.VMEM((mp_count * chunk_rows, LANES), f32)],
        compiler_params=limit(8),
        name="down",
    )(hidden, down_weight)
    shares = exchange(partial)

    draft_logits = pl.pallas_call(
        logits_kernel,
        out_shape=jax.ShapeDtypeStruct((req_count * req_local, draft_count, vocab_local), f32),
        in_specs=[SMEM, *vmem(1), HBM],
        out_specs=vmem(1)[0],
        scratch_shapes=[pltpu.VMEM(vocab_weight.shape, bf16), pltpu.SemaphoreType.DMA],
        compiler_params=limit(60),
        cost_estimate=pl.CostEstimate(flops=2**31, bytes_accessed=0, transcendentals=0),
        name="logits",
    )(origins, drafted, vocab_weight)
    residual_rows = lax.dynamic_slice_in_dim(residual, mp_place * row_share, row_share, 0)
    layer_out = pl.pallas_call(
        last_kernel,
        out_shape=jax.ShapeDtypeStruct((row_share, model_width), bf16),
        in_specs=vmem(3),
        out_specs=vmem(1)[0],
        compiler_params=limit(8),
        name="last",
    )(shares, residual_rows, last_gain)
    return (draft_logits, layer_out, accepted_kv)


def solution(mesh):
    chips = mesh.devices.reshape(-1, 2, mesh.devices.shape[1] // SIDE, SIDE)
    mesh = jax.sharding.Mesh(chips, (*REQ, *MP))
    both = (*REQ, *MP)
    placed = (
        P(REQ, None),
        P(None, None, MP),
        P(both, None),
        P(REQ, None),
        P(REQ, None),
        P(REQ),
        P(REQ, None),
        P(both, None, None, None),
        P(REQ),
        P(None, None, MP),
        P(),
        P(None, MP),
        P(None, None, MP),
        P(MP, None),
    )
    return jax.shard_map(
        per_device,
        mesh=mesh,
        in_specs=placed,
        out_specs=(P(None, None, both), P(both, None), P(REQ, None, None, MP)),
        check_vma=False,
    )
```

```python
import functools

import jax
import jax.numpy as jnp
from jax import lax
from jax.experimental import pallas as pl
from jax.experimental.pallas import tpu as pltpu
from jax.sharding import PartitionSpec as P

HEADS = 16
HEAD_DIM = 128
HALF = HEAD_DIM // 2
LANES = 128
SIDE = 4

rope_base = 500000.0
norm_epsilon = 1e-06
masked_score = -1e30


def tree_shape(parents):
    node_count = parents.shape[-1]
    step_one = (
        parents[..., :, None] == jnp.arange(node_count, dtype=jnp.int32)[None, None, :]
    ).astype(jnp.float32)
    step_two = jnp.einsum("rij,rjk->rik", step_one, step_one, precision=lax.Precision.HIGHEST)
    step_three = jnp.einsum("rij,rjk->rik", step_two, step_one, precision=lax.Precision.HIGHEST)
    ancestry = jnp.eye(node_count, dtype=jnp.float32)[None] + step_one + step_two + step_three
    return (ancestry, jnp.sum(ancestry, axis=-1))


def split_three(value):
    top = value.astype(jnp.bfloat16).astype(jnp.float32)
    rest = value - top
    middle = rest.astype(jnp.bfloat16).astype(jnp.float32)
    return top, middle, (rest - middle).astype(jnp.bfloat16).astype(jnp.float32)


def in_first(rows):
    return lax.broadcasted_iota(jnp.int32, (rows, LANES), 1) < HALF


def paired(left, right):
    first = in_first(left.shape[0])
    return (
        jnp.where(first, left, pltpu.roll(right, HALF, 1)),
        jnp.where(first, pltpu.roll(left, HALF, 1), right),
    )


def packed_inverse(squares, width):
    first = in_first(squares.shape[0])
    zero = jnp.zeros_like(squares)
    left = jnp.sum(jnp.where(first, squares, zero), axis=1, keepdims=True)
    right = jnp.sum(jnp.where(first, zero, squares), axis=1, keepdims=True)
    return lax.rsqrt(jnp.where(first, left, right) / width + norm_epsilon)


def spot_of(place):
    return place % SIDE * (2 * HEADS // SIDE) + place // SIDE


def columns_to_rows(columns):
    rest = LANES - columns.shape[0]
    return jnp.concatenate([columns, jnp.zeros((rest, LANES), jnp.float32)], axis=0).T


def project_kernel(
    place, hidden, inputs, weights, draft_weights, copies, own_key, own_value, rows, columns, heads, sems
):
    nodes = own_key.shape[0]
    pieces = sems.shape[0] - 1
    depth = rows.shape[1] // pieces
    fetches = []
    for piece in range(pieces):
        part = pl.ds(piece * depth, depth)
        fetches.append(
            [pltpu.make_async_copy(inputs.at[:, part], rows.at[:, part], sems.at[piece, 0])]
            + [
                pltpu.make_async_copy(
                    weights.at[kind, :, part],
                    columns.at[pl.ds(kind * HALF, HALF), part],
                    sems.at[piece, 1 + kind],
                )
                for kind in range(3)
            ]
        )
    drafting = pltpu.make_async_copy(draft_weights, heads, sems.at[pieces, 0])
    for group in fetches:
        for fetch in group:
            fetch.start()
    drafting.start()
    first = in_first(nodes)
    product = jnp.zeros((rows.shape[0], 2 * LANES), jnp.float32)
    for piece, group in enumerate(fetches):
        for fetch in group:
            fetch.wait()
        part = slice(piece * depth, (piece + 1) * depth)
        weight = jnp.concatenate([columns[:, part], columns[2 * HALF :, part]], axis=0)
        product = product + lax.dot_general(
            rows[:, part], weight, (((1,), (1,)), ((), ())), preferred_element_type=jnp.float32
        )
    query, key = paired(product[:nodes, :LANES], product[nodes:, :LANES])
    key = key.astype(jnp.bfloat16)
    query = query.astype(jnp.bfloat16)
    own_key[...] = key
    own_value[...] = jnp.where(first, product[:nodes, LANES:], product[nodes:, LANES:]).astype(
        jnp.bfloat16
    )
    squares = key.astype(jnp.float32)
    squares = squares * squares
    zero = jnp.zeros_like(squares)
    lane = lax.broadcasted_iota(jnp.int32, (nodes, LANES), 1)
    left = jnp.sum(jnp.where(first, squares, zero), axis=1, keepdims=True)
    right = jnp.sum(jnp.where(first, zero, squares), axis=1, keepdims=True)
    turned = columns_to_rows(jnp.where(lane == 0, left, jnp.where(lane == 1, right, zero)))
    sums = jnp.where(in_first(1), turned[0:1], pltpu.roll(turned[1:2], HALF, 1))
    drafting.wait()
    states = hidden[...]
    start = pl.multiple_of(place[0] // 2 * LANES, LANES)
    own = hidden[:, pl.ds(start, LANES)].astype(jnp.float32)
    swapped = pltpu.roll(own, HALF, 1)
    here = jnp.full(own.shape, place[0] % 2, jnp.int32) == lax.broadcasted_iota(jnp.int32, own.shape, 1) // HALF
    own = jnp.where(here, own, swapped)
    raw = lax.dot_general(
        heads[...], states, (((1,), (1,)), ((), ())), preferred_element_type=jnp.float32
    ).T
    raw = raw / (1.0 + jnp.exp(-raw))
    pairs = [own + raw[:, side * LANES : (side + 1) * LANES] for side in range(raw.shape[1] // LANES)]
    drafted = [part[r : r + 1] for r in range(states.shape[0]) for part in pairs]
    tail = jnp.concatenate([*split_three(sums), *drafted, jnp.zeros_like(sums)], axis=0)
    chunk = jnp.concatenate([query.astype(jnp.float32), tail], axis=0).astype(jnp.bfloat16)
    for target in range(copies.shape[0]):
        copies[target] = chunk


def tree_part(place, query, own_key, other_key, own_value, sums, gains, cosine, sine, ancestry):
    requests, nodes, _ = ancestry.shape
    width = 2 * HEADS * HALF
    head = place[0] // 2
    parity = jnp.full((nodes, LANES), place[0] % 2, jnp.int32)
    even = parity == 0
    side = lax.broadcasted_iota(jnp.int32, (nodes, LANES), 1) // HALF
    first = in_first(nodes)
    square = jnp.broadcast_to(sums, (LANES, LANES)).T
    square = jnp.where(first, square[:nodes], square[HALF : HALF + nodes])
    inverse = lax.rsqrt(square / width + norm_epsilon)
    own = own_key[...].astype(jnp.float32)
    other = other_key[...].astype(jnp.float32)
    front = jnp.where(even, own, other) * inverse * gains[pl.ds(2 * head, 1)]
    back = jnp.where(even, other, own) * inverse * gains[pl.ds(2 * head + 1, 1)]
    front, back = rotated(front, back, cosine[...], sine[...])
    kept = jnp.where(even, front, back).astype(jnp.bfloat16)
    keys = paired(front, back)
    value = own_value[...]
    tops, totals, mixed = [], [], []
    for request in range(requests):
        scores = lax.dot_general(
            query[request * nodes : (request + 1) * nodes],
            keys[request].astype(jnp.bfloat16),
            (((1,), (1,)), ((), ())),
            preferred_element_type=jnp.float32,
        ) * (HEAD_DIM ** (-0.5))
        visible = ancestry[request] > 0.5
        scores = jnp.where(visible, scores, masked_score)
        top = jnp.max(scores, axis=1, keepdims=True)
        weights = jnp.where(visible, jnp.exp(scores - top), 0.0)
        tops.append(top)
        totals.append(jnp.sum(weights, axis=1, keepdims=True))
        found = jnp.dot(weights.astype(jnp.bfloat16), value, preferred_element_type=jnp.float32)
        turned = pltpu.roll(found, HALF, 1)
        lined = jnp.where(parity == request, found, turned)
        mixed.append(jnp.where(side == parity, lined, 0.0))
    return (
        jnp.concatenate(tops, axis=0),
        jnp.concatenate(totals, axis=0),
        jnp.concatenate(mixed, axis=0),
        kept,
    )


def pages_kernel(
    place,
    counts,
    gathered,
    gains,
    key_gains,
    cosine,
    sine,
    own_key,
    other_key,
    own_value,
    ancestry,
    cache,
    out,
    drafts,
    kept_out,
    kv,
    held,
    queries,
    sems,
):
    pages, _, page_len, width = cache.shape
    nodes = cosine.shape[0]
    groups = sems.shape[0]
    group_width = width // groups

    def fetch(group):
        columns = pl.ds(group * group_width, group_width)
        return pltpu.make_async_copy(
            cache.at[:, :, :, columns], kv.at[:, :, :, columns], sems.at[group]
        )

    for group in range(groups):
        fetch(group).start()
    squares = jnp.zeros((nodes, LANES), jnp.float32)
    extra = jnp.zeros((8, LANES), jnp.float32)
    for source in range(2 * HEADS):
        chunk = gathered[source].astype(jnp.float32)
        squares = squares + chunk[:nodes] * chunk[:nodes]
        extra = extra + chunk[nodes : nodes + 8]
    inverse = packed_inverse(squares, width)
    sums = (extra[0:1] + extra[1:2]) + extra[2:3]
    for head in range(HEADS):
        tails = [gathered[spot_of(2 * head + side)].astype(jnp.float32)[nodes:] for side in range(2)]
        even, odd = paired(*tails)
        lines = [part[row : row + 1] for row in range(3, 7) for part in (even, odd)]
        drafts[:, head * HEAD_DIM : (head + 1) * HEAD_DIM] = jnp.concatenate(lines, axis=0).astype(
            jnp.bfloat16
        )
    token = lax.broadcasted_iota(jnp.int32, (nodes, page_len), 1)
    bias = []
    for page in range(pages):
        halves = [
            jnp.where(token < counts[2 * page + request : 2 * page + request + 1], 0.0, masked_score)
            for request in range(2)
        ]
        bias.append(jnp.concatenate(halves, axis=0))
    scale = HEAD_DIM ** (-0.5)
    cos_rows = cosine[...]
    sin_rows = sine[...]
    lane = lax.broadcasted_iota(jnp.int32, (2 * nodes, LANES), 1)
    stats = jnp.zeros((2 * nodes, LANES), jnp.float32)
    count = out.shape[0]
    share = 2 * nodes // count
    chunk_rows = share * HEADS

    def scored(head):
        if head % (HEADS // groups) == 0:
            fetch(head // (HEADS // groups)).wait()
        front = gathered[spot_of(2 * head)][:nodes].astype(jnp.float32)
        back = gathered[spot_of(2 * head + 1)][:nodes].astype(jnp.float32)
        front = front * inverse * gains[2 * head : 2 * head + 1]
        back = back * inverse * gains[2 * head + 1 : 2 * head + 2]
        front, back = rotated(front, back, cos_rows, sin_rows)
        query = jnp.concatenate(paired(front, back), axis=0).astype(jnp.bfloat16)
        queries[head] = query
        keys = kv[:, 0, :, head * HEAD_DIM : (head + 1) * HEAD_DIM]
        return lax.dot_general(
            query,
            keys.reshape(pages * page_len, HEAD_DIM),
            (((1,), (1,)), ((), ())),
            preferred_element_type=jnp.float32,
        )

    ahead = 4
    waiting = [scored(head) for head in range(ahead)]
    for head in range(HEADS):
        scores = waiting.pop(0)
        if head + ahead < HEADS:
            waiting.append(scored(head + ahead))
        base = head * HEAD_DIM
        scores = [
            scores[:, page * page_len : (page + 1) * page_len] * scale + bias[page]
            for page in range(pages)
        ]
        top = jnp.max(functools.reduce(jnp.maximum, scores), axis=1, keepdims=True)
        weights = [jnp.exp(score - top) for score in scores]
        total = jnp.sum(functools.reduce(jnp.add, weights), axis=1, keepdims=True)
        values = kv[:, 1, :, base : base + HEAD_DIM].reshape(pages * page_len, HEAD_DIM)
        mixed = jnp.dot(
            jnp.concatenate(weights, axis=1).astype(jnp.bfloat16),
            values,
            preferred_element_type=jnp.float32,
        )
        stats = jnp.where(lane == head, top, stats)
        stats = jnp.where(lane == HEADS + head, total, stats)
        for row in range(share):
            held[pl.ds(row * HEADS + head, count, stride=chunk_rows), :] = mixed[
                row * count : (row + 1) * count
            ]
    own_head = place[0] // 2
    tree_top, tree_total, tree_mixed, kept = tree_part(
        place, queries[own_head], own_key, other_key, own_value, sums, key_gains, cosine, sine, ancestry
    )
    kept_out[...] = kept
    is_top = lane == own_head
    is_total = lane == HEADS + own_head
    top = jnp.sum(jnp.where(is_top, stats, 0.0), axis=1, keepdims=True)
    total = jnp.sum(jnp.where(is_total, stats, 0.0), axis=1, keepdims=True)
    both_top = jnp.maximum(top, tree_top)
    page_factor = jnp.exp(top - both_top)
    tree_factor = jnp.exp(tree_top - both_top)
    adds = (1 - place[0] % 2).astype(jnp.float32)
    stats = jnp.where(is_top, both_top, stats)
    stats = jnp.where(is_total, total * page_factor + tree_total * tree_factor * adds, stats)
    tree_mixed = tree_mixed * tree_factor
    for row in range(share):
        spot = pl.ds(row * HEADS + own_head, count, stride=chunk_rows)
        lines = slice(row * count, (row + 1) * count)
        held[spot, :] = held[spot, :] * page_factor[lines] + tree_mixed[lines]
    spread = lax.broadcasted_iota(jnp.int32, (count, LANES), 1) // HEADS

    def by_device(kind):
        found = jnp.zeros((count, LANES), jnp.float32)
        for row in range(share):
            turned = pltpu.roll(
                stats[row * count : (row + 1) * count], (row - kind) * HEADS % LANES, 1
            )
            found = jnp.where(spread == row, turned, found)
        return found

    rows = [*split_three(by_device(0)), *split_three(by_device(1))]
    rows += [jnp.zeros_like(rows[0])] * 2
    for target in range(count):
        tail = jnp.concatenate([row[target : target + 1] for row in rows], axis=0)
        block = jnp.concatenate(
            [held[target * chunk_rows : (target + 1) * chunk_rows], tail], axis=0
        )
        out[target] = block.astype(jnp.bfloat16)


def path_kernel(accepted, kept, own_value, ancestry, depth, out):
    requests, nodes, _ = ancestry.shape
    pickers = []
    for request in range(requests):
        on_path = ancestry[request, pl.ds(accepted[request], 1), :]
        levels = depth[pl.ds(request, 1), :]
        wanted = (lax.broadcasted_iota(jnp.int32, (8, nodes), 0) + 1).astype(jnp.float32)
        pickers.append(jnp.where(wanted == levels, on_path, 0.0).astype(jnp.bfloat16))
    for kind, block in enumerate((kept[...], own_value[...])):
        picked = [
            jnp.dot(picker, block, preferred_element_type=jnp.float32) for picker in pickers
        ]
        out[kind] = jnp.where(in_first(8), picked[0], picked[1])


def order_kernel(side, own, *rest):
    *others, out = rest
    for turn, block in enumerate((own, *others)):
        out[pl.ds((side[0] + SIDE - turn) % SIDE, 1)] = block[...][None]


def held_kernel(large, out, sem):
    copy = pltpu.make_async_copy(large, out, sem)
    copy.start()
    copy.wait()


def merge_kernel(parts, out):
    count = parts.shape[0]
    rows = parts.shape[1] - 8
    tops = []
    totals = []
    for source in range(count):
        tail = parts[source].astype(jnp.float32)[rows:]
        tops.append((tail[0:1] + tail[1:2]) + tail[2:3])
        totals.append((tail[3:4] + tail[4:5]) + tail[5:6])
    tops = jnp.concatenate(tops, axis=0)
    totals = jnp.concatenate(totals, axis=0)
    factors = jnp.exp(tops - jnp.max(tops, axis=0, keepdims=True))
    shares = factors / jnp.sum(factors * totals, axis=0, keepdims=True)
    turned = columns_to_rows(shares)
    mixed = jnp.zeros((rows, LANES), jnp.float32)
    for source in range(count):
        mixed = mixed + turned[:rows, source : source + 1] * parts[source].astype(jnp.float32)[:rows]
    result = mixed.astype(jnp.bfloat16)
    for target in range(out.shape[0]):
        out[target] = result


def out_kernel(gathered, weight, out, wide, rows):
    depth, chunk_rows, _ = gathered.shape
    for source in range(depth):
        wide[source * chunk_rows : (source + 1) * chunk_rows] = gathered[source].astype(jnp.float32)
    for head in range(HEADS):
        lines = [
            wide[pl.ds(row * HEADS + head, depth, stride=chunk_rows), :]
            for row in range(chunk_rows // HEADS)
        ]
        rows[:, head * HEAD_DIM : (head + 1) * HEAD_DIM] = jnp.concatenate(lines, axis=0)
    product = lax.dot_general(
        rows[...].astype(jnp.bfloat16),
        weight[...],
        (((1,), (1,)), ((), ())),
        preferred_element_type=jnp.float32,
    )
    result = jnp.concatenate([product[:, :LANES], product[:, LANES:]], axis=0).astype(jnp.bfloat16)
    for target in range(out.shape[0]):
        out[target] = result


def residual_kernel(gathered, gain, inputs, out, rows, sem):
    fetch = pltpu.make_async_copy(inputs, rows, sem)
    fetch.start()
    count, chunk_rows, _ = gathered.shape
    depth = count // SIDE
    lines = chunk_rows // 2
    width = out.shape[1]
    eight = lines // 3

    def block(side, place, half):
        chunk = gathered[side * depth + place].astype(jnp.float32)
        return chunk[half * lines : (half + 1) * lines]

    def in_order(parts):
        return jnp.concatenate(
            [parts[side][row * eight : (row + 1) * eight] for row in range(3) for side in range(SIDE)],
            axis=0,
        )

    inverses = []
    for side in range(SIDE):
        squares = jnp.zeros((lines, LANES), jnp.float32)
        for place in range(depth):
            for half in range(2):
                found = block(side, place, half)
                squares = squares + found * found
        square = jnp.sum(squares, axis=1, keepdims=True) / width
        inverses.append(jnp.broadcast_to(lax.rsqrt(square + norm_epsilon), (lines, LANES)))
    inverse = in_order(inverses)
    fetch.wait()
    for place in range(depth):
        for half in range(2):
            start = (2 * place + half) * LANES
            columns = slice(start, start + LANES)
            found = in_order([block(side, place, half) for side in range(SIDE)])
            grown = rows[:, columns].astype(jnp.float32) + found * inverse * gain[:, columns]
            out[:, columns] = grown.astype(jnp.bfloat16)


def down_kernel(hidden, weight, out, held):
    count, chunk_rows, _ = out.shape
    total_rows = hidden.shape[0]
    share = total_rows // count
    line = lax.broadcasted_iota(jnp.int32, (total_rows, total_rows), 0)
    column = lax.broadcasted_iota(jnp.int32, (total_rows, total_rows), 1)
    spot = line % count
    depth = count // SIDE
    owner = spot % depth * SIDE + spot // depth
    turn = (column == owner * share + line // count).astype(jnp.bfloat16)
    rows = jnp.dot(turn, hidden[...], preferred_element_type=jnp.float32).astype(jnp.bfloat16)
    for block in range(chunk_rows // share):
        sums = jnp.dot(
            rows,
            weight[:, block * LANES : (block + 1) * LANES],
            preferred_element_type=jnp.float32,
        )
        for row in range(share):
            held[pl.ds(block * share + row, count, stride=chunk_rows), :] = sums[
                row * count : (row + 1) * count
            ]
    for target in range(count):
        out[target] = held[target * chunk_rows : (target + 1) * chunk_rows].astype(jnp.bfloat16)


def last_kernel(shares, residual, gain, out):
    count, chunk_rows, _ = shares.shape
    share = out.shape[0]
    blocks = chunk_rows // share
    sums = jnp.zeros((chunk_rows, LANES), jnp.float32)
    for source in range(count):
        sums = sums + shares[source].astype(jnp.float32)
    parts = [sums[block * share : (block + 1) * share] for block in range(blocks)]
    squares = functools.reduce(jnp.add, [part * part for part in parts])
    square = jnp.sum(squares, axis=1, keepdims=True) / (blocks * LANES)
    inverse = lax.rsqrt(square + norm_epsilon)
    for block, part in enumerate(parts):
        columns = slice(block * LANES, (block + 1) * LANES)
        grown = residual[:, columns].astype(jnp.float32) + part * inverse * gain[:, columns]
        out[:, columns] = grown.astype(jnp.bfloat16)


def logits_kernel(origins, drafts, vocab, out, table, sem):
    fetch = pltpu.make_async_copy(vocab, table, sem)
    fetch.start()
    requests, levels, _ = out.shape
    vectors = drafts[...]
    fetch.wait()
    logits = lax.dot_general(
        table[...], vectors, (((1,), (1,)), ((), ())), preferred_element_type=jnp.float32
    ).T
    for spot in range(requests):
        out[pl.ds(origins[spot], 1)] = logits[spot * levels : (spot + 1) * levels][None]


def rotated(front, back, cosine, sine):
    return front * cosine - back * sine, back * cosine + front * sine


def vmem(count):
    return [pl.BlockSpec(memory_space=pltpu.VMEM)] * count


SMEM = pl.BlockSpec(memory_space=pltpu.SMEM)


HBM = pl.BlockSpec(memory_space=pltpu.HBM)
MP = ("z", "x")
REQ = ("y", "c")
TURN = ("x", "z")


def limit(mib):
    return pltpu.CompilerParams(vmem_limit_bytes=mib * 2**20)


def exchange(chunks):
    return lax.all_to_all(chunks, TURN, 0, 0)


def per_device(
    draft_hidden,
    draft_weight,
    vocab_weight,
    tree_inputs,
    tree_parent,
    cache_len,
    page_table,
    kv_cache,
    accepted_node,
    qkv_weight,
    norm_gains,
    out_weight,
    gate_up_weight,
    down_weight,
):
    mp_count = lax.axis_size(MP)
    req_count = lax.axis_size(REQ)
    mp_place = lax.axis_index(MP)
    req_place = lax.axis_index(REQ)
    req_local, model_width = draft_hidden.shape
    draft_count = draft_weight.shape[0]
    slab = draft_weight.shape[2]
    vocab_local = vocab_weight.shape[0]
    rows = tree_inputs.shape[0]
    tree_size = tree_parent.shape[1]
    page_count, _, page_len, _ = kv_cache.shape
    table_width = page_table.shape[1]
    bf16 = jnp.bfloat16
    f32 = jnp.float32

    query_copies, own_key, own_value = pl.pallas_call(
        project_kernel,
        out_shape=(
            jax.ShapeDtypeStruct((mp_count, tree_size + 8, LANES), bf16),
            jax.ShapeDtypeStruct((tree_size, LANES), bf16),
            jax.ShapeDtypeStruct((tree_size, LANES), bf16),
        ),
        in_specs=[SMEM, *vmem(1), HBM, HBM, HBM],
        out_specs=tuple(vmem(3)),
        scratch_shapes=[
            pltpu.VMEM((rows, model_width), bf16),
            pltpu.VMEM((3 * slab, model_width), bf16),
            pltpu.VMEM((draft_count * slab, model_width), bf16),
            pltpu.SemaphoreType.DMA((5, 4)),
        ],
        compiler_params=limit(60),
        cost_estimate=pl.CostEstimate(flops=2**32, bytes_accessed=0, transcendentals=0),
        name="project",
    )(
        mp_place.reshape(1),
        draft_hidden,
        tree_inputs,
        jnp.transpose(qkv_weight, (1, 2, 0)),
        jnp.transpose(draft_weight, (0, 2, 1)).reshape(draft_count * slab, model_width),
    )
    gathered = exchange(query_copies)
    gate_up_copy = pl.pallas_call(
        held_kernel,
        out_shape=jax.ShapeDtypeStruct(gate_up_weight.shape, bf16),
        in_specs=[HBM],
        out_specs=vmem(1)[0],
        scratch_shapes=[pltpu.SemaphoreType.DMA],
        compiler_params=limit(52),
        cost_estimate=pl.CostEstimate(flops=2**31, bytes_accessed=0, transcendentals=0),
        name="held",
    )(gate_up_weight)
    gathered, gate_up_copy = lax.optimization_barrier((gathered, gate_up_copy))
    other_key = lax.ppermute(own_key, "x", [(i, i ^ 1) for i in range(SIDE)])
    out_own, other_key = lax.optimization_barrier((out_weight.T, other_key))
    out_parts = [out_own] + [
        lax.ppermute(out_own, "x", [(i, (i + k) % SIDE) for i in range(SIDE)]) for k in range(1, SIDE)
    ]

    ancestry, node_depth = tree_shape(tree_parent)
    positions = cache_len[:, None].astype(f32) + node_depth - 1.0
    freqs = rope_base ** (-jnp.arange(HALF, dtype=f32) * 2.0 / HEAD_DIM)
    angles = positions.T[:, :, None] * freqs[None, None, :]
    angles = angles.reshape(tree_size, LANES)
    cosine = jnp.cos(angles)
    sine = jnp.sin(angles)
    gain_rows = norm_gains.astype(f32)
    twice = gain_rows[:2].reshape(2, mp_count, slab)
    twice = jnp.concatenate([twice, twice], axis=2)

    slots = (req_place * mp_count + mp_place) * page_count + jnp.arange(page_count, dtype=jnp.int32)
    matches = page_table[None, :, :] == slots[:, None, None]
    starts = jnp.arange(table_width, dtype=jnp.int32) * page_len
    left = jnp.clip(cache_len[:, None] - starts[None, :], 0, page_len)
    counts = jnp.sum(jnp.where(matches, left[None], 0), axis=2).reshape(page_count * req_local, 1)

    groups = 4
    parts, drafts, kept = pl.pallas_call(
        pages_kernel,
        out_shape=(
            jax.ShapeDtypeStruct((mp_count, tree_size + 8, LANES), bf16),
            jax.ShapeDtypeStruct((req_local * draft_count, model_width), bf16),
            jax.ShapeDtypeStruct((tree_size, LANES), bf16),
        ),
        in_specs=[SMEM, *vmem(10), HBM],
        out_specs=tuple(vmem(3)),
        scratch_shapes=[
            pltpu.VMEM(kv_cache.shape, bf16),
            pltpu.VMEM((mp_count * tree_size, LANES), f32),
            pltpu.VMEM((HEADS, rows, HEAD_DIM), bf16),
            pltpu.SemaphoreType.DMA((groups,)),
        ],
        compiler_params=limit(52),
        cost_estimate=pl.CostEstimate(flops=2**33, bytes_accessed=0, transcendentals=0),
        name="pages",
    )(
        mp_place.reshape(1),
        counts,
        gathered,
        twice[0],
        twice[1],
        cosine,
        sine,
        own_key,
        other_key,
        own_value,
        ancestry,
        kv_cache,
    )
    arrived = exchange(parts)

    path = pl.pallas_call(
        path_kernel,
        out_shape=jax.ShapeDtypeStruct((2, 8, LANES), f32),
        in_specs=[SMEM, *vmem(4)],
        out_specs=vmem(1)[0],
        compiler_params=limit(8),
        name="path",
    )(accepted_node, kept, own_value, ancestry, node_depth)
    side_place = lax.axis_index("x").reshape(1)
    out_wide = pl.pallas_call(
        order_kernel,
        out_shape=jax.ShapeDtypeStruct((SIDE, slab, model_width), bf16),
        in_specs=[SMEM, *vmem(SIDE)],
        out_specs=vmem(1)[0],
        compiler_params=limit(12),
        name="order",
    )(side_place, *out_parts).reshape(SIDE * slab, model_width)

    pair = lax.ppermute(drafts, "c", [(0, 1), (1, 0)])
    both = jnp.concatenate([drafts, pair], axis=0)
    turns = req_count // 2
    drafted = [both] + [
        lax.ppermute(both, "y", [(i, (i + k) % turns) for i in range(turns)])
        for k in range(1, turns)
    ]
    drafted = jnp.concatenate(drafted, axis=0)
    spot = jnp.arange(req_count * req_local, dtype=jnp.int32)
    turn = spot // (2 * req_local)
    side = (spot // req_local) % 2
    holder = 2 * ((req_place // 2 - turn) % turns) + ((req_place % 2) ^ side)
    origins = holder * req_local + spot % req_local

    accepted_kv = jnp.transpose(
        path[:, :draft_count].reshape(2, draft_count, req_local, slab), (2, 1, 0, 3)
    ).astype(bf16)

    attended_copies = pl.pallas_call(
        merge_kernel,
        out_shape=jax.ShapeDtypeStruct((mp_count // SIDE, tree_size, LANES), bf16),
        in_specs=vmem(1),
        out_specs=vmem(1)[0],
        compiler_params=limit(8),
        name="merge",
    )(arrived)
    out_gain = gain_rows[2:3]
    last_gain = gain_rows[3:4]
    attended_copies, out_wide, accepted_kv, out_gain, last_gain, drafted, origins = (
        lax.optimization_barrier(
            (attended_copies, out_wide, accepted_kv, out_gain, last_gain, drafted, origins)
        )
    )
    attended = lax.all_to_all(attended_copies, "z", 0, 0)
    out_copies = pl.pallas_call(
        out_kernel,
        out_shape=jax.ShapeDtypeStruct((mp_count, tree_size, LANES), bf16),
        in_specs=vmem(2),
        out_specs=vmem(1)[0],
        scratch_shapes=[
            pltpu.VMEM((mp_count // SIDE * tree_size, LANES), f32),
            pltpu.VMEM((rows // SIDE, model_width), f32),
        ],
        compiler_params=limit(8),
        name="out_columns",
    )(attended, out_wide)
    projected_out = exchange(out_copies)
    projected_out, drafted, origins = lax.optimization_barrier((projected_out, drafted, origins))
    residual = pl.pallas_call(
        residual_kernel,
        out_shape=jax.ShapeDtypeStruct((rows, model_width), bf16),
        in_specs=[*vmem(2), HBM],
        out_specs=vmem(1)[0],
        scratch_shapes=[pltpu.VMEM((rows, model_width), bf16), pltpu.SemaphoreType.DMA],
        compiler_params=limit(8),
        name="residual",
    )(projected_out, out_gain, tree_inputs)
    gate_up = jnp.einsum("td,dce->tce", residual, gate_up_copy, preferred_element_type=f32)
    hidden = (jax.nn.silu(gate_up[:, 0]) * gate_up[:, 1]).astype(bf16)
    row_share = rows // mp_count
    chunk_rows = row_share * model_width // LANES
    partial = pl.pallas_call(
        down_kernel,
        out_shape=jax.ShapeDtypeStruct((mp_count, chunk_rows, LANES), bf16),
        in_specs=vmem(2),
        out_specs=vmem(1)[0],
        scratch_shapes=[pltpu.VMEM((mp_count * chunk_rows, LANES), f32)],
        compiler_params=limit(8),
        name="down",
    )(hidden, down_weight)
    shares = exchange(partial)

    draft_logits = pl.pallas_call(
        logits_kernel,
        out_shape=jax.ShapeDtypeStruct((req_count * req_local, draft_count, vocab_local), f32),
        in_specs=[SMEM, *vmem(1), HBM],
        out_specs=vmem(1)[0],
        scratch_shapes=[pltpu.VMEM(vocab_weight.shape, bf16), pltpu.SemaphoreType.DMA],
        compiler_params=limit(60),
        cost_estimate=pl.CostEstimate(flops=2**31, bytes_accessed=0, transcendentals=0),
        name="logits",
    )(origins, drafted, vocab_weight)
    residual_rows = lax.dynamic_slice_in_dim(residual, mp_place * row_share, row_share, 0)
    layer_out = pl.pallas_call(
        last_kernel,
        out_shape=jax.ShapeDtypeStruct((row_share, model_width), bf16),
        in_specs=vmem(3),
        out_specs=vmem(1)[0],
        compiler_params=limit(8),
        name="last",
    )(shares, residual_rows, last_gain)
    return (draft_logits, layer_out, accepted_kv)


def solution(mesh):
    chips = mesh.devices.reshape(-1, 2, mesh.devices.shape[1] // SIDE, SIDE)
    mesh = jax.sharding.Mesh(chips, (*REQ, *MP))
    both = (*REQ, *MP)
    placed = (
        P(REQ, None),
        P(None, None, MP),
        P(both, None),
        P(REQ, None),
        P(REQ, None),
        P(REQ),
        P(REQ, None),
        P(both, None, None, None),
        P(REQ),
        P(None, None, MP),
        P(),
        P(None, MP),
        P(None, None, MP),
        P(MP, None),
    )
    return jax.shard_map(
        per_device,
        mesh=mesh,
        in_specs=placed,
        out_specs=(P(None, None, both), P(both, None), P(REQ, None, None, MP)),
        check_vma=False,
    )
```
